32 devices in a mesh: batch: 2 (over x), seq: 16 (over z, y, core).
Axes of the slice: x: 2, y: 2, z: 4, core: 2. Of those that a mesh axis runs over, the one named last changes fastest.
Arguments:
- tokens_in: bfloat16 [8, 1024, 312], P('batch', 'seq'), may hold values from -6 to 6
- teacher_in: bfloat16 [8, 1024, 768], P('batch', 'seq'), may hold values from -6 to 6
- out_grad: bfloat16 [8, 1024, 312], P('batch', 'seq'), may hold values from -6 to 6
- mask_pos: int32 [8, 384], P('batch'), may hold values from -1 to 1023, as said below
- slot_ids: int32 [8, 384], P('batch'), may hold values from 0 to 30463
- w_query: bfloat16 [312, 312], replicated, may hold values from -0.3125 to 0.3125
- b_query: bfloat16 [312], replicated, may hold values from -3 to 3
- w_key: bfloat16 [312, 312], replicated, may hold values from -0.3125 to 0.3125
- b_key: bfloat16 [312], replicated, may hold values from -3 to 3
- w_value: bfloat16 [312, 312], replicated, may hold values from -0.3125 to 0.3125
- b_value: bfloat16 [312], replicated, may hold values from -0.15625 to 0.15625
- w_out: bfloat16 [312, 312], replicated, may hold values from -6 to 6
- b_out: bfloat16 [312], replicated, may hold values from -3 to 3
- ln1_gain: bfloat16 [312], replicated, may hold values from 0.5 to 1.5
- ln1_bias: bfloat16 [312], replicated, may hold values from -1.75 to 1.75
- w_up: bfloat16 [312, 1200], replicated, may hold values from -0.3125 to 0.3125
- b_up: bfloat16 [1200], replicated, may hold values from -3 to 3
- w_down: bfloat16 [1200, 312], replicated, may hold values from -0.25 to 0.25
- b_down: bfloat16 [312], replicated, may hold values from -1.75 to 1.75
- ln2_gain: bfloat16 [312], replicated, may hold values from 0.5 to 1.5
- ln2_bias: bfloat16 [312], replicated, may hold values from -1.75 to 1.75
- w_proj: bfloat16 [312, 768], replicated, may hold values from -0.3125 to 0.3125
- b_proj: bfloat16 [768], replicated, may hold values from -3 to 3
- t_query: bfloat16 [768, 768], replicated, may hold values from -0.21875 to 0.21875
- t_key: bfloat16 [768, 768], replicated, may hold values from -0.21875 to 0.21875
- t_value: bfloat16 [768, 768], replicated, may hold values from -0.21875 to 0.21875
- t_out: bfloat16 [768, 768], replicated, may hold values from -4 to 4
- t_up: bfloat16 [768, 3072], replicated, may hold values from -0.21875 to 0.21875
- t_down: bfloat16 [3072, 768], replicated, may hold values from -0.15625 to 0.15625
- embedding: bfloat16 [30464, 768], P('seq'), may hold values from -0.4375 to 0.4375
Outputs:
- layer_out: bfloat16 [8, 1024, 312], P('batch', 'seq')
- input_grad: float32 [8, 1024, 312], P('batch', 'seq')
- grad_w_query: float32 [312, 312], replicated
- grad_b_query: float32 [312], replicated
- grad_w_key: float32 [312, 312], replicated
- grad_b_key: float32 [312], replicated
- grad_w_value: float32 [312, 312], replicated
- grad_b_value: float32 [312], replicated
- grad_w_out: float32 [312, 312], replicated
- grad_b_out: float32 [312], replicated
- grad_ln1_gain: float32 [312], replicated
- grad_ln1_bias: float32 [312], replicated
- grad_w_up: float32 [312, 1200], replicated
- grad_b_up: float32 [1200], replicated
- grad_w_down: float32 [1200, 312], replicated
- grad_b_down: float32 [312], replicated
- grad_ln2_gain: float32 [312], replicated
- grad_ln2_bias: float32 [312], replicated
- grad_w_proj: float32 [312, 768], replicated
- grad_b_proj: float32 [768], replicated
The draws below stay inside these ranges and needn't reach their ends.
Inputs may be any that keep to these rules, and one draw needn't show every extreme that they name: `mask_pos`: in every sequence, slots 24 * d to 24 * d + 23 hold distinct positions of d * 64 to d * 64 + 63 first and -1 in the rest; at most 24 positions to a device and sequence, and in every sequence some device's slots are all live.
All inputs are finite; a program needn't handle non-finite values.
Results may differ from the reference program's by a relative error of at most 0.035.
Values may be sent and summed in bfloat16 or wider, within the bound.
No kernel may reach another device: no remote copies, remote signals or barrier semaphores. Data moves between devices by JAX's collectives and lax.ppermute only.
A program may use at most 192 MiB of HBM per device.

```python
import math
import jax
import jax.numpy as jnp
import numpy as np
from jax import lax

D = 312
HEADS = 12
FF = 1200
DT = 768
FFT = 3072
VOCAB = 30464
LOC = 64
CAP = 24
SEQS_ALL = 8
LENGTH = 1024
SLOTS = 384


def draw_mask_pos(key, part):
    key = jax.random.fold_in(key, 11)
    k_count, k_full, k_order = jax.random.split(key, 3)
    groups = SLOTS // CAP
    counts = jax.random.randint(k_count, (SEQS_ALL, groups), max(1, CAP // 4), CAP + 1)
    chosen = jax.random.randint(k_full, (SEQS_ALL, 1), 0, groups)
    counts = jnp.where(jnp.arange(groups)[None, :] == chosen, CAP, counts)
    subkeys = jax.random.split(k_order, SEQS_ALL * groups)
    orders = jax.vmap(lambda subkey: jax.random.permutation(subkey, LOC))(subkeys)
    orders = orders.reshape(SEQS_ALL, groups, LOC)[:, :, :CAP]
    starts = (jnp.arange(groups) * LOC)[None, :, None]
    filled = jnp.arange(CAP)[None, None, :] < counts[:, :, None]
    return jnp.where(filled, orders + starts, -1).reshape(SEQS_ALL, SLOTS).astype(jnp.int32)


def touch_ends(drawn, rng, smallest, largest):
    index_at = [jax.random.randint(jax.random.fold_in(rng, axis), (), 0, length) for axis, length in enumerate(drawn.shape)]
    longest = drawn.shape.index(max(drawn.shape))
    neighbour = index_at[:longest] + [(index_at[longest] + 1) % drawn.shape[longest]] + index_at[longest + 1:]
    return drawn.at[tuple(index_at)].set(smallest).at[tuple(neighbour)].set(largest)


def block_levels(stream_key, extent, pieces, least, high):
    def one(axis_at, shards_of):
        steps = jax.random.uniform(jax.random.fold_in(jax.random.fold_in(stream_key, 6), axis_at), (shards_of,), jnp.float32, least / len(pieces), high / len(pieces))
        return jnp.repeat(jnp.exp(steps), extent[axis_at] // shards_of).reshape((-1,) + (1,) * (len(extent) - axis_at - 1))

    loudness = one(*pieces[0])
    for cut in pieces[1:]:
        loudness = loudness * one(*cut)
    return loudness


def cumulative_ranks(amount, lean):
    weights = [(1 << 20) // math.isqrt(grade ** lean) + 1 for grade in range(1, amount + 1)]
    spread = 1 + sum(weights) // (1 << 30)
    return np.cumsum(np.array([max(1, weight // spread) for weight in weights]))


def ranked(own_key, shape, amount, skew):
    listing = cumulative_ranks(amount, skew)
    lot = jax.random.randint(jax.random.fold_in(own_key, 1), shape, 0, int(listing[amount - 1]))
    rank = jnp.searchsorted(jnp.asarray(listing, jnp.int32), lot, side="right")
    return jax.random.permutation(jax.random.fold_in(own_key, 2), amount)[rank].astype(jnp.int32)


def gaussian(key, extent, scale, bound, pieces=(), kind=jnp.bfloat16):
    loudness = block_levels(key, extent, pieces, -0.22, 0.18) if pieces else 1.0
    values = jax.random.normal(key, extent, jnp.float32) * scale * loudness
    return jnp.minimum(jnp.maximum(values, -bound), bound).astype(kind)


def setup_inputs(seed: int = 0) -> dict:
    arg_keys = jax.random.split(jax.random.key(seed), 31)
    return {
        "tokens_in": gaussian(arg_keys[0], (SEQS_ALL, LENGTH, D), 1.0, 6.0, ((0, 2), (1, 16))),
        "teacher_in": gaussian(arg_keys[1], (SEQS_ALL, LENGTH, DT), 1.0, 6.0, ((0, 2), (1, 16))),
        "out_grad": gaussian(arg_keys[2], (SEQS_ALL, LENGTH, D), 1.0, 6.0, ((0, 2), (1, 16))),
        "mask_pos": draw_mask_pos(jax.random.fold_in(arg_keys[30], 71), 0),
        "slot_ids": touch_ends(ranked(arg_keys[4], (SEQS_ALL, SLOTS), VOCAB, 2), jax.random.fold_in(arg_keys[4], 3), 0, VOCAB - 1).astype(jnp.int32),
        "w_query": gaussian(arg_keys[5], (D, D), D ** -0.5, 0.3125),
        "b_query": gaussian(arg_keys[6], (D,), 0.5, 3.0),
        "w_key": gaussian(arg_keys[7], (D, D), D ** -0.5, 0.3125),
        "b_key": gaussian(arg_keys[8], (D,), 0.5, 3.0),
        "w_value": gaussian(arg_keys[9], (D, D), D ** -0.5, 0.3125),
        "b_value": gaussian(arg_keys[10], (D,), (0.5 * (3 / LENGTH) ** 0.5), 0.15625),
        "w_out": gaussian(arg_keys[11], (D, D), ((LENGTH / (3 * D)) ** 0.5), 6.0),
        "b_out": gaussian(arg_keys[12], (D,), 0.5, 3.0),
        "ln1_gain": jnp.clip(1.0 + 0.1 * jax.random.normal(arg_keys[13], (D,), jnp.float32), 0.5, 1.5).astype(jnp.bfloat16),
        "ln1_bias": gaussian(arg_keys[14], (D,), 0.3, 1.75),
        "w_up": gaussian(arg_keys[15], (D, FF), D ** -0.5, 0.3125),
        "b_up": gaussian(arg_keys[16], (FF,), 0.5, 3.0),
        "w_down": gaussian(arg_keys[17], (FF, D), (FF // 2) ** -0.5, 0.25),
        "b_down": gaussian(arg_keys[18], (D,), 0.3, 1.75),
        "ln2_gain": jnp.clip(1.0 + 0.1 * jax.random.normal(arg_keys[19], (D,), jnp.float32), 0.5, 1.5).astype(jnp.bfloat16),
        "ln2_bias": gaussian(arg_keys[20], (D,), 0.3, 1.75),
        "w_proj": gaussian(arg_keys[21], (D, DT), D ** -0.5, 0.3125),
        "b_proj": gaussian(arg_keys[22], (DT,), 0.5, 3.0),
        "t_query": gaussian(arg_keys[23], (DT, DT), DT ** -0.5, 0.21875),
        "t_key": gaussian(arg_keys[24], (DT, DT), DT ** -0.5, 0.21875),
        "t_value": gaussian(arg_keys[25], (DT, DT), DT ** -0.5, 0.21875),
        "t_out": gaussian(arg_keys[26], (DT, DT), ((LENGTH / (3 * DT)) ** 0.5), 4.0),
        "t_up": gaussian(arg_keys[27], (DT, FFT), DT ** -0.5, 0.21875),
        "t_down": gaussian(arg_keys[28], (FFT, DT), (FFT // 2) ** -0.5, 0.15625),
        "embedding": gaussian(arg_keys[29], (VOCAB, DT), (2 / DT ** 0.5), 0.4375, ((0, 16),)),
    }


@jax.custom_vjp
def low(v):
    return lax.optimization_barrier(v.astype(jnp.bfloat16)).astype(jnp.float32)

@jax.custom_vjp
def low_back(v):
    return v

def low_keep(v):
    return (low(v), None)

def low_pass(kept, grad):
    return (grad,)

def back_keep(v):
    return (v, None)

def back_low(kept, grad):
    return (low(grad),)
low.defvjp(low_keep, low_pass)
low_back.defvjp(back_keep, back_low)
EPSILON = 1e-06
HID_WEIGHT = 0.05
CE_WEIGHT = 4.0
MIXING = 0.5

def matmul(left_arr, right_arr):
    return jnp.dot(left_arr, right_arr, precision=lax.Precision.HIGHEST)

def rounded_both(values):
    return low_back(low(values))

def layer_norm(values, gain, offset):
    centered = values - lax.optimization_barrier(jnp.mean(values, axis=-1, keepdims=True))
    inverse = lax.rsqrt(lax.optimization_barrier(jnp.mean(centered * centered, axis=-1, keepdims=True)) + EPSILON)
    return centered * inverse * gain + offset

def head_scores(queries, key_rows):
    span_len, model_width = queries.shape
    head_size = model_width // HEADS
    left_heads = queries.reshape(span_len, HEADS, head_size)
    right_heads = key_rows.reshape(span_len, HEADS, head_size)
    return jnp.einsum('qhd,khd->hqk', left_heads, right_heads, precision=lax.Precision.HIGHEST) * (1.0 / math.sqrt(head_size))

def mix_values(weights, value_rows):
    span_len, model_width = value_rows.shape
    head_size = model_width // HEADS
    mixed = jnp.einsum('hqk,khd->qhd', weights, value_rows.reshape(span_len, HEADS, head_size), precision=lax.Precision.HIGHEST)
    return mixed.reshape(span_len, model_width)

def teacher_layer(teacher_rows, teacher_w):
    t_query, t_key, t_value, t_out, t_up, t_down = teacher_w
    t_queries = low(matmul(teacher_rows, t_query))
    t_key_rows = low(matmul(teacher_rows, t_key))
    t_value_rows = low(matmul(teacher_rows, t_value))
    t_scores = head_scores(t_queries, t_key_rows)
    t_attended = low(mix_values(low(jax.nn.softmax(t_scores, axis=-1)), t_value_rows))
    t_hidden = layer_norm(teacher_rows + matmul(t_attended, t_out), 1.0, 0.0)
    t_inner = low(jax.nn.gelu(matmul(low(t_hidden), t_up), approximate=False))
    t_output = layer_norm(t_hidden + matmul(t_inner, t_down), 1.0, 0.0)
    return (t_scores, t_output)

def sequence_loss(params, rows_in, teacher_rows, positions, targets, teacher_w, table):
    w_query, b_query, w_key, b_key, w_value, b_value, w_out, b_out, ln1_gain, ln1_bias, w_up, b_up, w_down, b_down, ln2_gain, ln2_bias, w_proj, b_proj = params
    span_len = rows_in.shape[0]
    queries = rounded_both(matmul(rows_in, w_query) + b_query)
    key_rows = rounded_both(matmul(rows_in, w_key) + b_key)
    value_rows = rounded_both(matmul(rows_in, w_value) + b_value)
    scores = low_back(head_scores(queries, key_rows))
    t_scores, t_output = teacher_layer(teacher_rows, teacher_w)
    score_loss = jnp.sum((scores - t_scores) ** 2) / (HEADS * span_len)
    attended = rounded_both(mix_values(low(jax.nn.softmax(scores, axis=-1)), value_rows))
    branch = low_back(matmul(attended, w_out) + b_out)
    hidden = layer_norm(rows_in + branch, ln1_gain, ln1_bias)
    inner = low_back(matmul(low(hidden), w_up) + b_up)
    outer_part = low_back(matmul(low(jax.nn.gelu(inner, approximate=False)), w_down) + b_down)
    output = layer_norm(hidden + outer_part, ln2_gain, ln2_bias)
    mapped = low_back(matmul(low(output), w_proj) + b_proj)
    hidden_loss = HID_WEIGHT * jnp.sum((mapped - t_output) ** 2)
    live_slot = positions >= 0
    row_at = jnp.maximum(positions, 0)
    picked = low(mapped)[row_at]
    t_picked = low(t_output)[row_at]
    s_logits = low_back(matmul(picked, table.T))
    t_logits = matmul(t_picked, table.T)
    vocab_size = table.shape[0]
    matches = (targets[:, None] == jnp.arange(vocab_size)[None, :]).astype(jnp.float32)
    target = MIXING * jax.nn.softmax(t_logits, axis=-1) + (1.0 - MIXING) * matches
    cross = jax.scipy.special.logsumexp(s_logits, axis=-1) - lax.optimization_barrier(jnp.sum(target * s_logits, axis=-1))
    ce_loss = CE_WEIGHT * jnp.sum(jnp.where(live_slot, cross, 0.0))
    return (output, score_loss + hidden_loss + ce_loss)

def reference(tokens_in, teacher_in, out_grad, mask_pos, slot_ids, w_query, b_query, w_key, b_key, w_value, b_value, w_out, b_out, ln1_gain, ln1_bias, w_up, b_up, w_down, b_down, ln2_gain, ln2_bias, w_proj, b_proj, t_query, t_key, t_value, t_out, t_up, t_down, embedding):
    params = tuple((member.astype(jnp.float32) for member in (w_query, b_query, w_key, b_key, w_value, b_value, w_out, b_out, ln1_gain, ln1_bias, w_up, b_up, w_down, b_down, ln2_gain, ln2_bias, w_proj, b_proj)))
    teacher_w = tuple((member.astype(jnp.float32) for member in (t_query, t_key, t_value, t_out, t_up, t_down)))
    table = embedding.astype(jnp.float32)
    teacher_f = teacher_in.astype(jnp.float32)
    inputs_f = tokens_in.astype(jnp.float32)

    def forward(student_in, weights):

        def one_sequence(packed):
            rows_in, teacher_rows, positions, targets = packed
            return sequence_loss(weights, rows_in, teacher_rows, positions, targets, teacher_w, table)
        outputs, losses = lax.map(jax.checkpoint(one_sequence), (student_in, teacher_f, mask_pos, slot_ids))
        return (outputs, jnp.sum(losses))
    (outputs, total_loss), pullback = jax.vjp(forward, inputs_f, params)
    d_input, grads = pullback((out_grad.astype(jnp.float32), jnp.ones((), jnp.float32)))
    return (outputs.astype(jnp.bfloat16), d_input, grads[0], grads[1], grads[2], grads[3], grads[4], grads[5], grads[6], grads[7], grads[8], grads[9], grads[10], grads[11], grads[12], grads[13], grads[14], grads[15], grads[16], grads[17])
```

```python
import functools
import math

import jax
import jax.numpy as jnp
from jax import lax
from jax.experimental import pallas as pl
from jax.experimental.pallas import tpu as pltpu
from jax.sharding import Mesh
from jax.sharding import PartitionSpec as P

HEADS = 12
EPSILON = 1e-06
HID_WEIGHT = 0.05
CE_WEIGHT = 4.0
MIXING = 0.5
ROOT_HALF = 0.7071067811865476
ROOT_TWO_PI = 2.5066282746310002
LANES = 128
BF = jnp.bfloat16
F32 = jnp.float32
MIB = 1 << 20


def mm(left, right):
    return lax.dot_general(left, right, (((1,), (0,)), ((), ())), preferred_element_type=F32)


def mm_nt(left, right):
    return lax.dot_general(left, right, (((1,), (1,)), ((), ())), preferred_element_type=F32)


def mm_tn(left, right):
    return lax.dot_general(left, right, (((0,), (0,)), ((), ())), preferred_element_type=F32)


def normalize(values):
    centered = values - jnp.mean(values, axis=-1, keepdims=True)
    inverse = lax.rsqrt(jnp.mean(centered * centered, axis=-1, keepdims=True) + EPSILON)
    return centered * inverse, inverse


def norm_back(grads, scaled, inverse):
    return inverse * (
        grads
        - jnp.mean(grads, axis=-1, keepdims=True)
        - scaled * jnp.mean(grads * scaled, axis=-1, keepdims=True)
    )


def gelu(inputs):
    return inputs * (0.5 * (1.0 + lax.erf(inputs * ROOT_HALF)))


def gelu_slope(inputs):
    cumulative = 0.5 * (1.0 + lax.erf(inputs * ROOT_HALF))
    density = jnp.exp(-0.5 * inputs * inputs) * (1.0 / ROOT_TWO_PI)
    return cumulative + inputs * density


def column_sum(values):
    return jnp.sum(values.astype(F32), axis=0, keepdims=True)


def head_mask(rows, head, per_group, size):
    lane = lax.broadcasted_iota(jnp.int32, (rows, LANES), 1)
    low = lax.rem(head, per_group) * size
    return (lane >= low) & (lane < low + size)


def group_of(head, per_group):
    return pl.ds(pl.multiple_of(lax.div(head, per_group) * LANES, LANES), LANES)


def attend_head(head, at, q_ref, k_ref, v_ref, per_group, size):
    cols = group_of(head, per_group)
    mask = head_mask(at.stop - at.start, head, per_group, size)
    query = jnp.where(mask, q_ref[at, cols].astype(F32), 0.0).astype(BF)
    scores = mm_nt(query, k_ref[:, cols]) * (1.0 / math.sqrt(size))
    top = jnp.max(scores, axis=-1, keepdims=True)
    weights = jnp.exp(scores - top)
    total = jnp.sum(weights, axis=-1, keepdims=True)
    mixed = mm(weights.astype(BF), v_ref[:, cols])
    return cols, mask, mixed / total, top, total


def row_cuts(own, length):
    step = own if length <= 2048 else 64
    return [slice(at, at + step) for at in range(0, own, step)]


def call(kernel, outs, scratch=(), limit=16, name=None, cost=1, far=()):
    spaces = {"vmem": pltpu.VMEM, "smem": pltpu.SMEM, "any": pl.ANY}

    def space(at, arg):
        small = arg.ndim == 1 and arg.dtype == jnp.int32
        return pl.BlockSpec(memory_space=spaces["any" if at in far else "smem" if small else "vmem"])

    def run(*args):
        return pl.pallas_call(
            kernel,
            out_shape=outs,
            in_specs=[space(at, arg) for at, arg in enumerate(args)],
            out_specs=[pl.BlockSpec(memory_space=pltpu.VMEM)] * len(outs),
            scratch_shapes=list(scratch),
            compiler_params=pltpu.CompilerParams(vmem_limit_bytes=limit * MIB),
            cost_estimate=pl.CostEstimate(
                flops=int(cost * 1e9), bytes_accessed=int(cost * 3e6), transcendentals=0
            ),
            name=name,
        )(*args)

    return run


def sds(shape, dtype):
    return jax.ShapeDtypeStruct(shape, dtype)


def lines_of(ref, first, width):
    count = -(-width // LANES)
    return jnp.concatenate([ref[at:at + 1, :] for at in range(first, first + count)], axis=1)[:, :width]


def split_kernel(*refs):
    ins, outs = refs[:-3], refs[-3:]
    rows = ins[0].shape[0]
    for turn, ref in enumerate(ins):
        at = 0
        for out in outs:
            width = out.shape[1]
            out[turn * rows:(turn + 1) * rows, :] = ref[:, at:at + width]
            at += width


def prepare_kernel(order, cap, per_device, peers, vocab_rows, at_vec, me_ref, *refs):
    many_in = 6 + len(at_vec) - 1
    sources, outs, copied = refs[:many_in], refs[many_in:many_in + 7], refs[many_in + 7:-1]
    vec_ref, live_ref, want_ref, line_ref, wqkv_ref, bqkv_ref, wo_ref = outs
    copies = [pltpu.make_async_copy(*pair, refs[-1].at[at]) for at, pair in enumerate(zip(sources, copied))]
    for copy in copies:
        copy.start()
    for copy in copies:
        copy.wait()
    pos_ref, ids_ref, wq_ref, wk_ref, wv_ref, wout_ref, *vec_refs = copied
    vec_ref[...] = jnp.zeros_like(vec_ref)
    rows_of = [ref[...].astype(F32).reshape(1, ref.shape[0]) for ref in vec_refs]
    for first, value in zip(at_vec, rows_of):
        for at in range(0, value.shape[1], LANES):
            part = value[:, at:at + LANES]
            vec_ref[first + at // LANES:first + at // LANES + 1, :part.shape[1]] = part
    width = wq_ref.shape[0]
    pad = wo_ref.shape[0]
    valid = width * LANES // pad
    row = lax.broadcasted_iota(jnp.int32, (width, pad), 0)
    col = lax.broadcasted_iota(jnp.int32, (width, pad), 1)
    inside = lax.rem(col, LANES)
    select = jnp.where((inside < valid) & (row == lax.div(col, LANES) * valid + inside), 1.0, 0.0).astype(BF)
    for at, ref in enumerate((wq_ref, wk_ref, wv_ref)):
        wqkv_ref[:, at * pad:(at + 1) * pad] = mm(ref[...], select).astype(BF)
        bias = jnp.broadcast_to(rows_of[8 + at], (8, width)).astype(BF)
        bqkv_ref[:, at * pad:(at + 1) * pad] = mm(bias, select)[:1]
    wo_ref[...] = mm_tn(select, wout_ref[...]).astype(BF)

    planes, many = pos_ref.shape
    z_at, p_at = me_ref[0], me_ref[1]
    first = (z_at * peers + p_at) * vocab_rows
    lane = lax.broadcasted_iota(jnp.int32, (8, LANES), 1)

    def lines(ref, seq, peer):
        whole = jnp.broadcast_to(ref[pl.ds(seq, 1), :], (8, many))
        out = jnp.full((8, LANES), -1, jnp.int32)
        for plane in range(planes):
            shift = lax.rem(plane * cap - (plane * peers + peer) * cap + 2 * many, many)
            moved = pltpu.roll(whole, shift, 1)[:, :LANES]
            out = jnp.where((lane >= plane * cap) & (lane < (plane + 1) * cap), moved, out)
        return out

    own = lines(pos_ref, z_at, p_at)
    local = own
    for plane in range(planes):
        move = jnp.bitwise_xor(z_at, plane) * per_device - (plane * peers + p_at) * per_device
        local = jnp.where((lane >= plane * cap) & (lane < (plane + 1) * cap), own + move, local)
    line_ref[...] = jnp.where(own >= 0, local, -1)[:1]

    def one(turn, carry):
        key = jnp.int32(0)
        for bit, value in enumerate(order):
            key = jnp.where(lax.rem(lax.div(turn, 1 << bit), 2) == 1, jnp.bitwise_xor(key, value), key)
        for plane in range(planes):
            seq, peer = jnp.bitwise_xor(z_at, plane), jnp.bitwise_xor(p_at, key)
            live_ref[turn * planes + plane] = jnp.where(lines(pos_ref, seq, peer) >= 0, 1.0, 0.0)[:1]
            want_ref[turn * planes + plane] = (lines(ids_ref, seq, peer) - first)[:1]
        return carry

    lax.fori_loop(0, peers, one, 0)


def hot_kernel(slots, want_ref, table_ref, hot_ref, hot_scr):
    rows, vocab_rows = hot_scr.shape
    planes = rows // slots
    column = lax.broadcasted_iota(jnp.int32, (slots, vocab_rows), 1)

    def one(turn, carry):
        for plane in range(planes):
            ids = jnp.broadcast_to(want_ref[turn * planes + plane].astype(F32), (LANES, LANES)).T
            hot_scr[plane * slots:(plane + 1) * slots, :] = jnp.where(
                column == ids[:slots, :1].astype(jnp.int32), 1.0, 0.0
            ).astype(BF)
        hot_ref[pl.ds(pl.multiple_of(turn * rows, rows), rows), :] = mm(hot_scr[...], table_ref[...]).astype(BF)
        return carry

    lax.fori_loop(0, hot_ref.shape[0] // rows, one, 0)


def place_kernel(me_ref, *refs):
    *ins, out_ref = refs
    for key, ref in enumerate(ins):
        out_ref[jnp.bitwise_xor(me_ref[0], key)] = ref[...].astype(out_ref.dtype)


def pick(line_ref, slots, values):
    own = values.shape[0]
    at = lax.broadcasted_iota(jnp.int32, (own, LANES), 0)
    chosen = jnp.where(at == line_ref[...], 1.0, 0.0).astype(BF)
    return mm_tn(chosen, values)[:slots]


def teacher_attend_kernel(tq_ref, tk_ref, tv_ref, *refs):
    *row_refs, att_ref, q_ref, k_ref, v_scr = refs
    own = q_ref.shape[0]
    width = tq_ref.shape[1]
    size = width // HEADS
    per_group = LANES // size
    wide = v_scr.shape[1]
    per_wide = wide // size
    cuts = row_cuts(own, v_scr.shape[0])
    q_ref[...] = mm(row_refs[0][:own], tq_ref[...]).astype(BF)
    att_ref[...] = jnp.zeros_like(att_ref)
    for part in range(width // wide):
        cols = slice(part * wide, (part + 1) * wide)
        at = 0
        for row_ref in row_refs:
            there = slice(at, at + row_ref.shape[0])
            k_ref[there, cols] = mm(row_ref[...], tk_ref[:, cols]).astype(BF)
            v_scr[there, :] = mm(row_ref[...], tv_ref[:, cols]).astype(BF)
            at += row_ref.shape[0]
        q_part, k_part = q_ref.at[:, cols], k_ref.at[:, cols]

        def one(head, carry):
            at = pl.ds(pl.multiple_of(lax.div(head, per_group) * LANES + part * wide, LANES), LANES)
            for cut in cuts:
                _, mask, mixed, _, _ = attend_head(head, cut, q_part, k_part, v_scr, per_group, size)
                att_ref[cut, at] = jnp.where(mask, mixed, att_ref[cut, at])
            return carry

        lax.fori_loop(0, per_wide, one, 0, unroll=2 if len(cuts) == 1 else 1)


def teacher_feed_kernel(line_ref, rows_ref, att_ref, to_ref, up_ref, down_ref, out_ref, pick_ref):
    own, width = att_ref.shape
    branch = mm(att_ref[...].astype(BF), to_ref[...])
    hidden, _ = normalize(rows_ref[:own].astype(F32) + branch)
    low = hidden.astype(BF)
    step = width
    outer = jnp.zeros((own, width), F32)
    for at in range(0, up_ref.shape[1], step):
        inner = gelu(mm(low, up_ref[:, at:at + step])).astype(BF)
        outer = outer + mm(inner, down_ref[at:at + step])
    output, _ = normalize(hidden + outer)
    out_ref[...] = output
    pick_ref[...] = pick(line_ref, pick_ref.shape[0], output.astype(BF)).astype(BF)


def student_kernel(
    at_vec, line_ref, vec_ref, wqkv_ref, bqkv_ref, wo_ref, up_ref, down_ref, *refs,
):
    *row_refs, q_ref, kv_ref, keep_ref, out_ref, pick_ref = refs
    own, pad = q_ref.shape
    length = kv_ref.shape[0]
    width = wo_ref.shape[1]
    ff = up_ref.shape[1]
    size = width // HEADS
    per_group = HEADS * LANES // pad
    rows = row_refs[0][:own]
    q_ref[...] = (mm(rows, wqkv_ref[:, :pad]) + bqkv_ref[:, :pad]).astype(BF)
    at = 0
    for row_ref in row_refs:
        there = slice(at, at + row_ref.shape[0])
        kv_ref[there, :] = (mm(row_ref[...], wqkv_ref[:, pad:]) + bqkv_ref[:, pad:]).astype(BF)
        at += row_ref.shape[0]
    k_ref, v_ref = kv_ref.at[:, :pad], kv_ref.at[:, pad:]
    keep_ref[...] = jnp.zeros_like(keep_ref)
    cuts = row_cuts(own, length)
    lane = lax.broadcasted_iota(jnp.int32, (cuts[0].stop, LANES), 1)
    stat = slice(3 * pad, 3 * pad + LANES)

    def one(head, carry):
        for cut in cuts:
            group, mask, mixed, top, total = attend_head(head, cut, q_ref, k_ref, v_ref, per_group, size)
            keep_ref[cut, group] = jnp.where(mask, mixed, keep_ref[cut, group])
            keep_ref[cut, stat] = jnp.where(lane == head, top + jnp.log(total), keep_ref[cut, stat])
        return carry

    lax.fori_loop(0, HEADS, one, 0, unroll=2 if len(cuts) == 1 else 1)
    bo, g1, c1, bdown, g2, c2 = (lines_of(vec_ref, at, width) for at in at_vec[:6])
    branch = mm(keep_ref[:, :pad].astype(BF), wo_ref[...]) + bo
    n1, i1 = normalize(rows.astype(F32) + branch)
    hidden = n1 * g1 + c1
    inner = mm(hidden.astype(BF), up_ref[...]) + lines_of(vec_ref, at_vec[6], ff)
    outer = mm_nt(gelu(inner).astype(BF), down_ref[...]) + bdown
    n2, i2 = normalize(hidden + outer)
    output = (n2 * g2 + c2).astype(BF)
    keep_ref[:, pad:pad + width] = n1
    keep_ref[:, 2 * pad:2 * pad + width] = n2
    at = lax.broadcasted_iota(jnp.int32, (own, LANES), 1)
    keep_ref[:, stat] = jnp.where(at == HEADS, i1, jnp.where(at == HEADS + 1, i2, keep_ref[:, stat]))
    out_ref[...] = output
    pick_ref[...] = pick(line_ref, pick_ref.shape[0], output).astype(BF)


def logits_kernel(at_bias, slots, *refs):
    if at_bias is None:
        rows_ref, table_ref, mix_ref, top_ref, lse_ref = refs
    else:
        rows_ref, table_ref, proj_ref, vec_ref, mix_ref, top_ref, lse_ref = refs
    block = 2 * slots
    lane = lax.broadcasted_iota(jnp.int32, (block, LANES), 1)

    def one(step, carry):
        for half in range(2):
            at = pl.ds(pl.multiple_of((2 * step + half) * block, block), block)
            picked = rows_ref[at, :]
            if at_bias is not None:
                picked = (mm(picked, proj_ref[...]) + lines_of(vec_ref, at_bias, proj_ref.shape[1])).astype(BF)
            logits = mm_nt(picked, table_ref[...])
            top = jnp.max(logits, axis=-1, keepdims=True)
            weights = jnp.exp(logits - top)
            total = top + jnp.log(jnp.sum(weights, axis=-1, keepdims=True))
            mix_ref[at, :] = mm(weights.astype(BF), table_ref[...]).astype(BF)
            both = jnp.where(lane == 0, top, jnp.where(lane == 1, total, 0.0))
            for part in range(2):
                value = both[part * slots:(part + 1) * slots]
                if slots < LANES:
                    value = jnp.concatenate([value, jnp.zeros((LANES - slots, LANES), F32)], axis=0)
                value = value.T
                top_ref[4 * step + 2 * half + part] = value[0:1]
                lse_ref[4 * step + 2 * half + part] = value[1:2]
        return carry

    steps = rows_ref.shape[0] // (2 * block)
    if steps == 1:
        one(0, 0)
    else:
        lax.fori_loop(0, steps, one, 0)


def combine_kernel(first, slots, chained, *refs):
    if chained:
        gproj_in, gbproj_in, *refs = refs
    (
        live_ref, s_top_ref, t_top_ref, all_ref, s_mix_ref, t_mix_ref, hot_ref, rows_ref, proj_ref,
        back_ref, gproj_ref, gbproj_ref, low_scr,
    ) = refs
    blocks = s_top_ref.shape[0]
    sources = all_ref.shape[0]
    line = lax.broadcasted_iota(jnp.int32, (LANES, LANES), 0)
    gbproj_ref[...] = gbproj_in[...] if chained else jnp.zeros_like(gbproj_ref)

    def share(block, which, top):
        known = [all_ref[key, jnp.bitwise_xor(block, key), which:which + 1, :] for key in range(sources)]
        peak = functools.reduce(jnp.maximum, known)
        total = functools.reduce(jnp.add, [jnp.exp(value - peak) for value in known])
        return jnp.exp(top - peak) / total

    def one(step, carry):
        block = step + first
        at = pl.ds(pl.multiple_of(step * slots, slots), slots)
        live = CE_WEIGHT * live_ref[block]
        s_part = live * share(block, 0, s_top_ref[step])
        t_part = live * (MIXING * share(block, 1, t_top_ref[step]))
        lines = jnp.where(line == 0, s_part, jnp.where(line == 1, t_part, live * (1.0 - MIXING)))
        cols = lines.T[:slots]
        grads = (
            cols[:, 0:1] * s_mix_ref[at, :].astype(F32)
            - cols[:, 1:2] * t_mix_ref[at, :].astype(F32)
            - cols[:, 2:3] * hot_ref[at, :].astype(F32)
        )
        low_scr[at, :] = grads.astype(BF)
        gbproj_ref[...] += column_sum(grads)
        return carry

    if blocks <= 4:
        for step in range(blocks):
            one(step, 0)
    else:
        lax.fori_loop(0, blocks, one, 0)
    low = low_scr[...]
    back_ref[...] = mm_nt(low, proj_ref[...]).astype(BF)
    gproj = mm_tn(rows_ref[...], low)
    gproj_ref[...] = gproj + gproj_in[...] if chained else gproj


def place(me_ref):
    peer = me_ref[1]
    return me_ref[2] * 2 + lax.rem(lax.div(peer, 2), 2), me_ref[0], lax.rem(peer, 2)


def scatter_blocks(stage_ref, me, keep_ref, send_ref):
    xy_at, z_at, c_at = me
    planes = keep_ref.shape[1]
    rows, wide = keep_ref.shape[2:]
    half = planes * wide
    for xy in range(4):
        for plane in range(planes):
            at, lanes = xy * rows, plane * wide
            key = (jnp.bitwise_xor(xy, xy_at), jnp.bitwise_xor(plane, z_at))
            low = stage_ref[at:at + rows, lanes:lanes + wide]
            high = stage_ref[at:at + rows, half + lanes:half + lanes + wide]
            keep_ref[key] = jnp.where(c_at == 0, low, high).astype(BF)
            send_ref[key] = jnp.where(c_at == 0, high, low).astype(BF)


def feed_back_kernel(
    layout, at_vec, me_ref, line_ref, vec_ref, gproj_ref, gbproj_ref, proj_ref, down_ref, up_ref, wo_ref,
    og_ref, tout_ref, out_ref, keep_ref, *refs,
):
    *ce_refs, datt_ref, dres_ref, mine_ref, send_ref, stage_ref = refs
    own, width = og_ref.shape
    pad = wo_ref.shape[0]
    at_up, at_down, at_proj, at_out = layout
    t_width = proj_ref.shape[1]
    ff = up_ref.shape[1]
    at = lax.broadcasted_iota(jnp.int32, (own, LANES), 0)
    slots = ce_refs[0].shape[0]
    chosen = jnp.where(at == line_ref[...], 1.0, 0.0).astype(BF)[:, :slots]
    ce = functools.reduce(jnp.add, [ref[...].astype(F32) for ref in ce_refs])
    high = ce.astype(BF)
    rest = (ce - high.astype(F32)).astype(BF)
    scattered = mm(chosen, high) + mm(chosen, rest)
    g1, c1, g2 = (lines_of(vec_ref, at_vec[at], width) for at in (1, 2, 4))
    n1, n2 = keep_ref[:, pad:pad + width], keep_ref[:, 2 * pad:2 * pad + width]
    stat = 3 * pad + HEADS
    i1, i2 = keep_ref[:, stat:stat + 1], keep_ref[:, stat + 1:stat + 2]
    hidden = (n1 * g1 + c1).astype(BF)
    inner = mm(hidden, up_ref[...]) + lines_of(vec_ref, at_vec[6], ff)
    cumulative = 0.5 * (1.0 + lax.erf(inner * ROOT_HALF))
    active = (inner * cumulative).astype(BF)
    slope = cumulative + inner * (jnp.exp(-0.5 * inner * inner) * (1.0 / ROOT_TWO_PI))
    output = out_ref[...]
    mapped = mm(output, proj_ref[...]) + lines_of(vec_ref, at_vec[7], t_width)
    d_map = (2.0 * HID_WEIGHT * (mapped - tout_ref[...])).astype(BF)
    stage_ref[width:, :] = jnp.zeros((stage_ref.shape[0] - width, stage_ref.shape[1]), F32)
    stage_ref[:width, at_proj:at_proj + t_width] = mm_tn(output, d_map) + gproj_ref[...]
    stage_ref[width:width + 1, at_proj:at_proj + t_width] = column_sum(d_map) + gbproj_ref[...]
    d_out = og_ref[...].astype(F32) + mm_nt(d_map, proj_ref[...]) + scattered
    d_res2 = norm_back(d_out * g2, n2, i2)
    d_outer = d_res2.astype(BF)
    stage_ref[:width, at_down:at_down + ff] = mm_tn(d_outer, active)
    d_inner = (mm(d_outer, down_ref[...]) * slope).astype(BF)
    stage_ref[:width, at_up:at_up + ff] = mm_tn(hidden, d_inner)
    stage_ref[width:width + 1, at_up:at_up + ff] = column_sum(d_inner)
    d_hid = d_res2 + mm_nt(d_inner, up_ref[...])
    d_res1 = norm_back(d_hid * g1, n1, i1)
    d_branch = d_res1.astype(BF)
    datt_ref[...] = mm_nt(d_branch, wo_ref[...]).astype(BF)
    dres_ref[...] = d_res1
    gout = mm_tn(keep_ref[:, :pad].astype(BF), d_branch)
    head_groups = pad // LANES
    valid = width // head_groups
    for group in range(head_groups):
        stage_ref[group * valid:(group + 1) * valid, at_out:at_out + width] = gout[group * LANES:group * LANES + valid]
    lines = [
        column_sum(d_branch),
        column_sum(d_hid * n1),
        column_sum(d_hid),
        column_sum(d_outer),
        column_sum(d_out * n2),
        column_sum(d_out),
    ]
    for at, value in enumerate(lines):
        stage_ref[width + at:width + at + 1, at_out:at_out + width] = value
    scatter_blocks(stage_ref, place(me_ref), mine_ref, send_ref)


def attend_back_kernel(
    weight_mse, size, group, datt_ref, keep_ref, q_ref, kv_ref, tq_ref, tk_ref,
    dq_ref, dk_ref, dv_ref, sums_ref, dq_scr,
):
    own, pad = q_ref.shape
    per_group = HEADS * LANES // pad
    t_size = tq_ref.shape[1] // HEADS
    t_group = LANES // t_size
    length = kv_ref.shape[0]
    chunk = length if length <= 2048 else 256
    cols = slice(group * LANES, (group + 1) * LANES)
    v_cols = slice(pad + group * LANES, pad + (group + 1) * LANES)
    s_scaling = 1.0 / math.sqrt(size)
    t_scaling = 1.0 / math.sqrt(t_size)
    lane = lax.broadcasted_iota(jnp.int32, (own, LANES), 1)
    query_all = q_ref[:, cols].astype(F32)
    grad_all = datt_ref[:, cols].astype(F32)
    product = grad_all * keep_ref[:, cols]
    lses = keep_ref[:, 3 * pad:].T
    dots = jnp.zeros((own, LANES), F32)
    heads = []
    for turn in range(per_group):
        head = group * per_group + turn
        mask = (lane >= turn * size) & (lane < (turn + 1) * size)
        dots = jnp.where(lane == turn, jnp.sum(jnp.where(mask, product, 0.0), axis=-1, keepdims=True), dots)
        t_cols = slice(head // t_group * LANES, (head // t_group + 1) * LANES)
        t_low = head % t_group * t_size
        t_mask = (lane >= t_low) & (lane < t_low + t_size)
        heads.append((
            mask,
            jnp.where(mask, query_all, 0.0).astype(BF),
            jnp.where(mask, grad_all, 0.0).astype(BF),
            t_cols,
            jnp.where(t_mask, tq_ref[:, t_cols].astype(F32), 0.0).astype(BF),
            lses[head:head + 1],
        ))
    dots = dots.T
    dq_scr[...] = jnp.zeros_like(dq_scr)
    sums_ref[...] = jnp.zeros_like(sums_ref)

    def one_chunk(at):
        keys, values = kv_ref[at, cols], kv_ref[at, v_cols]
        d_keys, d_values = jnp.zeros(keys.shape, F32), jnp.zeros(keys.shape, F32)
        for turn, (mask, query, grad, t_cols, t_query, lse) in enumerate(heads):
            scores = mm_nt(keys, query) * s_scaling
            probs = jnp.exp(scores - lse)
            teacher = mm_nt(tk_ref[at, t_cols], t_query) * t_scaling
            d_probs = mm_nt(values, grad)
            d_scores = (
                probs * (d_probs - dots[turn:turn + 1]) + weight_mse * (scores - teacher)
            ).astype(BF)
            d_keys += mm(d_scores, query)
            d_values += mm(probs.astype(BF), grad)
            dq_scr[...] += jnp.where(mask, mm_tn(d_scores, keys), 0.0)
        d_keys = d_keys * s_scaling
        sums_ref[1:2, :] += column_sum(d_keys)
        sums_ref[2:3, :] += column_sum(d_values)
        dk_ref[at, :] = d_keys.astype(BF)
        dv_ref[at, :] = d_values.astype(BF)

    if chunk == length:
        one_chunk(slice(0, length))
    else:

        def inside(turn, carry):
            one_chunk(pl.ds(pl.multiple_of(turn * chunk, chunk), chunk))
            return carry

        lax.fori_loop(0, length // chunk, inside, 0)
    d_queries = dq_scr[...] * s_scaling
    sums_ref[0:1, :] = column_sum(d_queries)
    dq_ref[...] = d_queries.astype(BF)


def attend_out_kernel(groups, me_ref, wqkv_ref, dres_ref, *refs):
    dq_refs, dk_refs, dv_refs, sum_refs = (refs[at * groups:(at + 1) * groups] for at in range(4))
    *row_refs, far_ref, near_ref, own_ref, mine_ref, send_ref, g_scr, stage_ref = refs[4 * groups:]
    own, width = dres_ref.shape
    pad = groups * LANES
    half = far_ref.shape[0]
    piece = row_refs[0].shape[0]
    g_scr[width:, :] = jnp.zeros((g_scr.shape[0] - width, g_scr.shape[1]), F32)
    total = dres_ref[...]
    for group in range(groups):
        cols = slice(group * LANES, (group + 1) * LANES)
        g_scr[:width, cols] = mm_tn(row_refs[0][:own], dq_refs[group][...])
        total = total + mm_nt(dq_refs[group][...], wqkv_ref[:, cols])
        for which, refs_of in ((1, dk_refs), (2, dv_refs)):
            there = slice(which * pad + group * LANES, which * pad + (group + 1) * LANES)
            parts = [
                mm_tn(row_ref[...], refs_of[group][at * piece:(at + 1) * piece, :]) for at, row_ref in enumerate(row_refs)
            ]
            g_scr[:width, there] = functools.reduce(jnp.add, parts)
        for which in range(3):
            there = slice(which * pad + group * LANES, which * pad + (group + 1) * LANES)
            g_scr[width:width + 1, there] = sum_refs[group][which:which + 1, :]
    own_ref[...] = total
    step = min(half, 512)
    for at in range(0, 2 * half, step):
        there = slice(at, at + step)
        back = jnp.zeros((step, width), F32)
        for group in range(groups):
            k_cols = slice(pad + group * LANES, pad + (group + 1) * LANES)
            v_cols = slice(2 * pad + group * LANES, 2 * pad + (group + 1) * LANES)
            back += mm_nt(dk_refs[group][there, :], wqkv_ref[:, k_cols])
            back += mm_nt(dv_refs[group][there, :], wqkv_ref[:, v_cols])
        out_ref, start = (near_ref, at) if at < half else (far_ref, at - half)
        out_ref[start:start + step, :] = back.astype(BF)
    valid = width // groups
    parts = [g_scr[:, at * LANES:at * LANES + valid] for at in range(3 * groups)]
    stage_ref[...] = jnp.zeros_like(stage_ref)
    stage_ref[:, :3 * width] = jnp.concatenate(parts, axis=1)
    scatter_blocks(stage_ref, place(me_ref), mine_ref, send_ref)


def add_kernel(many, *refs):
    ins, outs = refs[:many], refs[many:]
    for at, out in enumerate(outs):
        if out.ndim == ins[0].ndim:
            size = out.shape[0]
            parts = [ref[at * size:(at + 1) * size] for ref in ins]
        else:
            parts = [ref[at] for ref in ins]
        out[...] = functools.reduce(jnp.add, [part.astype(F32) for part in parts]).astype(out.dtype)


def unpack_kernel(layout, ff, width, t_width, me_ref, mine_ref, other_ref, *refs):
    gq, gk, gv, gout, gup, gdown, gproj, *vec_refs, wide_ref, thin_ref = refs
    at_up, at_down, at_proj, at_out = layout
    xy_at, z_at, c_at = place(me_ref)
    planes, rows = mine_ref.shape[1:3]
    wide, thin = (ref.shape[1] // (2 * planes) for ref in (wide_ref, thin_ref))
    for core in range(2):
        for xy in range(4):
            for plane in range(planes):
                key = (jnp.bitwise_xor(xy, xy_at), jnp.bitwise_xor(plane, z_at))
                block = jnp.where(c_at == core, mine_ref[key], other_ref[key]).astype(F32)
                at, lanes = slice(xy * rows, (xy + 1) * rows), core * planes + plane
                wide_ref[at, lanes * wide:(lanes + 1) * wide] = block[:, :wide]
                thin_ref[at, lanes * thin:(lanes + 1) * thin] = block[:, wide:]
    gup[...] = wide_ref[:width, at_up:at_up + ff]
    gdown[...] = wide_ref[:width, at_down:at_down + ff]
    gproj[...] = wide_ref[:width, at_proj:at_proj + t_width]
    gout[...] = wide_ref[:width, at_out:at_out + width]
    for at, grad in enumerate((gq, gk, gv)):
        grad[...] = thin_ref[:width, at * width:(at + 1) * width]

    def put(which, row):
        vec_refs[which][...] = row.reshape(row.shape[1])

    for at in range(6):
        put(at, wide_ref[width + at:width + at + 1, at_out:at_out + width])
    put(6, wide_ref[width:width + 1, at_up:at_up + ff])
    put(7, wide_ref[width:width + 1, at_proj:at_proj + t_width])
    for at in range(3):
        put(8 + at, thin_ref[width:width + 1, at * width:(at + 1) * width])


def swap(value, axis, key):
    if isinstance(axis, tuple):
        size = math.prod(lax.axis_size(name) for name in axis)
    else:
        size = lax.axis_size(axis)
    return lax.ppermute(value, axis, [(at, at ^ key) for at in range(size)])


def swap_xy(value, key):
    return swap(value, ("batch", "p"), (key // 2) * lax.axis_size("p") + (key % 2) * 2)


def bits_of(size):
    return [1 << at for at in range(size.bit_length() - 1)]


def after(values, *done):
    return lax.optimization_barrier((values, done))[0]


def spread_over_z(parts):
    return [parts[0]] + [swap(parts[key], "z", key) for key in range(1, len(parts))]


def plane_pieces(value):
    bits = list(reversed(bits_of(lax.axis_size("p"))))
    for bit in bits[:-2]:
        value = jnp.concatenate([value, swap(value, "p", bit)], axis=0)
    pieces = [value]
    for bit in bits[-2:]:
        pieces = pieces + [swap(piece, "p", bit) for piece in pieces]
    return pieces


def gather_z(value):
    return jnp.concatenate([value] + [swap(value, "z", key) for key in range(1, lax.axis_size("z"))], axis=0)


def gather_plane(value):
    for bit in reversed(bits_of(lax.axis_size("p"))):
        value = jnp.concatenate([value, swap(value, "p", bit)], axis=0)
    return value


def add_cut(values, parts, dtype=BF):
    rows = values[0].shape[0] // parts
    shape = values[0].shape[1:] if rows == 1 else (rows,) + values[0].shape[1:]
    return call(functools.partial(add_kernel, len(values)), [sds(shape, dtype)] * parts, name="add", cost=0.5)(*values)


def add_low(*values):
    return add_cut(values, 1)[0]


def gather_blocks(value):
    value = jnp.stack([value] + [swap(value, "z", key) for key in range(1, lax.axis_size("z"))])
    value = jnp.stack([value] + [swap_xy(value, key) for key in range(1, 4)])
    return value, swap(value, "p", 1)


def body(
    tokens_in, teacher_in, out_grad, mask_pos, slot_ids, w_query, b_query, w_key, b_key, w_value,
    b_value, w_out, b_out, ln1_gain, ln1_bias, w_up, b_up, w_down, b_down, ln2_gain, ln2_bias,
    w_proj, b_proj, t_query, t_key, t_value, t_out, t_up, t_down, embedding,
):
    planes, peers = lax.axis_size("z"), lax.axis_size("p")
    z_at, p_at = lax.axis_index("z"), lax.axis_index("p")
    me = jnp.stack([z_at, p_at, lax.axis_index("batch")]).astype(jnp.int32)
    groups = planes * peers
    seq_count, per_device, width = tokens_in.shape
    t_width = teacher_in.shape[2]
    ff = w_up.shape[1]
    own = seq_count * per_device
    length = per_device * groups
    cap = mask_pos.shape[1] // groups
    slots = planes * cap
    size = width // HEADS
    per_group = max(n for n in range(1, LANES // size + 1) if HEADS % n == 0)
    pad = HEADS // per_group * LANES
    roomy = 16 + length // 256

    vectors = (b_out, ln1_gain, ln1_bias, b_down, ln2_gain, ln2_bias, b_up, b_proj, b_query, b_key, b_value)
    at_vec = [0]
    for vector in vectors:
        at_vec.append(at_vec[-1] - (-vector.shape[0] // LANES))
    vec_lines = -(-at_vec[-1] // 8) * 8
    down = w_down.T

    def side_by_side(plane):
        parts = [lax.dynamic_index_in_dim(x, plane, 0, keepdims=False) for x in (teacher_in, tokens_in, out_grad)]
        return jnp.concatenate(parts, axis=1)

    t_rows, s_rows, og_rows = call(
        split_kernel, [sds((own, t_width), BF), sds((own, width), BF), sds((own, width), BF)], name="split"
    )(*spread_over_z([side_by_side(z_at ^ key) for key in range(planes)]))
    s_pieces = plane_pieces(s_rows)
    t_pieces = plane_pieces(after(t_rows, s_pieces[1]))

    raws = (mask_pos, slot_ids, w_query, w_key, w_value, w_out) + vectors
    vec, live, want, line, wqkv, bqkv, wo = call(
        functools.partial(
            prepare_kernel, list(reversed(bits_of(peers))), cap, per_device, peers, embedding.shape[0], at_vec
        ),
        [
            sds((vec_lines, LANES), F32), sds((groups, 1, LANES), F32), sds((groups, 1, LANES), jnp.int32),
            sds((1, LANES), jnp.int32), sds((width, 3 * pad), BF), sds((1, 3 * pad), F32), sds((pad, width), BF),
        ],
        [pltpu.VMEM(raw.shape, raw.dtype) for raw in raws] + [pltpu.SemaphoreType.DMA((len(raws),))],
        name="prepare",
        cost=3,
        far=range(1, 1 + len(raws)),
    )(me, *raws)
    hot = call(
        functools.partial(hot_kernel, slots),
        [sds((groups * slots, t_width), BF)],
        [pltpu.VMEM((planes * slots, embedding.shape[0]), BF)],
        name="hot",
        cost=6,
    )(want, embedding)[0]

    q, kv, keep, output, s_pick = call(
        functools.partial(student_kernel, at_vec),
        [
            sds((own, pad), BF), sds((length, 2 * pad), BF), sds((own, 3 * pad + LANES), F32),
            sds((own, width), BF), sds((slots, width), BF),
        ],
        limit=roomy,
        name="student",
        cost=10,
    )(line, vec, wqkv, bqkv, wo, w_up, down, *s_pieces)

    wide = min(2 * LANES, t_width)
    t_att, t_q, t_k = call(
        teacher_attend_kernel,
        [sds((own, t_width), F32), sds((own, t_width), BF), sds((length, t_width), BF)],
        [pltpu.VMEM((length, wide), BF)],
        limit=roomy,
        name="teacher_attend",
        cost=9,
    )(t_query, t_key, t_value, *t_pieces)
    t_output, t_pick = call(
        teacher_feed_kernel,
        [sds((own, t_width), F32), sds((slots, t_width), BF)],
        name="teacher_feed",
        cost=6,
    )(line, t_pieces[0], t_att, t_out, t_up, t_down)

    def placed(parts, dtype):
        return call(place_kernel, [sds((planes, per_device, width), dtype)], name="place")(me, *spread_over_z(parts))[0]

    s_z = gather_z(s_pick)
    t_parts = spread_over_z([t_pick] * planes)
    s_all = plane_pieces(after(s_z, t_att))
    s_all = after(s_all, t_parts[1])
    here = s_all[0].shape[0]
    blocks = here // slots
    stat_shape = sds((blocks, 1, LANES), F32)
    mix_shapes = [sds((here, t_width), BF), stat_shape, stat_shape]
    t_logits = call(functools.partial(logits_kernel, None, slots), mix_shapes, name="t_logits", cost=4)
    s_logits = call(functools.partial(logits_kernel, at_vec[7], slots), mix_shapes, name="s_logits", cost=4)
    s_done = [s_logits(piece, embedding, w_proj, vec) for piece in s_all]
    t_all = plane_pieces(after(jnp.concatenate(t_parts, axis=0), s_done[0][0], s_done[1][0], s_done[2][0]))
    s_mix, s_top, s_lse = zip(*s_done)
    t_mix, t_top, t_lse = zip(*[t_logits(piece, embedding) for piece in t_all])
    stat = jnp.concatenate([jnp.concatenate(s_lse, axis=0), jnp.concatenate(t_lse, axis=0)], axis=1)
    stats = gather_plane(gather_z(stat[None]))
    sums = []

    def combined(turn):
        outs = [sds((here, width), BF), sds((width, t_width), F32), sds((1, t_width), F32)]
        back, *sums[:] = call(
            functools.partial(combine_kernel, turn * blocks, slots, bool(sums)),
            outs,
            [pltpu.VMEM((here, t_width), BF)],
            name="combine", cost=1,
        )(
            *sums, live, s_top[turn], t_top[turn], stats, s_mix[turn], t_mix[turn],
            hot[turn * here:(turn + 1) * here], s_all[turn], w_proj,
        )
        return back

    def reduced(turn, bits):
        if not bits:
            return combined(turn)
        bit = bits[-1]
        far = swap(reduced(turn + len(s_all) // (2 * bit), bits[:-1]), "p", bit)
        near = reduced(turn, bits[:-1])
        if len(bits) == 2 and peers == 4:
            return add_cut([near, far], planes)
        return add_low(near, far)

    back = reduced(0, bits_of(len(s_all)))
    for bit in bits_of(peers)[2:]:
        half = back.shape[0] // 2
        back = add_low(back[:half], swap(back[half:], "p", bit))
    if peers > 4:
        back = add_cut([back], planes)
    ce = spread_over_z(back)

    lanes_of = lambda many: -(-many // LANES) * LANES
    at_up, at_down = 0, lanes_of(ff)
    at_proj = at_down + lanes_of(ff)
    at_out = at_proj + lanes_of(t_width)
    layout = (at_up, at_down, at_proj, at_out)
    unit = 2 * planes * LANES
    wide_lanes = -(-(at_out + lanes_of(width)) // unit) * unit
    thin_lanes = -(-3 * width // unit) * unit
    tall = -(-(width + 8) // 64) * 64
    wide_block = sds((4, planes, tall // 4, wide_lanes // (2 * planes)), BF)
    thin_block = sds((4, planes, tall // 4, thin_lanes // (2 * planes)), BF)
    d_att, d_res, wide_mine, wide_send = call(
        functools.partial(feed_back_kernel, layout, at_vec),
        [sds((own, pad), BF), sds((own, width), F32), wide_block, wide_block],
        [pltpu.VMEM((tall, wide_lanes), F32)],
        name="feed_back", cost=4,
    )(me, line, vec, *sums, w_proj, down, w_up, wo, og_rows, t_output, output, keep, *ce)

    def attend_back(group, *done):
        return call(
            functools.partial(attend_back_kernel, 2.0 / (HEADS * length), size, group),
            [sds((own, LANES), BF), sds((length, LANES), BF), sds((length, LANES), BF), sds((8, LANES), F32)],
            [pltpu.VMEM((own, LANES), F32)],
            limit=20,
            name="attend_back",
            cost=6,
        )(after(d_att, *done), keep, q, kv, t_q, t_k)

    head_groups = pad // LANES
    wide_other = swap(wide_send, "p", 1)
    wide_parts = add_cut([wide_mine, wide_other], 4)
    wide_near = [swap_xy(wide_parts[key], key) for key in range(1, 4)]
    grads = [attend_back(0)]
    for group in range(1, head_groups):
        grads.append(attend_back(group, wide_parts[0], *grads[-1]))
    wide_line = add_cut([wide_parts[0]] + wide_near, planes)
    out_blocks = after(output, wide_parts[0]).reshape(planes, per_device, width)
    layer_out = placed([out_blocks[key] for key in range(planes)], BF)
    g_far, g_near, g_own, thin_mine, thin_send = call(
        functools.partial(attend_out_kernel, head_groups),
        [
            sds((length // 2, width), BF), sds((length // 2, width), BF), sds((own, width), F32), thin_block, thin_block,
        ],
        [pltpu.VMEM((tall, 3 * pad), F32), pltpu.VMEM((tall, thin_lanes), F32)],
        name="attend_out",
        cost=4,
    )(me, wqkv, after(d_res, layer_out, *wide_line), *[part for kind in zip(*grads) for part in kind], *s_pieces)

    thin_other, g_other = swap(thin_send, "p", 1), swap(g_far, "p", 1)
    g_parts = add_cut([g_near, g_other], peers // 2)
    for bit in bits_of(peers)[1:-1]:
        half = len(g_parts) // 2
        moved = swap(jnp.concatenate(g_parts[half:], axis=0), "p", bit)
        g_parts = add_cut([jnp.concatenate(g_parts[:half], axis=0), moved], half)
    total = add_cut([g_own, g_parts[0], swap(g_parts[1], "p", bits_of(peers)[-1])], planes)
    input_grad = placed(total, F32)

    thin_parts = add_cut([thin_mine, thin_other], 4)
    thin_near = [swap_xy(thin_parts[key], key) for key in range(1, 4)]

    def sum_line(line_parts):
        value = add_low(line_parts[0], *[swap(line_parts[key], "z", key) for key in range(1, planes)])
        for bit in bits_of(peers)[2:]:
            value = add_low(value, swap(value, "p", bit))
        return value

    wide_sum = sum_line(wide_line)
    thin_sum = sum_line(add_cut([thin_parts[0]] + thin_near, planes))
    mine, other = gather_blocks(jnp.concatenate([wide_sum, thin_sum], axis=1))
    square = sds((width, width), F32)
    gq, gk, gv, gout, gup, gdown, gproj, *vecs = call(
        functools.partial(unpack_kernel, layout, ff, width, t_width),
        [
            square, square, square, square, sds((width, ff), F32), sds((width, ff), F32), sds((width, t_width), F32),
        ] + [sds(vector.shape, F32) for vector in vectors],
        [pltpu.VMEM((tall, wide_lanes), F32), pltpu.VMEM((tall, thin_lanes), F32)],
        limit=24,
        name="unpack",
        cost=3,
    )(me, mine, other)
    gbo, gg1, gc1, gbd, gg2, gc2, gbup, gbproj, gbq, gbk, gbv = vecs
    return (
        layer_out, input_grad, gq, gbq, gk, gbk, gv, gbv, gout, gbo, gg1, gc1, gup, gbup, gdown.T, gbd, gg2, gc2,
        gproj, gbproj,
    )


def solution(mesh):
    batch, seq = mesh.shape["batch"], mesh.shape["seq"]
    split = P("batch", ("z", "p"), None)
    in_specs = (split,) * 3 + (P("batch", None),) * 2 + (P(),) * 24 + (P(("z", "p"), None),)
    out_specs = (split,) * 2 + (P(),) * 18

    def run(*args):
        planes = args[0].shape[0] // batch
        fine = Mesh(mesh.devices.reshape(batch, planes, seq // planes), ("batch", "z", "p"))
        return jax.shard_map(body, mesh=fine, in_specs=in_specs, out_specs=out_specs, check_vma=False)(*args)

    return run
```

```python
import functools
import math

import jax
import jax.numpy as jnp
from jax import lax
from jax.experimental import pallas as pl
from jax.experimental.pallas import tpu as pltpu
from jax.sharding import Mesh
from jax.sharding import PartitionSpec as P

HEADS = 12
EPSILON = 1e-06
HID_WEIGHT = 0.05
CE_WEIGHT = 4.0
MIXING = 0.5
ROOT_HALF = 0.7071067811865476
ROOT_TWO_PI = 2.5066282746310002
LANES = 128
BF = jnp.bfloat16
F32 = jnp.float32
MIB = 1 << 20


def mm(left, right):
    return lax.dot_general(left, right, (((1,), (0,)), ((), ())), preferred_element_type=F32)


def mm_nt(left, right):
    return lax.dot_general(left, right, (((1,), (1,)), ((), ())), preferred_element_type=F32)


def mm_tn(left, right):
    return lax.dot_general(left, right, (((0,), (0,)), ((), ())), preferred_element_type=F32)


def normalize(values):
    centered = values - jnp.mean(values, axis=-1, keepdims=True)
    inverse = lax.rsqrt(jnp.mean(centered * centered, axis=-1, keepdims=True) + EPSILON)
    return centered * inverse, inverse


def norm_back(grads, scaled, inverse):
    return inverse * (
        grads
        - jnp.mean(grads, axis=-1, keepdims=True)
        - scaled * jnp.mean(grads * scaled, axis=-1, keepdims=True)
    )


def gelu(inputs):
    return inputs * (0.5 * (1.0 + lax.erf(inputs * ROOT_HALF)))


def gelu_slope(inputs):
    cumulative = 0.5 * (1.0 + lax.erf(inputs * ROOT_HALF))
    density = jnp.exp(-0.5 * inputs * inputs) * (1.0 / ROOT_TWO_PI)
    return cumulative + inputs * density


def column_sum(values):
    return jnp.sum(values.astype(F32), axis=0, keepdims=True)


def attend(at, q_ref, k_ref, v_ref, per_group, size, emit):
    rows = at.size if isinstance(at, pl.Slice) else at.stop - at.start
    heads = q_ref.shape[1] // LANES * per_group
    lane = lax.broadcasted_iota(jnp.int32, (rows, LANES), 1)
    scaling = math.log2(math.e) / math.sqrt(size)

    def scores_of(head):
        cols = slice(head // per_group * LANES, (head // per_group + 1) * LANES)
        low = head % per_group * size
        mask = (lane >= low) & (lane < low + size)
        query = jnp.where(mask, q_ref[at, cols].astype(F32), 0.0).astype(BF)
        return cols, mask, mm_nt(query, k_ref[:, cols])

    later = scores_of(0)
    for head in range(heads):
        cols, mask, scores = later
        later = scores_of(head + 1) if head + 1 < heads else None
        top = jnp.max(scores, axis=-1, keepdims=True) * scaling
        weights = jnp.exp2(scores * scaling - top)
        total = jnp.sum(weights, axis=-1, keepdims=True)
        mixed = mm(weights.astype(BF), v_ref[:, cols])
        emit(head, cols, mask, mixed * (1.0 / total), top + jnp.log2(total))


def over_rows(own, length, one):
    if length <= 2048:
        one(slice(0, own))
    else:
        step = 64

        def inside(turn, carry):
            one(pl.ds(pl.multiple_of(turn * step, step), step))
            return carry

        lax.fori_loop(0, own // step, inside, 0)


def call(kernel, outs, scratch=(), limit=16, name=None, cost=1, far=(), wait=()):
    spaces = {"vmem": pltpu.VMEM, "smem": pltpu.SMEM, "any": pl.ANY}

    def space(at, arg):
        small = arg.ndim == 1 and arg.dtype == jnp.int32
        return pl.BlockSpec(memory_space=spaces["any" if at in far else "smem" if small else "vmem"])

    def run(*args):
        count = len(args)

        def body_of(*refs):
            kernel(*refs[:count], *refs[count + len(wait):])

        return pl.pallas_call(
            body_of,
            out_shape=outs,
            in_specs=[space(at, arg) for at, arg in enumerate(args)] + [pl.BlockSpec(memory_space=pl.ANY)] * len(wait),
            out_specs=[pl.BlockSpec(memory_space=pltpu.VMEM)] * len(outs),
            scratch_shapes=list(scratch),
            compiler_params=pltpu.CompilerParams(vmem_limit_bytes=limit * MIB),
            cost_estimate=pl.CostEstimate(
                flops=int(cost * 1e9), bytes_accessed=int(cost * 3e6), transcendentals=0
            ),
            name=name,
        )(*args, *wait)

    return run


def sds(shape, dtype):
    return jax.ShapeDtypeStruct(shape, dtype)


def lines_of(ref, first, width):
    count = -(-width // LANES)
    return jnp.concatenate([ref[at:at + 1, :] for at in range(first, first + count)], axis=1)[:, :width]


def pack_kernel(many, me_ref, *refs):
    ins, outs = refs[:many], refs[many:]
    for key, out in enumerate(outs):
        at = 0
        for ref in ins:
            width = ref.shape[2]
            out[:, at:at + width] = ref[jnp.bitwise_xor(me_ref[0], key)]
            at += width


def split_kernel(many, *refs):
    ins, outs = refs[:-many], refs[-many:]
    rows = ins[0].shape[0]
    for turn, ref in enumerate(ins):
        at = 0
        for out in outs:
            width = out.shape[1]
            out[turn * rows:(turn + 1) * rows, :] = ref[:, at:at + width]
            at += width


def flip_kernel(table_ref, flip_ref):
    flip_ref[...] = table_ref[...].T


def prepare_kernel(order, cap, per_device, peers, vocab_rows, at_vec, me_ref, *refs):
    many_in = 6 + len(at_vec) - 1
    sources, outs, copied = refs[:many_in], refs[many_in:many_in + 7], refs[many_in + 7:-1]
    vec_ref, live_ref, want_ref, line_ref, wqkv_ref, bqkv_ref, wo_ref = outs
    copies = [pltpu.make_async_copy(*pair, refs[-1].at[at]) for at, pair in enumerate(zip(sources, copied))]
    for copy in copies:
        copy.start()
    for copy in copies:
        copy.wait()
    pos_ref, ids_ref, wq_ref, wk_ref, wv_ref, wout_ref, *vec_refs = copied
    vec_ref[...] = jnp.zeros_like(vec_ref)
    rows_of = [ref[...].astype(F32).reshape(1, ref.shape[0]) for ref in vec_refs]
    for first, value in zip(at_vec, rows_of):
        for at in range(0, value.shape[1], LANES):
            part = value[:, at:at + LANES]
            vec_ref[first + at // LANES:first + at // LANES + 1, :part.shape[1]] = part
    width = wq_ref.shape[0]
    pad = wo_ref.shape[0]
    valid = width * LANES // pad
    row = lax.broadcasted_iota(jnp.int32, (width, pad), 0)
    col = lax.broadcasted_iota(jnp.int32, (width, pad), 1)
    inside = lax.rem(col, LANES)
    select = jnp.where((inside < valid) & (row == lax.div(col, LANES) * valid + inside), 1.0, 0.0).astype(BF)
    for at, ref in enumerate((wq_ref, wk_ref, wv_ref)):
        wqkv_ref[:, at * pad:(at + 1) * pad] = mm(ref[...], select).astype(BF)
        bias = jnp.broadcast_to(rows_of[8 + at], (8, width)).astype(BF)
        bqkv_ref[:, at * pad:(at + 1) * pad] = mm(bias, select)[:1]
    wo_ref[...] = mm_tn(select, wout_ref[...]).astype(BF)

    planes, many = pos_ref.shape
    z_at, p_at = me_ref[0], me_ref[1]
    first = (z_at * peers + p_at) * vocab_rows
    lane = lax.broadcasted_iota(jnp.int32, (8, LANES), 1)

    def lines(ref, seq, peer):
        whole = jnp.broadcast_to(ref[pl.ds(seq, 1), :], (8, many))
        out = jnp.full((8, LANES), -1, jnp.int32)
        for plane in range(planes):
            shift = lax.rem(plane * cap - (plane * peers + peer) * cap + 2 * many, many)
            moved = pltpu.roll(whole, shift, 1)[:, :LANES]
            out = jnp.where((lane >= plane * cap) & (lane < (plane + 1) * cap), moved, out)
        return out

    own = lines(pos_ref, z_at, p_at)
    local = own
    for plane in range(planes):
        move = jnp.bitwise_xor(z_at, plane) * per_device - (plane * peers + p_at) * per_device
        local = jnp.where((lane >= plane * cap) & (lane < (plane + 1) * cap), own + move, local)
    line_ref[...] = jnp.where(own >= 0, local, -1)[:1]

    def one(turn, carry):
        key = jnp.int32(0)
        for bit, value in enumerate(order):
            key = jnp.where(lax.rem(lax.div(turn, 1 << bit), 2) == 1, jnp.bitwise_xor(key, value), key)
        for plane in range(planes):
            seq, peer = jnp.bitwise_xor(z_at, plane), jnp.bitwise_xor(p_at, key)
            live_ref[turn * planes + plane] = jnp.where(lines(pos_ref, seq, peer) >= 0, 1.0, 0.0)[:1]
            want_ref[turn * planes + plane] = (lines(ids_ref, seq, peer) - first)[:1]
        return carry

    lax.fori_loop(0, peers, one, 0)


def place_kernel(me_ref, *refs):
    *ins, out_ref = refs
    for key, ref in enumerate(ins):
        out_ref[jnp.bitwise_xor(me_ref[0], key)] = ref[...].astype(out_ref.dtype)


def pick(line_ref, slots, values):
    own = values.shape[0]
    at = lax.broadcasted_iota(jnp.int32, (own, LANES), 0)
    chosen = jnp.where(at == line_ref[...], 1.0, 0.0).astype(BF)
    return mm_tn(chosen, values)[:slots]


def teacher_attend_kernel(tq_ref, tk_ref, tv_ref, *refs):
    *row_refs, att_ref, q_ref, k_ref, mark_ref, v_scr = refs
    mark_ref[...] = jnp.zeros_like(mark_ref)
    own = q_ref.shape[0]
    width = tq_ref.shape[1]
    size = width // HEADS
    per_group = LANES // size
    wide = v_scr.shape[1]
    q_ref[...] = mm(row_refs[0][:own], tq_ref[...]).astype(BF)
    for part in range(width // wide):
        cols = slice(part * wide, (part + 1) * wide)
        at = 0
        for row_ref in row_refs:
            there = slice(at, at + row_ref.shape[0])
            k_ref[there, cols] = mm(row_ref[...], tk_ref[:, cols]).astype(BF)
            v_scr[there, :] = mm(row_ref[...], tv_ref[:, cols]).astype(BF)
            at += row_ref.shape[0]
        out_ref = att_ref.at[:, cols]

        def one(at):
            def emit(head, there, mask, mixed, lse):
                out_ref[at, there] = mixed if head % per_group == 0 else jnp.where(mask, mixed, out_ref[at, there])

            attend(at, q_ref.at[:, cols], k_ref.at[:, cols], v_scr, per_group, size, emit)

        over_rows(own, v_scr.shape[0], one)


def teacher_feed_kernel(line_ref, rows_ref, att_ref, to_ref, up_ref, down_ref, out_ref, pick_ref):
    own, width = att_ref.shape
    branch = mm(att_ref[...].astype(BF), to_ref[...])
    hidden, _ = normalize(rows_ref[:own].astype(F32) + branch)
    low = hidden.astype(BF)
    step = width
    outer = jnp.zeros((own, width), F32)
    for at in range(0, up_ref.shape[1], step):
        inner = gelu(mm(low, up_ref[:, at:at + step])).astype(BF)
        outer = outer + mm(inner, down_ref[at:at + step])
    output, _ = normalize(hidden + outer)
    out_ref[...] = output
    pick_ref[...] = pick(line_ref, pick_ref.shape[0], output.astype(BF)).astype(BF)


def student_kernel(
    at_vec, line_ref, vec_ref, wqkv_ref, bqkv_ref, wo_ref, up_ref, down_ref, *refs,
):
    *row_refs, q_ref, kv_ref, keep_ref, out_ref, pick_ref = refs
    own, pad = q_ref.shape
    length = kv_ref.shape[0]
    width = wo_ref.shape[1]
    ff = up_ref.shape[1]
    size = width // HEADS
    per_group = HEADS * LANES // pad
    rows = row_refs[0][:own]
    q_ref[...] = (mm(rows, wqkv_ref[:, :pad]) + bqkv_ref[:, :pad]).astype(BF)
    at = 0
    for row_ref in row_refs:
        there = slice(at, at + row_ref.shape[0])
        kv_ref[there, :] = (mm(row_ref[...], wqkv_ref[:, pad:]) + bqkv_ref[:, pad:]).astype(BF)
        at += row_ref.shape[0]
    k_ref, v_ref = kv_ref.at[:, :pad], kv_ref.at[:, pad:]
    keep_ref[:, pad:] = jnp.zeros((own, keep_ref.shape[1] - pad), F32)
    stat = slice(3 * pad, 3 * pad + LANES)

    def one(at):
        def emit(head, there, mask, mixed, lse):
            old = 0.0 if head % per_group == 0 else keep_ref[at, there]
            keep_ref[at, there] = jnp.where(mask, mixed, old)
            lane = lax.broadcasted_iota(jnp.int32, (lse.shape[0], LANES), 1)
            keep_ref[at, stat] = jnp.where(lane == head, lse, keep_ref[at, stat])

        attend(at, q_ref, k_ref, v_ref, per_group, size, emit)

    over_rows(own, length, one)
    bo, g1, c1, bdown, g2, c2 = (lines_of(vec_ref, at, width) for at in at_vec[:6])
    branch = mm(keep_ref[:, :pad].astype(BF), wo_ref[...]) + bo
    n1, i1 = normalize(rows.astype(F32) + branch)
    hidden = n1 * g1 + c1
    inner = mm(hidden.astype(BF), up_ref[...]) + lines_of(vec_ref, at_vec[6], ff)
    outer = mm_nt(gelu(inner).astype(BF), down_ref[...]) + bdown
    n2, i2 = normalize(hidden + outer)
    output = (n2 * g2 + c2).astype(BF)
    keep_ref[:, pad:pad + width] = n1
    keep_ref[:, 2 * pad:2 * pad + width] = n2
    at = lax.broadcasted_iota(jnp.int32, (own, LANES), 1)
    keep_ref[:, stat] = jnp.where(at == HEADS, i1, jnp.where(at == HEADS + 1, i2, keep_ref[:, stat]))
    out_ref[...] = output
    pick_ref[...] = pick(line_ref, pick_ref.shape[0], output).astype(BF)


def logits_kernel(at_bias, slots, many, *refs):
    pieces, flip_ref, refs = refs[:many], refs[many], refs[many + 1:]
    if at_bias is not None:
        (proj_ref, vec_ref), refs = refs[:2], refs[2:]
        bias = lines_of(vec_ref, at_bias, proj_ref.shape[1])
    rows = pieces[0].shape[0]
    block = 2 * slots
    lane = lax.broadcasted_iota(jnp.int32, (block, LANES), 1)

    def logits_of(piece, at):
        picked = pieces[piece][at, :]
        if at_bias is not None:
            picked = (mm(picked, proj_ref[...]) + bias).astype(BF)
        return mm(picked, flip_ref[...])

    def finish(logits, piece, at, first):
        raised_ref, top_ref, lse_ref = refs[3 * piece:3 * piece + 3]
        top = jnp.max(logits, axis=-1, keepdims=True)
        weights = jnp.exp(logits - top)
        total = top + jnp.log(jnp.sum(weights, axis=-1, keepdims=True))
        raised_ref[at, :] = weights.astype(BF)
        both = jnp.where(lane == 0, top, jnp.where(lane == 1, total, 0.0))
        for part in range(2):
            value = both[part * slots:(part + 1) * slots]
            if slots < LANES:
                value = jnp.concatenate([value, jnp.zeros((LANES - slots, LANES), F32)], axis=0)
            value = value.T
            top_ref[first + part] = value[0:1]
            lse_ref[first + part] = value[1:2]

    if rows // block <= 2:
        work = [(piece, at) for piece in range(many) for at in range(0, rows, block)]
        later = logits_of(work[0][0], slice(work[0][1], work[0][1] + block))
        for turn, (piece, at) in enumerate(work):
            logits = later
            if turn + 1 < len(work):
                after_piece, after_at = work[turn + 1]
                later = logits_of(after_piece, slice(after_at, after_at + block))
            finish(logits, piece, slice(at, at + block), at // slots)
    else:
        for piece in range(many):

            def one(turn, carry, piece=piece):
                at = pl.ds(pl.multiple_of(turn * block, block), block)
                finish(logits_of(piece, at), piece, at, 2 * turn)
                return carry

            lax.fori_loop(0, rows // block, one, 0)


def combine_kernel(first, slots, chained, *refs):
    if chained:
        gproj_in, gbproj_in, *refs = refs
    (
        live_ref, want_ref, s_top_ref, t_top_ref, all_ref, s_ref, t_ref, rows_ref, table_ref, proj_ref,
        back_ref, gproj_ref, gbproj_ref, low_scr,
    ) = refs
    blocks = s_top_ref.shape[0]
    sources = all_ref.shape[0]
    line = lax.broadcasted_iota(jnp.int32, (LANES, LANES), 0)
    column = lax.broadcasted_iota(jnp.int32, (slots, table_ref.shape[0]), 1)
    gbproj_ref[...] = gbproj_in[...] if chained else jnp.zeros_like(gbproj_ref)

    def share(block, which, top):
        known = [all_ref[key, jnp.bitwise_xor(block, key), which:which + 1, :] for key in range(sources)]
        peak = functools.reduce(jnp.maximum, known)
        total = functools.reduce(jnp.add, [jnp.exp(value - peak) for value in known])
        return jnp.exp(top - peak) / total

    def logit_grads(step):
        block = step + first
        at = pl.ds(pl.multiple_of(step * slots, slots), slots)
        live = CE_WEIGHT * live_ref[block]
        s_part = live * share(block, 0, s_top_ref[step])
        t_part = live * (MIXING * share(block, 1, t_top_ref[step]))
        lines = jnp.where(line == 0, s_part, jnp.where(line == 1, t_part, live * (1.0 - MIXING)))
        lines = jnp.where(line == 3, want_ref[block].astype(F32), lines)
        cols = lines.T[:slots]
        hot = jnp.where(column == cols[:, 3:4].astype(jnp.int32), cols[:, 2:3], 0.0)
        grads = cols[:, 0:1] * s_ref[at, :].astype(F32) - cols[:, 1:2] * t_ref[at, :].astype(F32) - hot
        return grads.astype(BF)

    def one(turn, carry):
        for half in range(2):
            step = 2 * turn + half
            at = pl.ds(pl.multiple_of(step * slots, slots), slots)
            low_scr[at, :] = logit_grads(step)
        at = pl.ds(pl.multiple_of(2 * turn * slots, 2 * slots), 2 * slots)
        picked = mm(low_scr[at, :], table_ref[...])
        gbproj_ref[...] += column_sum(picked)
        picked = picked.astype(BF)
        back_ref[at, :] = mm_nt(picked, proj_ref[...]).astype(BF)
        gproj = mm_tn(rows_ref[at, :], picked)
        gproj_ref[...] += gproj
        return carry

    gproj_ref[...] = gproj_in[...] if chained else jnp.zeros_like(gproj_ref)
    if blocks <= 4:
        for turn in range(blocks // 2):
            one(turn, 0)
    else:
        lax.fori_loop(0, blocks // 2, one, 0)


def place(me_ref):
    peer = me_ref[1]
    return me_ref[2] * 2 + lax.rem(lax.div(peer, 2), 2), me_ref[0], lax.rem(peer, 2)


def scatter_blocks(stage_ref, me, keep_ref, send_ref):
    xy_at, z_at, c_at = me
    planes = keep_ref.shape[1]
    rows, wide = keep_ref.shape[2:]
    half = planes * wide
    for xy in range(4):
        for plane in range(planes):
            at, lanes = xy * rows, plane * wide
            key = (jnp.bitwise_xor(xy, xy_at), jnp.bitwise_xor(plane, z_at))
            low = stage_ref[at:at + rows, lanes:lanes + wide]
            high = stage_ref[at:at + rows, half + lanes:half + lanes + wide]
            keep_ref[key] = jnp.where(c_at == 0, low, high).astype(BF)
            send_ref[key] = jnp.where(c_at == 0, high, low).astype(BF)


def feed_again_kernel(at_vec, vec_ref, proj_ref, up_ref, og_ref, tout_ref, out_ref, keep_ref, *refs):
    hid_ref, act_ref, slope_ref, dout_ref, gproj_ref, gbproj_ref, *block_refs = refs
    own, width = og_ref.shape
    for at, ref in enumerate(block_refs):
        ref[...] = out_ref[at * ref.shape[0]:(at + 1) * ref.shape[0], :]
    pad = (keep_ref.shape[1] - LANES) // 3
    g1, c1 = (lines_of(vec_ref, at_vec[at], width) for at in (1, 2))
    hidden = (keep_ref[:, pad:pad + width] * g1 + c1).astype(BF)
    inner = mm(hidden, up_ref[...]) + lines_of(vec_ref, at_vec[6], up_ref.shape[1])
    cumulative = 0.5 * (1.0 + lax.erf(inner * ROOT_HALF))
    hid_ref[...] = hidden
    act_ref[...] = (inner * cumulative).astype(BF)
    slope_ref[...] = cumulative + inner * (jnp.exp(-0.5 * inner * inner) * (1.0 / ROOT_TWO_PI))
    output = out_ref[...]
    mapped = mm(output, proj_ref[...]) + lines_of(vec_ref, at_vec[7], proj_ref.shape[1])
    d_map = (2.0 * HID_WEIGHT * (mapped - tout_ref[...])).astype(BF)
    gproj_ref[...] = mm_tn(output, d_map)
    gbproj_ref[...] = column_sum(d_map)
    dout_ref[...] = og_ref[...].astype(F32) + mm_nt(d_map, proj_ref[...])


def feed_back_kernel(
    layout, at_vec, me_ref, line_ref, vec_ref, gproj_ref, gbproj_ref, hid_ref, act_ref, slope_ref, dout_ref,
    gproj_add, gbproj_add, down_ref, up_ref, wo_ref, keep_ref, *refs,
):
    *ce_refs, datt_ref, dres_ref, mine_ref, send_ref, stage_ref = refs
    own, width = dout_ref.shape
    pad = wo_ref.shape[0]
    at_up, at_down, at_proj, at_out = layout
    t_width = gproj_ref.shape[1]
    ff = up_ref.shape[1]
    at = lax.broadcasted_iota(jnp.int32, (own, LANES), 0)
    slots = ce_refs[0].shape[0]
    chosen = jnp.where(at == line_ref[...], 1.0, 0.0).astype(BF)[:, :slots]
    ce = functools.reduce(jnp.add, [ref[...].astype(F32) for ref in ce_refs])
    high = ce.astype(BF)
    rest = (ce - high.astype(F32)).astype(BF)
    d_out = dout_ref[...] + mm(chosen, high) + mm(chosen, rest)
    g1, g2 = (lines_of(vec_ref, at_vec[at], width) for at in (1, 4))
    n1, n2 = keep_ref[:, pad:pad + width], keep_ref[:, 2 * pad:2 * pad + width]
    stat = 3 * pad + HEADS
    i1, i2 = keep_ref[:, stat:stat + 1], keep_ref[:, stat + 1:stat + 2]
    stage_ref[width:, :] = jnp.zeros((stage_ref.shape[0] - width, stage_ref.shape[1]), F32)
    stage_ref[:width, at_proj:at_proj + t_width] = gproj_ref[...] + gproj_add[...]
    stage_ref[width:width + 1, at_proj:at_proj + t_width] = gbproj_ref[...] + gbproj_add[...]
    d_res2 = norm_back(d_out * g2, n2, i2)
    d_outer = d_res2.astype(BF)
    stage_ref[:width, at_down:at_down + ff] = mm_tn(d_outer, act_ref[...])
    d_inner = (mm(d_outer, down_ref[...]) * slope_ref[...]).astype(BF)
    stage_ref[:width, at_up:at_up + ff] = mm_tn(hid_ref[...], d_inner)
    stage_ref[width:width + 1, at_up:at_up + ff] = column_sum(d_inner)
    d_hid = d_res2 + mm_nt(d_inner, up_ref[...])
    d_res1 = norm_back(d_hid * g1, n1, i1)
    d_branch = d_res1.astype(BF)
    datt_ref[...] = mm_nt(d_branch, wo_ref[...]).astype(BF)
    dres_ref[...] = d_res1
    gout = mm_tn(keep_ref[:, :pad].astype(BF), d_branch)
    head_groups = pad // LANES
    valid = width // head_groups
    for group in range(head_groups):
        stage_ref[group * valid:(group + 1) * valid, at_out:at_out + width] = gout[group * LANES:group * LANES + valid]
    lines = [
        column_sum(d_branch),
        column_sum(d_hid * n1),
        column_sum(d_hid),
        column_sum(d_outer),
        column_sum(d_out * n2),
        column_sum(d_out),
    ]
    for at, value in enumerate(lines):
        stage_ref[width + at:width + at + 1, at_out:at_out + width] = value
    scatter_blocks(stage_ref, place(me_ref), mine_ref, send_ref)


def attend_back_kernel(
    weight_mse, size, group, datt_ref, keep_ref, q_ref, kv_ref, tq_ref, tk_ref,
    dq_ref, dk_ref, dv_ref, sums_ref, dq_scr,
):
    own, pad = q_ref.shape
    per_group = HEADS * LANES // pad
    t_size = tq_ref.shape[1] // HEADS
    t_group = LANES // t_size
    length = kv_ref.shape[0]
    chunk = length if length <= 2048 else 256
    cols = slice(group * LANES, (group + 1) * LANES)
    v_cols = slice(pad + group * LANES, pad + (group + 1) * LANES)
    s_scaling = 1.0 / math.sqrt(size)
    t_scaling = 1.0 / math.sqrt(t_size)
    lane = lax.broadcasted_iota(jnp.int32, (own, LANES), 1)
    query_all = q_ref[:, cols].astype(F32)
    grad_all = datt_ref[:, cols].astype(F32)
    product = grad_all * keep_ref[:, cols]
    lses = keep_ref[:, 3 * pad:].T
    dots = jnp.zeros((own, LANES), F32)
    heads = []
    for turn in range(per_group):
        head = group * per_group + turn
        mask = (lane >= turn * size) & (lane < (turn + 1) * size)
        dots = jnp.where(lane == turn, jnp.sum(jnp.where(mask, product, 0.0), axis=-1, keepdims=True), dots)
        t_cols = slice(head // t_group * LANES, (head // t_group + 1) * LANES)
        t_low = head % t_group * t_size
        t_mask = (lane >= t_low) & (lane < t_low + t_size)
        heads.append((
            mask,
            jnp.where(mask, query_all, 0.0).astype(BF),
            jnp.where(mask, grad_all, 0.0).astype(BF),
            t_cols,
            jnp.where(t_mask, tq_ref[:, t_cols].astype(F32), 0.0).astype(BF),
            lses[head:head + 1],
        ))
    dots = dots.T
    dq_scr[...] = jnp.zeros_like(dq_scr)
    sums_ref[...] = jnp.zeros_like(sums_ref)

    def one_chunk(at):
        keys, values = kv_ref[at, cols], kv_ref[at, v_cols]
        d_keys, d_values = jnp.zeros(keys.shape, F32), jnp.zeros(keys.shape, F32)

        def products(turn):
            _, query, grad, t_cols, t_query, _ = heads[turn]
            return mm_nt(keys, query), mm_nt(tk_ref[at, t_cols], t_query), mm_nt(values, grad)

        later = products(0)
        for turn, (mask, query, grad, _, _, lse) in enumerate(heads):
            scores, teacher, d_probs = later
            later = products(turn + 1) if turn + 1 < per_group else None
            probs = jnp.exp2(scores * (s_scaling * math.log2(math.e)) - lse)
            d_scores = (
                probs * (d_probs - dots[turn:turn + 1])
                + (scores * (weight_mse * s_scaling) - teacher * (weight_mse * t_scaling))
            ).astype(BF)
            d_keys += mm(d_scores, query)
            d_values += mm(probs.astype(BF), grad)
            dq_scr[...] += jnp.where(mask, mm_tn(d_scores, keys), 0.0)
        d_keys = d_keys * s_scaling
        sums_ref[1:2, :] += column_sum(d_keys)
        sums_ref[2:3, :] += column_sum(d_values)
        dk_ref[at, :] = d_keys.astype(BF)
        dv_ref[at, :] = d_values.astype(BF)

    if chunk == length:
        one_chunk(slice(0, length))
    else:

        def inside(turn, carry):
            one_chunk(pl.ds(pl.multiple_of(turn * chunk, chunk), chunk))
            return carry

        lax.fori_loop(0, length // chunk, inside, 0)
    d_queries = dq_scr[...] * s_scaling
    sums_ref[0:1, :] = column_sum(d_queries)
    dq_ref[...] = d_queries.astype(BF)


def attend_weights_kernel(groups, me_ref, *refs):
    dq_refs, dk_refs, dv_refs, sum_refs = (refs[at * groups:(at + 1) * groups] for at in range(4))
    *row_refs, mine_ref, send_ref, g_scr, stage_ref = refs[4 * groups:]
    own = dq_refs[0].shape[0]
    width = row_refs[0].shape[1]
    pad = groups * LANES
    piece = row_refs[0].shape[0]
    g_scr[width:, :] = jnp.zeros((g_scr.shape[0] - width, g_scr.shape[1]), F32)
    for group in range(groups):
        cols = slice(group * LANES, (group + 1) * LANES)
        g_scr[:width, cols] = mm_tn(row_refs[0][:own], dq_refs[group][...])
        for which, refs_of in ((1, dk_refs), (2, dv_refs)):
            there = slice(which * pad + group * LANES, which * pad + (group + 1) * LANES)
            parts = [
                mm_tn(row_ref[...], refs_of[group][at * piece:(at + 1) * piece, :]) for at, row_ref in enumerate(row_refs)
            ]
            g_scr[:width, there] = functools.reduce(jnp.add, parts)
        for which in range(3):
            there = slice(which * pad + group * LANES, which * pad + (group + 1) * LANES)
            g_scr[width:width + 1, there] = sum_refs[group][which:which + 1, :]
    valid = width // groups
    parts = [g_scr[:, at * LANES:at * LANES + valid] for at in range(3 * groups)]
    stage_ref[...] = jnp.zeros_like(stage_ref)
    stage_ref[:, :3 * width] = jnp.concatenate(parts, axis=1)
    scatter_blocks(stage_ref, place(me_ref), mine_ref, send_ref)


def attend_rows_kernel(groups, wqkv_ref, dres_ref, *refs):
    dq_refs, dk_refs, dv_refs = (refs[at * groups:(at + 1) * groups] for at in range(3))
    far_ref, near_ref, own_ref = refs[3 * groups:]
    width = dres_ref.shape[1]
    pad = groups * LANES
    half = far_ref.shape[0]
    total = dres_ref[...]
    for group in range(groups):
        total = total + mm_nt(dq_refs[group][...], wqkv_ref[:, group * LANES:(group + 1) * LANES])
    own_ref[...] = total
    step = min(half, 512)
    for at in range(0, 2 * half, step):
        there = slice(at, at + step)
        back = jnp.zeros((step, width), F32)
        for group in range(groups):
            k_cols = slice(pad + group * LANES, pad + (group + 1) * LANES)
            v_cols = slice(2 * pad + group * LANES, 2 * pad + (group + 1) * LANES)
            back += mm_nt(dk_refs[group][there, :], wqkv_ref[:, k_cols])
            back += mm_nt(dv_refs[group][there, :], wqkv_ref[:, v_cols])
        out_ref, start = (near_ref, at) if at < half else (far_ref, at - half)
        out_ref[start:start + step, :] = back.astype(BF)


def stack_kernel(many, *refs):
    ins, (out,) = refs[:many], refs[many:]
    at = 0
    for turn, ref in enumerate(ins):
        if out.ndim > ref.ndim:
            out[turn] = ref[...]
        else:
            out[at:at + ref.shape[0]] = ref[...]
            at += ref.shape[0]


def copy_kernel(*refs):
    half = len(refs) // 2
    for source, target in zip(refs[:half], refs[half:]):
        target[...] = source[...]


def add_kernel(many, *refs):
    ins, outs = refs[:many], refs[many:]
    for at, out in enumerate(outs):
        if out.ndim == ins[0].ndim:
            size = out.shape[0]
            parts = [ref[at * size:(at + 1) * size] for ref in ins]
        else:
            parts = [ref[at] for ref in ins]
        out[...] = functools.reduce(jnp.add, [part.astype(F32) for part in parts]).astype(out.dtype)


def side_kernel(many, *refs):
    thin, rest = refs[:many], refs[many:]
    places = len(rest) // 2
    value = functools.reduce(jnp.add, [part[...].astype(F32) for part in thin]).astype(BF)
    planes, rows, lanes = value.shape
    for ref, out in zip(rest[:places], rest[places:]):
        for plane in range(planes):
            out[plane * rows:(plane + 1) * rows, :] = value[plane]
        height, width = ref.shape
        for turn, lane in enumerate(range(0, width, lanes)):
            at = slice(planes * rows + turn * height, planes * rows + (turn + 1) * height)
            part = ref[:, lane:lane + lanes]
            if part.shape[1] < lanes:
                out[at, :] = jnp.zeros((height, lanes), BF)
            out[at, :part.shape[1]] = part


def tail_kernel(planes, me_ref, *refs):
    ins, (sum_ref, place_ref) = refs[:planes], refs[planes:]
    _, rows, lanes = sum_ref.shape
    height, width = place_ref.shape[1:]
    for place in range(planes):
        parts = [ref[(place ^ key) * rows:((place ^ key) + 1) * rows, :].astype(F32) for key, ref in enumerate(ins)]
        sum_ref[place] = functools.reduce(jnp.add, parts).astype(BF)
    for key, ref in enumerate(ins):
        for turn, lane in enumerate(range(0, width, lanes)):
            at = planes * rows + turn * height
            many = min(lanes, width - lane)
            place_ref[jnp.bitwise_xor(me_ref[0], key), :, lane:lane + many] = ref[at:at + height, :many].astype(F32)


def collect(stage_ref, planes, me_ref, blocks):
    xy_at, z_at, c_at = place(me_ref)
    rows = stage_ref.shape[0] // 4
    each = stage_ref.shape[1] // (2 * planes)
    for core, ref in enumerate(blocks):
        for xy in range(4):
            for plane in range(planes):
                at = pl.ds(pl.multiple_of(jnp.bitwise_xor(xy, xy_at) * rows, 16), rows)
                lanes = jnp.bitwise_xor(core, c_at) * planes + jnp.bitwise_xor(plane, z_at)
                stage_ref[at, pl.ds(pl.multiple_of(lanes * each, LANES), each)] = ref[xy, plane].astype(F32)


def unpack_wide_kernel(layout, ff, width, t_width, planes, me_ref, *refs):
    blocks, (gout, gup, gdown, gproj, *vec_refs, mark_ref, wide_ref) = refs[:2], refs[2:]
    mark_ref[...] = jnp.zeros_like(mark_ref)
    at_up, at_down, at_proj, at_out = layout
    collect(wide_ref, planes, me_ref, blocks)
    gup[...] = wide_ref[:width, at_up:at_up + ff]
    gdown[...] = wide_ref[:width, at_down:at_down + ff]
    gproj[...] = wide_ref[:width, at_proj:at_proj + t_width]
    gout[...] = wide_ref[:width, at_out:at_out + width]
    for at in range(6):
        vec_refs[at][...] = wide_ref[width + at:width + at + 1, at_out:at_out + width].reshape(width)
    vec_refs[6][...] = wide_ref[width:width + 1, at_up:at_up + ff].reshape(ff)
    vec_refs[7][...] = wide_ref[width:width + 1, at_proj:at_proj + t_width].reshape(t_width)


def unpack_thin_kernel(planes, me_ref, *refs):
    blocks, outs, thin_ref = refs[:2], refs[2:8], refs[8]
    width = outs[0].shape[0]
    collect(thin_ref, planes, me_ref, blocks)
    for at in range(3):
        lanes = slice(at * width, (at + 1) * width)
        outs[at][...] = thin_ref[:width, lanes]
        outs[3 + at][...] = thin_ref[width:width + 1, lanes].reshape(width)


def swap(value, axis, key):
    if isinstance(axis, tuple):
        size = math.prod(lax.axis_size(name) for name in axis)
    else:
        size = lax.axis_size(axis)
    return lax.ppermute(value, axis, [(at, at ^ key) for at in range(size)])


def swap_xy(value, key):
    return swap(value, ("batch", "p"), (key // 2) * lax.axis_size("p") + (key % 2) * 2)


def bits_of(size):
    return [1 << at for at in range(size.bit_length() - 1)]


def passed(value):
    return swap(value, "p", 1)


def stacked(parts, wait=(), joined=True, cost=0.1):
    rows = sum(part.shape[0] for part in parts)
    shape = (rows,) + parts[0].shape[1:] if joined else (len(parts),) + parts[0].shape
    return call(
        functools.partial(stack_kernel, len(parts)), [sds(shape, parts[0].dtype)], name="stack", cost=cost, wait=wait
    )(*parts)[0]


def spread_over_z(parts):
    return [parts[0]] + [swap(parts[key], "z", key) for key in range(1, len(parts))]


def plane_pieces(value):
    bits = list(reversed(bits_of(lax.axis_size("p"))))
    for bit in bits[:-2]:
        value = jnp.concatenate([value, swap(value, "p", bit)], axis=0)
    pieces = [value]
    for bit in bits[-2:]:
        pieces = pieces + [swap(piece, "p", bit) for piece in pieces]
    return pieces


def plane_both(value, across):
    bits = list(reversed(bits_of(lax.axis_size("p"))))
    pieces = [value, across]
    for bit in bits[1:]:
        pieces = pieces + [swap(piece, "p", bit) for piece in pieces]
    many = len(pieces) // 4
    return [jnp.concatenate(pieces[at * many:(at + 1) * many], axis=0) if many > 1 else pieces[at] for at in range(4)]


def gather_z(value, *done):
    return stacked([value] + [swap(value, "z", key) for key in range(1, lax.axis_size("z"))], wait=done)


def gather_plane(value):
    for bit in reversed(bits_of(lax.axis_size("p"))):
        value = jnp.concatenate([value, swap(value, "p", bit)], axis=0)
    return value


def copied(values, wait):
    return call(copy_kernel, [sds(value.shape, value.dtype) for value in values], name="copy", cost=0.1, wait=wait)(*values)


def add_cut(values, parts, dtype=BF, wait=()):
    rows = values[0].shape[0] // parts
    shape = values[0].shape[1:] if rows == 1 else (rows,) + values[0].shape[1:]
    return call(functools.partial(add_kernel, len(values)), [sds(shape, dtype)] * parts, name="add", cost=0.1, wait=wait)(*values)


def add_low(*values, wait=()):
    return add_cut(values, 1, wait=wait)[0]


def body(
    tokens_in, teacher_in, out_grad, mask_pos, slot_ids, w_query, b_query, w_key, b_key, w_value,
    b_value, w_out, b_out, ln1_gain, ln1_bias, w_up, b_up, w_down, b_down, ln2_gain, ln2_bias,
    w_proj, b_proj, t_query, t_key, t_value, t_out, t_up, t_down, embedding,
):
    planes, peers = lax.axis_size("z"), lax.axis_size("p")
    z_at, p_at = lax.axis_index("z"), lax.axis_index("p")
    me = jnp.stack([z_at, p_at, lax.axis_index("batch")]).astype(jnp.int32)
    groups = planes * peers
    seq_count, per_device, width = tokens_in.shape
    t_width = teacher_in.shape[2]
    ff = w_up.shape[1]
    own = seq_count * per_device
    length = per_device * groups
    cap = mask_pos.shape[1] // groups
    slots = planes * cap
    size = width // HEADS
    per_group = max(n for n in range(1, LANES // size + 1) if HEADS % n == 0)
    pad = HEADS // per_group * LANES
    roomy = 16 + length // 256

    vectors = (b_out, ln1_gain, ln1_bias, b_down, ln2_gain, ln2_bias, b_up, b_proj, b_query, b_key, b_value)
    at_vec = [0]
    for vector in vectors:
        at_vec.append(at_vec[-1] - (-vector.shape[0] // LANES))
    vec_lines = -(-at_vec[-1] // 8) * 8
    down = w_down.T

    raws = (mask_pos, slot_ids, w_query, w_key, w_value, w_out) + vectors
    vec, live, want, line, wqkv, bqkv, wo = call(
        functools.partial(
            prepare_kernel, list(reversed(bits_of(peers))), cap, per_device, peers, embedding.shape[0], at_vec
        ),
        [
            sds((vec_lines, LANES), F32), sds((groups, 1, LANES), F32), sds((groups, 1, LANES), jnp.int32),
            sds((1, LANES), jnp.int32), sds((width, 3 * pad), BF), sds((1, 3 * pad), F32), sds((pad, width), BF),
        ],
        [pltpu.VMEM(raw.shape, raw.dtype) for raw in raws] + [pltpu.SemaphoreType.DMA((len(raws),))],
        name="prepare",
        cost=3,
        far=range(1, 1 + len(raws)),
    )(me, *raws)
    flipped = call(flip_kernel, [sds(embedding.shape[::-1], BF)], name="flip", cost=2)(embedding)[0]

    def packed(parts, wait=()):
        shape = sds((per_device, sum(part.shape[2] for part in parts)), BF)
        return call(
            functools.partial(pack_kernel, len(parts)), [shape] * planes, name="pack", cost=0.5, wait=wait
        )(me, *parts)

    def unpacked(blocks, widths, wait=()):
        shapes = [sds((own, each), BF) for each in widths]
        return call(
            functools.partial(split_kernel, len(widths)), shapes, name="split", cost=0.2, wait=wait
        )(*blocks)

    blocks = spread_over_z(packed([teacher_in, tokens_in, out_grad]))
    t_rows, s_rows, og_rows = unpacked(blocks, [t_width, width, width], wait=[passed(line)])
    s_pieces = plane_pieces(s_rows)
    q, kv, keep, output, s_pick = call(
        functools.partial(student_kernel, at_vec),
        [
            sds((own, pad), BF), sds((length, 2 * pad), BF), sds((own, 3 * pad + LANES), F32),
            sds((own, width), BF), sds((slots, width), BF),
        ],
        limit=roomy,
        name="student",
        cost=8,
    )(line, vec, wqkv, bqkv, wo, w_up, down, *s_pieces)

    wide = t_width if length <= 2048 else 2 * LANES
    t_across = swap(copied([t_rows], [s_pieces[1]])[0], "p", bits_of(peers)[-1])
    if peers == 4:
        t_pieces = [t_rows, t_across, swap(t_rows, "p", 1), swap(copied([t_across], [passed(s_pick)])[0], "p", 1)]
    else:
        t_pieces = plane_both(t_rows, t_across)
    t_att, t_q, t_k, t_mark = call(
        teacher_attend_kernel,
        [sds((own, t_width), F32), sds((own, t_width), BF), sds((length, t_width), BF), sds((8, LANES), F32)],
        [pltpu.VMEM((length, wide), BF)],
        limit=roomy,
        name="teacher_attend",
        cost=9,
    )(t_query, t_key, t_value, *t_pieces)
    t_output, t_pick = call(
        teacher_feed_kernel,
        [sds((own, t_width), F32), sds((slots, t_width), BF)],
        name="teacher_feed",
        cost=6,
    )(line, t_pieces[0], t_att, t_out, t_up, t_down)

    def placed(parts, dtype, wait=()):
        shape = sds((planes, per_device, width), dtype)
        return call(place_kernel, [shape], name="place", cost=0.1, wait=wait)(me, *parts)[0]

    s_all = plane_pieces(gather_z(s_pick, passed(t_mark)))
    t_parts = spread_over_z([t_pick] * planes)
    t_across = [swap(t_pick, "p", bits_of(peers)[-1])]
    here = s_all[0].shape[0]
    blocks = here // slots
    stat_shape = sds((blocks, 1, LANES), F32)
    logit_shapes = [sds((here, embedding.shape[0]), BF), stat_shape, stat_shape]
    def logits(at_bias, pieces, name, cost, wait=()):
        got = call(
            functools.partial(logits_kernel, at_bias, slots, 2), logit_shapes * 2, limit=20, name=name, cost=cost, wait=wait
        )(*pieces, flipped, *(() if at_bias is None else (w_proj, vec)))
        return [got[:3], got[3:]]

    def in_order(first, second):
        return zip(first[0], second[0], first[1], second[1])

    s_first = logits(at_vec[7], [s_all[0], s_all[2]], "s_logits", 4, wait=[t_pick])
    s_second = logits(at_vec[7], [s_all[1], s_all[3]], "s_logits", 0.1, wait=[s_first[0][1]])
    t_parts = copied(t_parts, [passed(s_second[0][1])])
    t_across += [swap(part, "p", bits_of(peers)[-1]) for part in t_parts[1:]]
    t_all = [stacked(t_parts)]
    if peers == 4:
        t_all += [None, swap(t_all[0], "p", 1), None]
    else:
        t_all = plane_both(t_all[0], stacked(t_across))
    t_first = logits(None, [t_all[0], t_all[2]], "t_logits", 4)
    again = call(
        functools.partial(feed_again_kernel, at_vec),
        [
            sds((own, width), BF), sds((own, ff), BF), sds((own, ff), F32), sds((own, width), F32),
            sds((width, t_width), F32), sds((1, t_width), F32),
        ] + [sds((per_device, width), BF)] * planes,
        name="feed_again",
        cost=0.5,
        wait=[t_first[0][1]],
    )(vec, w_proj, w_up, og_rows, t_output, output, keep)
    out_blocks = spread_over_z(again[6:])
    if peers == 4:
        t_all[1] = stacked(t_across, wait=[passed(t_first[0][1])] + out_blocks[1:])
        t_all[3] = swap(t_all[1], "p", 1)
    t_second = logits(None, [t_all[1], t_all[3]], "t_logits", 4)
    s_raised, s_top, s_lse = in_order(s_first, s_second)
    t_raised, t_top, t_lse = in_order(t_first, t_second)
    stat = jnp.concatenate([jnp.concatenate(s_lse, axis=0), jnp.concatenate(t_lse, axis=0)], axis=1)
    stats = gather_plane(gather_z(stat[None]))
    sums = []
    crossing = []

    def combined(turn, wait):
        outs = [sds((here, width), BF), sds((width, t_width), F32), sds((1, t_width), F32)]
        back, *sums[:] = call(
            functools.partial(combine_kernel, turn * blocks, slots, bool(sums)),
            outs,
            [pltpu.VMEM((here, embedding.shape[0]), BF)],
            name="combine", cost=3, wait=wait,
        )(
            *sums, live, want, s_top[turn], t_top[turn], stats, s_raised[turn], t_raised[turn], s_all[turn], embedding, w_proj,
        )
        return back

    def reduced(turn, bits, wait=()):
        if not bits:
            return combined(turn, wait)
        bit = bits[-1]
        far = reduced(turn + len(s_all) // (2 * bit), bits[:-1], wait)
        near = reduced(turn, bits[:-1], [far])
        if len(bits) == 2:
            crossing.append(far)
            if peers == 4:
                return add_cut([near, swap(far, "p", bit)], planes)
        return add_low(near, swap(far, "p", bit))

    back = reduced(0, bits_of(len(s_all)))
    for bit in bits_of(peers)[2:]:
        half = back.shape[0] // 2
        back = add_low(back[:half], swap(back[half:], "p", bit))
    if peers > 4:
        back = add_cut([back], planes)
    ce = spread_over_z(back)

    lanes_of = lambda many: -(-many // LANES) * LANES
    at_up, at_down = 0, lanes_of(ff)
    at_proj = at_down + lanes_of(ff)
    at_out = at_proj + lanes_of(t_width)
    layout = (at_up, at_down, at_proj, at_out)
    unit = 2 * planes * LANES
    wide_lanes = -(-(at_out + lanes_of(width)) // unit) * unit
    thin_lanes = -(-3 * width // unit) * unit
    tall = -(-(width + 8) // 64) * 64
    wide_block = sds((4, planes, tall // 4, wide_lanes // (2 * planes)), BF)
    thin_block = sds((4, planes, tall // 4, thin_lanes // (2 * planes)), BF)
    d_att, d_res, wide_mine, wide_send = call(
        functools.partial(feed_back_kernel, layout, at_vec),
        [sds((own, pad), BF), sds((own, width), F32), wide_block, wide_block],
        [pltpu.VMEM((tall, wide_lanes), F32)],
        name="feed_back", cost=4,
    )(me, line, vec, *sums, *again[:6], down, w_up, wo, keep, *ce)

    def attend_back(group, cost, *done):
        return call(
            functools.partial(attend_back_kernel, 2.0 / (HEADS * length), size, group),
            [sds((own, LANES), BF), sds((length, LANES), BF), sds((length, LANES), BF), sds((8, LANES), F32)],
            [pltpu.VMEM((own, LANES), F32)],
            limit=20,
            name="attend_back",
            cost=cost,
            wait=done,
        )(d_att, keep, q, kv, t_q, t_k)

    head_groups = pad // LANES
    wide_other = swap(wide_send, "p", 1)
    wide_parts = add_cut([wide_mine, wide_other], 4)
    wide_near = [swap_xy(wide_parts[key], key) for key in range(1, 4)]
    grads = [attend_back(0, 4)]
    for group in range(1, head_groups):
        grads.append(attend_back(group, 0.1, wide_parts[0], *grads[-1]))
    layer_out = placed(out_blocks, BF, wait=[d_res])
    wide_line = add_cut([wide_parts[0]] + wide_near, planes, wait=[grads[-1][3]])
    kinds = [list(kind) for kind in zip(*grads)]
    thin_mine, thin_send = call(
        functools.partial(attend_weights_kernel, head_groups),
        [thin_block, thin_block],
        [pltpu.VMEM((tall, 3 * pad), F32), pltpu.VMEM((tall, thin_lanes), F32)],
        name="attend_weights",
        cost=0.1,
    )(me, *[part for kind in kinds for part in kind], *s_pieces)
    g_far, g_near, g_own = call(
        functools.partial(attend_rows_kernel, head_groups),
        [sds((length // 2, width), BF), sds((length // 2, width), BF), sds((own, width), F32)],
        name="attend_rows",
        cost=0.1,
        wait=[layer_out, wide_line[0], thin_mine],
    )(wqkv, d_res, *[part for kind in kinds[:3] for part in kind])

    thin_other, g_other = swap(thin_send, "p", 1), swap(g_far, "p", 1)
    thin_parts = add_cut([thin_mine, thin_other], 4)
    thin_near = [swap_xy(thin_parts[key], key) for key in range(1, 4)]
    g_parts = add_cut([g_near, g_other], peers // 2)
    for bit in bits_of(peers)[1:-1]:
        half = len(g_parts) // 2
        moved = swap(jnp.concatenate(g_parts[half:], axis=0), "p", bit)
        g_parts = add_cut([jnp.concatenate(g_parts[:half], axis=0), moved], half)
    total = add_cut([g_own, g_parts[0], swap(g_parts[1], "p", bits_of(peers)[-1])], planes)

    def finished(value):
        for bit in bits_of(peers)[2:]:
            value = add_low(value, swap(value, "p", bit))
        return value

    wide_sum = finished(add_low(*spread_over_z(wide_line), wait=thin_near + [total[0]]))
    thin_shape = (planes, tall // 4, thin_lanes // (2 * planes))
    side_rows = planes * tall // 4 + per_device * (lanes_of(width) // LANES)
    tails = call(
        functools.partial(side_kernel, 4), [sds((side_rows, LANES), BF)] * planes, name="side", cost=0.1
    )(thin_parts[0], *thin_near, *total)
    wide_all = stacked(spread_over_z([wide_sum] * planes), joined=False)
    tails = spread_over_z(tails)
    thin_all, input_grad = call(
        functools.partial(tail_kernel, planes),
        [sds(thin_shape, BF), sds((planes, per_device, width), F32)],
        name="tail",
        cost=0.1,
        wait=[wide_all],
    )(me, *tails)
    thin_all = finished(thin_all)
    wide_far = [swap_xy(wide_all, key) for key in range(1, 4)]
    thin_far = [swap_xy(thin_all, key) for key in range(1, 4)]
    wide_all = stacked([wide_all] + wide_far, joined=False, wait=[thin_all])
    thin_all = stacked([thin_all] + thin_far, joined=False, wait=[wide_all])
    wide_all = [wide_all, swap(wide_all, "p", 1)]
    thin_all = [thin_all, swap(thin_all, "p", 1)]
    square = sds((width, width), F32)
    gout, gup, gdown, gproj, *vecs = call(
        functools.partial(unpack_wide_kernel, layout, ff, width, t_width, planes),
        [square, sds((width, ff), F32), sds((width, ff), F32), sds((width, t_width), F32)]
        + [sds(vector.shape, F32) for vector in vectors[:8]] + [sds((8, LANES), F32)],
        [pltpu.VMEM((tall, wide_lanes), F32)],
        limit=24,
        name="unpack_wide",
        cost=3,
    )(me, *wide_all)
    gbo, gg1, gc1, gbd, gg2, gc2, gbup, gbproj, wide_mark = vecs
    gq, gk, gv, gbq, gbk, gbv = call(
        functools.partial(unpack_thin_kernel, planes),
        [square] * 3 + [sds((width,), F32)] * 3,
        [pltpu.VMEM((tall, thin_lanes), F32)],
        name="unpack_thin",
        cost=1,
        wait=[passed(wide_mark)],
    )(me, *thin_all)
    return (
        layer_out, input_grad, gq, gbq, gk, gbk, gv, gbv, gout, gbo, gg1, gc1, gup, gbup, gdown.T, gbd, gg2, gc2,
        gproj, gbproj,
    )


def solution(mesh):
    batch, seq = mesh.shape["batch"], mesh.shape["seq"]
    split = P("batch", ("z", "p"), None)
    in_specs = (split,) * 3 + (P("batch", None),) * 2 + (P(),) * 24 + (P(("z", "p"), None),)
    out_specs = (split,) * 2 + (P(),) * 18

    def run(*args):
        planes = args[0].shape[0] // batch
        fine = Mesh(mesh.devices.reshape(batch, planes, seq // planes), ("batch", "z", "p"))
        return jax.shard_map(body, mesh=fine, in_specs=in_specs, out_specs=out_specs, check_vma=False)(*args)

    return run
```

```python
import functools
import math

import jax
import jax.numpy as jnp
from jax import lax
from jax.experimental import pallas as pl
from jax.experimental.pallas import tpu as pltpu
from jax.sharding import Mesh
from jax.sharding import PartitionSpec as P

HEADS = 12
EPSILON = 1e-06
HID_WEIGHT = 0.05
CE_WEIGHT = 4.0
MIXING = 0.5
ROOT_HALF = 0.7071067811865476
ROOT_TWO_PI = 2.5066282746310002
LANES = 128
BF = jnp.bfloat16
F32 = jnp.float32
MIB = 1 << 20


def mm(left, right):
    return lax.dot_general(left, right, (((1,), (0,)), ((), ())), preferred_element_type=F32)


def mm_nt(left, right):
    return lax.dot_general(left, right, (((1,), (1,)), ((), ())), preferred_element_type=F32)


def mm_tn(left, right):
    return lax.dot_general(left, right, (((0,), (0,)), ((), ())), preferred_element_type=F32)


def normalize(values):
    centered = values - jnp.mean(values, axis=-1, keepdims=True)
    inverse = lax.rsqrt(jnp.mean(centered * centered, axis=-1, keepdims=True) + EPSILON)
    return centered * inverse, inverse


def norm_back(grads, scaled, inverse):
    return inverse * (
        grads
        - jnp.mean(grads, axis=-1, keepdims=True)
        - scaled * jnp.mean(grads * scaled, axis=-1, keepdims=True)
    )


def gelu(inputs):
    return inputs * (0.5 * (1.0 + lax.erf(inputs * ROOT_HALF)))


def column_sum(values):
    return jnp.sum(values.astype(F32), axis=0, keepdims=True)


def attend(at, q_ref, k_ref, v_ref, per_group, size, emit):
    rows = at.size if isinstance(at, pl.Slice) else at.stop - at.start
    heads = q_ref.shape[1] // LANES * per_group
    lane = lax.broadcasted_iota(jnp.int32, (rows, LANES), 1)
    scaling = math.log2(math.e) / math.sqrt(size)

    def scores_of(head):
        cols = slice(head // per_group * LANES, (head // per_group + 1) * LANES)
        low = head % per_group * size
        mask = (lane >= low) & (lane < low + size)
        query = jnp.where(mask, q_ref[at, cols].astype(F32), 0.0).astype(BF)
        return cols, mask, mm_nt(query, k_ref[:, cols])

    later = scores_of(0)
    for head in range(heads):
        cols, mask, scores = later
        later = scores_of(head + 1) if head + 1 < heads else None
        top = jnp.max(scores, axis=-1, keepdims=True) * scaling
        weights = jnp.exp2(scores * scaling - top)
        total = jnp.sum(weights, axis=-1, keepdims=True)
        mixed = mm(weights.astype(BF), v_ref[:, cols])
        emit(head, cols, mask, mixed * (1.0 / total), top + jnp.log2(total))


def over_rows(own, length, one):
    if length <= 2048:
        one(slice(0, own))
    else:
        step = 64

        def inside(turn, carry):
            one(pl.ds(pl.multiple_of(turn * step, step), step))
            return carry

        lax.fori_loop(0, own // step, inside, 0)


COSTS = {
    "add:0": 20,
    "add:1": 7,
    "add:2": 0.5,
    "add:3": 20,
    "add:4": 0.1,
    "add:6": 2,
    "add:7": 12,
    "add:8": 1,
    "attend_back:0": 20,
    "attend_back:2": 2,
    "attend_ready:0": 20,
    "attend_rows:0": 12,
    "attend_weights:0": 1,
    "bottom:0": 12,
    "combine:0": 20,
    "combine:3": 4,
    "copy:0": 7,
    "copy:1": 0.5,
    "copy:2": 1,
    "copy:3": 12,
    "feed_again:0": 12,
    "feed_back:0": 7,
    "flip:0": 0.05,
    "s_logits:0": 7,
    "s_logits:1": 7,
    "side:0": 12,
    "split:0": 4,
    "stack:0": 12,
    "stack:1": 7,
    "stack:2": 1,
    "stack:3": 4,
    "stack:4": 20,
    "stack:5": 20,
    "student:0": 4,
    "t_logits:1": 0.1,
    "tail:0": 1,
    "teacher_attend:0": 2,
    "teacher_feed:0": 12,
    "unpack_thin:0": 20,
    "unpack_wide:0": 1,
}
FREE = frozenset((
    "add:0",
    "add:2",
    "add:4",
    "add:5",
    "add:6",
    "add:8",
    "attend_ready:2",
    "attend_rows:0",
    "combine:1",
    "combine:2",
    "combine:3",
    "feed_back:0",
    "s_logits:0",
    "side:0",
    "split:0",
    "stack:1",
    "student:0",
    "tail:0",
))
DIRECT = frozenset((
    "passed:1",
    "passed:4",
    "passed:5",
))
AFTER = {
    "add:0": ("t_logits:1", "swap:22"),
    "add:2": ("swap:28",),
    "add:3": ("add:2",),
    "add:4": ("swap:42",),
    "add:5": ("bottom:0", "add:4"),
    "add:6": ("add:5", "swap:50"),
    "add:7": ("swap:48",),
    "add:8": ("swap:50", "add:5"),
    "attend_back:1": ("feed_again:0",),
    "combine:0": ("swap:28", "attend_ready:1"),
    "combine:2": ("add:0", "swap:26"),
    "copy:0": ("swap:4",),
    "copy:1": ("split:0",),
    "copy:2": ("swap:4", "swap:11"),
    "copy:3": ("swap:26", "swap:19"),
    "feed_back:0": ("feed_again:0", "add:2"),
    "s_logits:0": ("swap:25",),
    "s_logits:1": ("top:0",),
    "side:0": ("swap:50",),
    "stack:0": ("swap:7",),
    "stack:3": ("attend_back:1",),
    "stack:4": ("add:7",),
    "stack:5": ("add:7", "swap:59"),
    "t_logits:0": ("swap:16",),
    "t_logits:1": ("t_logits:0", "swap:14"),
    "tail:0": ("swap:57",),
    "teacher_feed:0": ("swap:6", "swap:2", "split:0"),
    "top:0": ("swap:19",),
}
TURNS = {}
RESULTS = {}


def turn_of(name):
    TURNS[name] = TURNS.get(name, -1) + 1
    return f"{name}:{TURNS[name]}"


def begin(tuned):
    TURNS.clear()
    RESULTS.clear()
    RESULTS["tuned"] = tuned


def call(kernel, outs, scratch=(), limit=16, name=None, cost=1, far=(), wait=()):
    spaces = {"vmem": pltpu.VMEM, "smem": pltpu.SMEM, "far": pl.ANY}

    def space(at, arg):
        small = arg.ndim == 1 and arg.dtype == jnp.int32
        return pl.BlockSpec(memory_space=spaces["far" if at in far else "smem" if small else "vmem"])

    def run(*args):
        turn, price, later = turn_of(name), cost, list(wait)
        if RESULTS["tuned"]:
            price = COSTS.get(turn, cost)
            later = [] if turn in FREE else later
            later += [RESULTS[key] for key in AFTER.get(turn, ()) if key in RESULTS]
        count = len(args)

        def body_of(*refs):
            kernel(*refs[:count], *refs[count + len(later):])

        results = pl.pallas_call(
            body_of,
            out_shape=outs,
            in_specs=[space(at, arg) for at, arg in enumerate(args)] + [pl.BlockSpec(memory_space=pl.ANY)] * len(later),
            out_specs=[pl.BlockSpec(memory_space=pltpu.VMEM)] * len(outs),
            scratch_shapes=list(scratch),
            compiler_params=pltpu.CompilerParams(vmem_limit_bytes=limit * MIB),
            cost_estimate=pl.CostEstimate(
                flops=int(price * 1e9), bytes_accessed=int(price * 3e6), transcendentals=0
            ),
            name=name,
        )(*args, *later)
        RESULTS[turn] = results[0]
        return results

    return run


def sds(shape, dtype):
    return jax.ShapeDtypeStruct(shape, dtype)


def lines_of(ref, first, width):
    count = -(-width // LANES)
    return jnp.concatenate([ref[at:at + 1, :] for at in range(first, first + count)], axis=1)[:, :width]


def pack_kernel(many, me_ref, *refs):
    held, outs = refs[:many], refs[many:]
    for key, out in enumerate(outs):
        at = 0
        for ref in held:
            width = ref.shape[2]
            out[:, at:at + width] = ref[jnp.bitwise_xor(me_ref[0], key)]
            at += width


def split_kernel(many, *refs):
    ins, outs = refs[:-many], refs[-many:]
    rows = ins[0].shape[0]
    for turn, ref in enumerate(ins):
        at = 0
        for out in outs:
            width = out.shape[1]
            out[turn * rows:(turn + 1) * rows, :] = ref[:, at:at + width]
            at += width


def flip_kernel(table_ref, flip_ref):
    flip_ref[...] = table_ref[...].T


def prepare_kernel(order, cap, per_device, peers, vocab_rows, at_vec, me_ref, *refs):
    many_in = 6 + len(at_vec) - 1
    sources, outs, copied = refs[:many_in], refs[many_in:many_in + 7], refs[many_in + 7:-1]
    vec_ref, live_ref, want_ref, line_ref, wqkv_ref, bqkv_ref, wo_ref = outs
    copies = [pltpu.make_async_copy(*pair, refs[-1].at[at]) for at, pair in enumerate(zip(sources, copied))]
    for copy in copies:
        copy.start()
    for copy in copies:
        copy.wait()
    pos_ref, ids_ref, wq_ref, wk_ref, wv_ref, wout_ref, *vec_refs = copied
    vec_ref[...] = jnp.zeros_like(vec_ref)
    rows_of = [ref[...].astype(F32).reshape(1, ref.shape[0]) for ref in vec_refs]
    for first, value in zip(at_vec, rows_of):
        for at in range(0, value.shape[1], LANES):
            part = value[:, at:at + LANES]
            vec_ref[first + at // LANES:first + at // LANES + 1, :part.shape[1]] = part
    width = wq_ref.shape[0]
    pad = wo_ref.shape[0]
    valid = width * LANES // pad
    row = lax.broadcasted_iota(jnp.int32, (width, pad), 0)
    col = lax.broadcasted_iota(jnp.int32, (width, pad), 1)
    inside = lax.rem(col, LANES)
    select = jnp.where((inside < valid) & (row == lax.div(col, LANES) * valid + inside), 1.0, 0.0).astype(BF)
    for at, ref in enumerate((wq_ref, wk_ref, wv_ref)):
        wqkv_ref[:, at * pad:(at + 1) * pad] = mm(ref[...], select).astype(BF)
        bias = jnp.broadcast_to(rows_of[8 + at], (8, width)).astype(BF)
        bqkv_ref[:, at * pad:(at + 1) * pad] = mm(bias, select)[:1]
    wo_ref[...] = mm_tn(select, wout_ref[...]).astype(BF)

    planes, many = pos_ref.shape
    z_at, p_at = me_ref[0], me_ref[1]
    first = (z_at * peers + p_at) * vocab_rows
    lane = lax.broadcasted_iota(jnp.int32, (8, LANES), 1)

    def lines(ref, seq, peer):
        whole = jnp.broadcast_to(ref[pl.ds(seq, 1), :], (8, many))
        out = jnp.full((8, LANES), -1, jnp.int32)
        for plane in range(planes):
            shift = lax.rem(plane * cap - (plane * peers + peer) * cap + 2 * many, many)
            moved = pltpu.roll(whole, shift, 1)[:, :LANES]
            out = jnp.where((lane >= plane * cap) & (lane < (plane + 1) * cap), moved, out)
        return out

    own = lines(pos_ref, z_at, p_at)
    local = own
    for plane in range(planes):
        move = jnp.bitwise_xor(z_at, plane) * per_device - (plane * peers + p_at) * per_device
        local = jnp.where((lane >= plane * cap) & (lane < (plane + 1) * cap), own + move, local)
    line_ref[...] = jnp.where(own >= 0, local, -1)[:1]

    def one(turn, carry):
        key = jnp.int32(0)
        for bit, value in enumerate(order):
            key = jnp.where(lax.rem(lax.div(turn, 1 << bit), 2) == 1, jnp.bitwise_xor(key, value), key)
        for plane in range(planes):
            seq, peer = jnp.bitwise_xor(z_at, plane), jnp.bitwise_xor(p_at, key)
            live_ref[turn * planes + plane] = jnp.where(lines(pos_ref, seq, peer) >= 0, 1.0, 0.0)[:1]
            want_ref[turn * planes + plane] = (lines(ids_ref, seq, peer) - first)[:1]
        return carry

    lax.fori_loop(0, peers, one, 0)


def top_kernel(many, *refs):
    ins, (out,) = refs[:many], refs[many:]
    rows = out.shape[0] // many
    for turn, ref in enumerate(ins):
        out[turn * rows:(turn + 1) * rows, :] = ref[:rows, :]


def bottom_kernel(first, me_ref, *refs):
    *ins, out_ref = refs
    for key, ref in enumerate(ins):
        out_ref[jnp.bitwise_xor(me_ref[0], key)] = ref[first:, :]


def place_kernel(me_ref, *refs):
    *ins, out_ref = refs
    for key, ref in enumerate(ins):
        out_ref[jnp.bitwise_xor(me_ref[0], key)] = ref[...].astype(out_ref.dtype)


def pick(line_ref, slots, values):
    own = values.shape[0]
    at = lax.broadcasted_iota(jnp.int32, (own, LANES), 0)
    chosen = jnp.where(at == line_ref[...], 1.0, 0.0).astype(BF)
    return mm_tn(chosen, values)[:slots]


def teacher_attend_kernel(tq_ref, tk_ref, tv_ref, *refs):
    *row_refs, att_ref, q_ref, k_ref, mark_ref, v_scr, x_scr = refs
    mark_ref[...] = jnp.zeros_like(mark_ref)
    own = q_ref.shape[0]
    width = tq_ref.shape[1]
    size = width // HEADS
    per_group = LANES // size
    wide = v_scr.shape[1]
    q_ref[...] = mm(row_refs[0][:own], tq_ref[...]).astype(BF)
    for part in range(width // wide):
        cols = slice(part * wide, (part + 1) * wide)
        at = 0
        for row_ref in row_refs:
            there = slice(at, at + row_ref.shape[0])
            if x_scr.shape[0] == v_scr.shape[0]:
                x_scr[there, :] = row_ref[...]
            else:
                k_ref[there, cols] = mm(row_ref[...], tk_ref[:, cols]).astype(BF)
                v_scr[there, :] = mm(row_ref[...], tv_ref[:, cols]).astype(BF)
            at += row_ref.shape[0]
        if x_scr.shape[0] == v_scr.shape[0]:
            k_ref[:, cols] = mm(x_scr[...], tk_ref[:, cols]).astype(BF)
            v_scr[...] = mm(x_scr[...], tv_ref[:, cols]).astype(BF)
        out_ref = att_ref.at[:, cols]

        def one(at):
            def emit(head, there, mask, mixed, lse):
                out_ref[at, there] = mixed if head % per_group == 0 else jnp.where(mask, mixed, out_ref[at, there])

            attend(at, q_ref.at[:, cols], k_ref.at[:, cols], v_scr, per_group, size, emit)

        over_rows(own, v_scr.shape[0], one)


def teacher_feed_kernel(line_ref, rows_ref, att_ref, to_ref, up_ref, down_ref, out_ref, pick_ref):
    own, width = att_ref.shape
    branch = mm(att_ref[...].astype(BF), to_ref[...])
    hidden, _ = normalize(rows_ref[:own].astype(F32) + branch)
    low = hidden.astype(BF)
    step = width
    outer = jnp.zeros((own, width), F32)
    for at in range(0, up_ref.shape[1], step):
        inner = gelu(mm(low, up_ref[:, at:at + step])).astype(BF)
        outer = outer + mm(inner, down_ref[at:at + step])
    output, _ = normalize(hidden + outer)
    out_ref[...] = output
    pick_ref[...] = pick(line_ref, pick_ref.shape[0], output.astype(BF)).astype(BF)


def student_kernel(
    at_vec, planes, line_ref, vec_ref, wqkv_ref, bqkv_ref, wo_ref, up_ref, down_ref, *refs,
):
    *row_refs, q_ref, kv_ref, keep_ref, out_ref, mark_ref = refs[:-planes]
    block_refs = refs[-planes:]
    mark_ref[...] = jnp.zeros_like(mark_ref)
    own, pad = q_ref.shape
    length = kv_ref.shape[0]
    width = wo_ref.shape[1]
    ff = up_ref.shape[1]
    size = width // HEADS
    per_group = HEADS * LANES // pad
    rows = row_refs[0][:own]
    q_ref[...] = (mm(rows, wqkv_ref[:, :pad]) + bqkv_ref[:, :pad]).astype(BF)
    at = 0
    for row_ref in row_refs:
        there = slice(at, at + row_ref.shape[0])
        kv_ref[there, :] = (mm(row_ref[...], wqkv_ref[:, pad:]) + bqkv_ref[:, pad:]).astype(BF)
        at += row_ref.shape[0]
    k_ref, v_ref = kv_ref.at[:, :pad], kv_ref.at[:, pad:]
    keep_ref[:, pad:] = jnp.zeros((own, keep_ref.shape[1] - pad), F32)
    stat = slice(3 * pad, 3 * pad + LANES)

    def one(at):
        def emit(head, there, mask, mixed, lse):
            old = 0.0 if head % per_group == 0 else keep_ref[at, there]
            keep_ref[at, there] = jnp.where(mask, mixed, old)
            lane = lax.broadcasted_iota(jnp.int32, (lse.shape[0], LANES), 1)
            keep_ref[at, stat] = jnp.where(lane == head, lse, keep_ref[at, stat])

        attend(at, q_ref, k_ref, v_ref, per_group, size, emit)

    over_rows(own, length, one)
    bo, g1, c1, bdown, g2, c2 = (lines_of(vec_ref, at, width) for at in at_vec[:6])
    branch = mm(keep_ref[:, :pad].astype(BF), wo_ref[...]) + bo
    n1, i1 = normalize(rows.astype(F32) + branch)
    hidden = n1 * g1 + c1
    inner = mm(hidden.astype(BF), up_ref[...]) + lines_of(vec_ref, at_vec[6], ff)
    outer = mm_nt(gelu(inner).astype(BF), down_ref[...]) + bdown
    n2, i2 = normalize(hidden + outer)
    output = (n2 * g2 + c2).astype(BF)
    keep_ref[:, pad:pad + width] = n1
    keep_ref[:, 2 * pad:2 * pad + width] = n2
    at = lax.broadcasted_iota(jnp.int32, (own, LANES), 1)
    keep_ref[:, stat] = jnp.where(at == HEADS, i1, jnp.where(at == HEADS + 1, i2, keep_ref[:, stat]))
    out_ref[...] = output
    each = own // planes
    slots = block_refs[0].shape[0] - each
    picked = pick(line_ref, slots, output).astype(BF)
    for at, ref in enumerate(block_refs):
        ref[:slots] = picked
        ref[slots:] = output[at * each:(at + 1) * each]


def logits_kernel(at_bias, slots, many, *refs):
    pieces, flip_ref, refs = refs[:many], refs[many], refs[many + 1:]
    if at_bias is not None:
        (proj_ref, vec_ref), refs = refs[:2], refs[2:]
        bias = lines_of(vec_ref, at_bias, proj_ref.shape[1])
    rows = pieces[0].shape[0]
    block = 2 * slots
    lane = lax.broadcasted_iota(jnp.int32, (block, LANES), 1)

    def logits_of(piece, at):
        picked = pieces[piece][at, :]
        if at_bias is not None:
            picked = (mm(picked, proj_ref[...]) + bias).astype(BF)
        return mm(picked, flip_ref[...])

    def finish(logits, piece, at, first):
        raised_ref, top_ref, lse_ref = refs[3 * piece:3 * piece + 3]
        top = jnp.max(logits, axis=-1, keepdims=True)
        weights = jnp.exp(logits - top)
        total = top + jnp.log(jnp.sum(weights, axis=-1, keepdims=True))
        raised_ref[at, :] = weights.astype(BF)
        both = jnp.where(lane == 0, top, jnp.where(lane == 1, total, 0.0))
        for part in range(2):
            value = both[part * slots:(part + 1) * slots]
            if slots < LANES:
                value = jnp.concatenate([value, jnp.zeros((LANES - slots, LANES), F32)], axis=0)
            value = value.T
            top_ref[first + part] = value[0:1]
            lse_ref[first + part] = value[1:2]

    if rows // block <= 2:
        work = [(piece, at) for piece in range(many) for at in range(0, rows, block)]
        later = logits_of(work[0][0], slice(work[0][1], work[0][1] + block))
        for turn, (piece, at) in enumerate(work):
            logits = later
            if turn + 1 < len(work):
                after_piece, after_at = work[turn + 1]
                later = logits_of(after_piece, slice(after_at, after_at + block))
            finish(logits, piece, slice(at, at + block), at // slots)
    else:
        for piece in range(many):

            def one(turn, carry, piece=piece):
                at = pl.ds(pl.multiple_of(turn * block, block), block)
                finish(logits_of(piece, at), piece, at, 2 * turn)
                return carry

            lax.fori_loop(0, rows // block, one, 0)


def combine_kernel(first, slots, chained, *refs):
    if chained:
        gproj_in, gbproj_in, *refs = refs
    (
        live_ref, want_ref, s_top_ref, t_top_ref, all_ref, s_ref, t_ref, rows_ref, table_ref, proj_ref,
        back_ref, gproj_ref, gbproj_ref, low_scr,
    ) = refs
    blocks = s_top_ref.shape[0]
    sources = all_ref.shape[0]
    line = lax.broadcasted_iota(jnp.int32, (LANES, LANES), 0)
    column = lax.broadcasted_iota(jnp.int32, (slots, table_ref.shape[0]), 1)
    gbproj_ref[...] = gbproj_in[...] if chained else jnp.zeros_like(gbproj_ref)

    def share(block, which, top):
        known = [all_ref[key, jnp.bitwise_xor(block, key), which:which + 1, :] for key in range(sources)]
        peak = functools.reduce(jnp.maximum, known)
        total = functools.reduce(jnp.add, [jnp.exp(value - peak) for value in known])
        return jnp.exp(top - peak) / total

    def logit_grads(step):
        block = step + first
        at = pl.ds(pl.multiple_of(step * slots, slots), slots)
        live = CE_WEIGHT * live_ref[block]
        s_part = live * share(block, 0, s_top_ref[step])
        t_part = live * (MIXING * share(block, 1, t_top_ref[step]))
        lines = jnp.where(line == 0, s_part, jnp.where(line == 1, t_part, live * (1.0 - MIXING)))
        lines = jnp.where(line == 3, want_ref[block].astype(F32), lines)
        cols = lines.T[:slots]
        hot = jnp.where(column == cols[:, 3:4].astype(jnp.int32), cols[:, 2:3], 0.0)
        grads = cols[:, 0:1] * s_ref[at, :].astype(F32) - cols[:, 1:2] * t_ref[at, :].astype(F32) - hot
        return grads.astype(BF)

    def fill(turn):
        for step in (2 * turn, 2 * turn + 1):
            low_scr[pl.ds(pl.multiple_of(step * slots, slots), slots), :] = logit_grads(step)

    def use(turn):
        at = pl.ds(pl.multiple_of(2 * turn * slots, 2 * slots), 2 * slots)
        picked = mm(low_scr[at, :], table_ref[...])
        gbproj_ref[...] += column_sum(picked)
        picked = picked.astype(BF)
        back_ref[at, :] = mm_nt(picked, proj_ref[...]).astype(BF)
        gproj_ref[...] += mm_tn(rows_ref[at, :], picked)

    def one(turn, carry):
        fill(turn)
        use(turn)
        return carry

    gproj_ref[...] = gproj_in[...] if chained else jnp.zeros_like(gproj_ref)
    if blocks == 4:
        fill(0)
        fill(1)
        use(0)
        use(1)
    else:
        lax.fori_loop(0, blocks // 2, one, 0)


def place(me_ref):
    peer = me_ref[1]
    return me_ref[2] * 2 + lax.rem(lax.div(peer, 2), 2), me_ref[0], lax.rem(peer, 2)


def scatter_blocks(stage_ref, me, keep_ref, send_ref):
    xy_at, z_at, c_at = me
    planes = keep_ref.shape[1]
    rows, wide = keep_ref.shape[2:]
    half = planes * wide
    for xy in range(4):
        for plane in range(planes):
            at, lanes = xy * rows, plane * wide
            key = (jnp.bitwise_xor(xy, xy_at), jnp.bitwise_xor(plane, z_at))
            low = stage_ref[at:at + rows, lanes:lanes + wide]
            high = stage_ref[at:at + rows, half + lanes:half + lanes + wide]
            keep_ref[key] = jnp.where(c_at == 0, low, high).astype(BF)
            send_ref[key] = jnp.where(c_at == 0, high, low).astype(BF)


def feed_again_kernel(at_vec, vec_ref, proj_ref, up_ref, og_ref, tout_ref, out_ref, keep_ref, *refs):
    hid_ref, act_ref, slope_ref, dout_ref, gproj_ref, gbproj_ref = refs
    own, width = og_ref.shape
    pad = (keep_ref.shape[1] - LANES) // 3
    g1, c1 = (lines_of(vec_ref, at_vec[at], width) for at in (1, 2))
    hidden = (keep_ref[:, pad:pad + width] * g1 + c1).astype(BF)
    inner = mm(hidden, up_ref[...]) + lines_of(vec_ref, at_vec[6], up_ref.shape[1])
    cumulative = 0.5 * (1.0 + lax.erf(inner * ROOT_HALF))
    hid_ref[...] = hidden
    act_ref[...] = (inner * cumulative).astype(BF)
    slope_ref[...] = cumulative + inner * (jnp.exp(-0.5 * inner * inner) * (1.0 / ROOT_TWO_PI))
    output = out_ref[...]
    mapped = mm(output, proj_ref[...]) + lines_of(vec_ref, at_vec[7], proj_ref.shape[1])
    d_map = (2.0 * HID_WEIGHT * (mapped - tout_ref[...])).astype(BF)
    gproj_ref[...] = mm_tn(output, d_map)
    gbproj_ref[...] = column_sum(d_map)
    dout_ref[...] = og_ref[...].astype(F32) + mm_nt(d_map, proj_ref[...])


def feed_back_kernel(
    layout, at_vec, me_ref, line_ref, vec_ref, gproj_ref, gbproj_ref, hid_ref, act_ref, slope_ref, dout_ref,
    gproj_add, gbproj_add, down_ref, up_ref, wo_ref, keep_ref, *refs,
):
    *ce_refs, datt_ref, dres_ref, mine_ref, send_ref, stage_ref = refs
    own, width = dout_ref.shape
    pad = wo_ref.shape[0]
    at_up, at_down, at_proj, at_out = layout
    t_width = gproj_ref.shape[1]
    ff = up_ref.shape[1]
    at = lax.broadcasted_iota(jnp.int32, (own, LANES), 0)
    slots = ce_refs[0].shape[0]
    chosen = jnp.where(at == line_ref[...], 1.0, 0.0).astype(BF)[:, :slots]
    ce = functools.reduce(jnp.add, [ref[...].astype(F32) for ref in ce_refs])
    high = ce.astype(BF)
    rest = (ce - high.astype(F32)).astype(BF)
    d_out = dout_ref[...] + mm(chosen, high) + mm(chosen, rest)
    g1, g2 = (lines_of(vec_ref, at_vec[at], width) for at in (1, 4))
    n1, n2 = keep_ref[:, pad:pad + width], keep_ref[:, 2 * pad:2 * pad + width]
    stat = 3 * pad + HEADS
    i1, i2 = keep_ref[:, stat:stat + 1], keep_ref[:, stat + 1:stat + 2]
    stage_ref[width:, :] = jnp.zeros((stage_ref.shape[0] - width, stage_ref.shape[1]), F32)
    stage_ref[:width, at_proj:at_proj + t_width] = gproj_ref[...] + gproj_add[...]
    stage_ref[width:width + 1, at_proj:at_proj + t_width] = gbproj_ref[...] + gbproj_add[...]
    d_res2 = norm_back(d_out * g2, n2, i2)
    d_outer = d_res2.astype(BF)
    stage_ref[:width, at_down:at_down + ff] = mm_tn(d_outer, act_ref[...])
    d_inner = (mm(d_outer, down_ref[...]) * slope_ref[...]).astype(BF)
    stage_ref[:width, at_up:at_up + ff] = mm_tn(hid_ref[...], d_inner)
    stage_ref[width:width + 1, at_up:at_up + ff] = column_sum(d_inner)
    d_hid = d_res2 + mm_nt(d_inner, up_ref[...])
    d_res1 = norm_back(d_hid * g1, n1, i1)
    d_branch = d_res1.astype(BF)
    datt_ref[...] = mm_nt(d_branch, wo_ref[...]).astype(BF)
    dres_ref[...] = d_res1
    gout = mm_tn(keep_ref[:, :pad].astype(BF), d_branch)
    head_groups = pad // LANES
    valid = width // head_groups
    for group in range(head_groups):
        stage_ref[group * valid:(group + 1) * valid, at_out:at_out + width] = gout[group * LANES:group * LANES + valid]
    lines = [
        column_sum(d_branch),
        column_sum(d_hid * n1),
        column_sum(d_hid),
        column_sum(d_outer),
        column_sum(d_out * n2),
        column_sum(d_out),
    ]
    for at, value in enumerate(lines):
        stage_ref[width + at:width + at + 1, at_out:at_out + width] = value
    scatter_blocks(stage_ref, place(me_ref), mine_ref, send_ref)


def attend_back_kernel(
    weight_mse, size, group, datt_ref, keep_ref, q_ref, kv_ref, tq_ref, tk_ref,
    dq_ref, dk_ref, dv_ref, sums_ref, dq_scr,
):
    own, pad = q_ref.shape
    per_group = HEADS * LANES // pad
    t_size = tq_ref.shape[1] // HEADS
    t_group = LANES // t_size
    length = kv_ref.shape[0]
    chunk = length if length <= 2048 else 256
    cols = slice(group * LANES, (group + 1) * LANES)
    v_cols = slice(pad + group * LANES, pad + (group + 1) * LANES)
    s_scaling = 1.0 / math.sqrt(size)
    t_scaling = 1.0 / math.sqrt(t_size)
    lane = lax.broadcasted_iota(jnp.int32, (own, LANES), 1)
    query_all = q_ref[:, cols].astype(F32)
    grad_all = datt_ref[:, cols].astype(F32)
    product = grad_all * keep_ref[:, cols]
    lses = keep_ref[:, 3 * pad:].T
    dots = jnp.zeros((own, LANES), F32)
    heads = []
    for turn in range(per_group):
        head = group * per_group + turn
        mask = (lane >= turn * size) & (lane < (turn + 1) * size)
        dots = jnp.where(lane == turn, jnp.sum(jnp.where(mask, product, 0.0), axis=-1, keepdims=True), dots)
        t_cols = slice(head // t_group * LANES, (head // t_group + 1) * LANES)
        t_low = head % t_group * t_size
        t_mask = (lane >= t_low) & (lane < t_low + t_size)
        heads.append((
            mask,
            jnp.where(mask, query_all, 0.0).astype(BF),
            jnp.where(mask, grad_all, 0.0).astype(BF),
            t_cols,
            jnp.where(t_mask, tq_ref[:, t_cols].astype(F32), 0.0).astype(BF),
            lses[head:head + 1],
        ))
    dots = dots.T
    dq_scr[...] = jnp.zeros_like(dq_scr)
    sums_ref[...] = jnp.zeros_like(sums_ref)

    def one_chunk(at):
        keys, values = kv_ref[at, cols], kv_ref[at, v_cols]
        d_keys, d_values = jnp.zeros(keys.shape, F32), jnp.zeros(keys.shape, F32)

        def products(turn):
            _, query, grad, t_cols, t_query, _ = heads[turn]
            return mm_nt(keys, query), mm_nt(tk_ref[at, t_cols], t_query), mm_nt(values, grad)

        later = products(0)
        for turn, (mask, query, grad, _, _, lse) in enumerate(heads):
            scores, teacher, d_probs = later
            later = products(turn + 1) if turn + 1 < per_group else None
            probs = jnp.exp2(scores * (s_scaling * math.log2(math.e)) - lse)
            d_scores = (
                probs * (d_probs - dots[turn:turn + 1])
                + (scores * (weight_mse * s_scaling) - teacher * (weight_mse * t_scaling))
            ).astype(BF)
            d_keys += mm(d_scores, query)
            d_values += mm(probs.astype(BF), grad)
            dq_scr[...] += jnp.where(mask, mm_tn(d_scores, keys), 0.0)
        d_keys = d_keys * s_scaling
        sums_ref[1:2, :] += column_sum(d_keys)
        sums_ref[2:3, :] += column_sum(d_values)
        dk_ref[at, :] = d_keys.astype(BF)
        dv_ref[at, :] = d_values.astype(BF)

    if chunk == length:
        one_chunk(slice(0, length))
    else:

        def inside(turn, carry):
            one_chunk(pl.ds(pl.multiple_of(turn * chunk, chunk), chunk))
            return carry

        lax.fori_loop(0, length // chunk, inside, 0)
    d_queries = dq_scr[...] * s_scaling
    sums_ref[0:1, :] = column_sum(d_queries)
    dq_ref[...] = d_queries.astype(BF)


def attend_ready_kernel(weight_mse, size, group, keep_ref, q_ref, kv_ref, tq_ref, tk_ref, probs_ref, gap_ref):
    own, pad = q_ref.shape
    per_group = probs_ref.shape[0]
    t_size = tq_ref.shape[1] // HEADS
    t_group = LANES // t_size
    cols = slice(group * LANES, (group + 1) * LANES)
    s_scaling = 1.0 / math.sqrt(size)
    t_scaling = 1.0 / math.sqrt(t_size)
    lane = lax.broadcasted_iota(jnp.int32, (own, LANES), 1)
    lses = keep_ref[:, 3 * pad:].T

    def products(turn):
        head = group * per_group + turn
        mask = (lane >= turn * size) & (lane < (turn + 1) * size)
        query = jnp.where(mask, q_ref[:, cols].astype(F32), 0.0).astype(BF)
        t_cols = slice(head // t_group * LANES, (head // t_group + 1) * LANES)
        t_low = head % t_group * t_size
        t_mask = (lane >= t_low) & (lane < t_low + t_size)
        t_query = jnp.where(t_mask, tq_ref[:, t_cols].astype(F32), 0.0).astype(BF)
        return mm_nt(kv_ref[:, cols], query), mm_nt(tk_ref[:, t_cols], t_query)

    later = products(0)
    for turn in range(per_group):
        scores, teacher = later
        later = products(turn + 1) if turn + 1 < per_group else None
        lse = lses[group * per_group + turn:group * per_group + turn + 1]
        probs_ref[turn] = jnp.exp2(scores * (s_scaling * math.log2(math.e)) - lse).astype(BF)
        gap_ref[turn] = (scores * (weight_mse * s_scaling) - teacher * (weight_mse * t_scaling)).astype(BF)


def attend_rest_kernel(
    size, group, datt_ref, keep_ref, q_ref, kv_ref, probs_ref, gap_ref, dq_ref, dk_ref, dv_ref, sums_ref,
):
    own, pad = q_ref.shape
    per_group = probs_ref.shape[0]
    cols = slice(group * LANES, (group + 1) * LANES)
    v_cols = slice(pad + group * LANES, pad + (group + 1) * LANES)
    s_scaling = 1.0 / math.sqrt(size)
    lane = lax.broadcasted_iota(jnp.int32, (own, LANES), 1)
    query_all, grad_all = q_ref[:, cols].astype(F32), datt_ref[:, cols].astype(F32)
    product = grad_all * keep_ref[:, cols]
    masks = [(lane >= turn * size) & (lane < (turn + 1) * size) for turn in range(per_group)]
    dots = jnp.zeros((own, LANES), F32)
    for turn, mask in enumerate(masks):
        dots = jnp.where(lane == turn, jnp.sum(jnp.where(mask, product, 0.0), axis=-1, keepdims=True), dots)
    dots = dots.T
    keys, values = kv_ref[:, cols], kv_ref[:, v_cols]
    grads = [jnp.where(mask, grad_all, 0.0).astype(BF) for mask in masks]
    d_queries = jnp.zeros((own, LANES), F32)
    d_keys, d_values = jnp.zeros(keys.shape, F32), jnp.zeros(keys.shape, F32)
    later = mm_nt(values, grads[0])
    for turn, mask in enumerate(masks):
        d_probs = later
        later = mm_nt(values, grads[turn + 1]) if turn + 1 < per_group else None
        probs = probs_ref[turn]
        d_scores = (
            probs.astype(F32) * (d_probs - dots[turn:turn + 1]) + gap_ref[turn].astype(F32)
        ).astype(BF)
        d_keys += mm(d_scores, jnp.where(mask, query_all, 0.0).astype(BF))
        d_values += mm(probs, grads[turn])
        d_queries += jnp.where(mask, mm_tn(d_scores, keys), 0.0)
    d_keys, d_queries = d_keys * s_scaling, d_queries * s_scaling
    sums_ref[...] = jnp.zeros_like(sums_ref)
    sums_ref[0:1, :] = column_sum(d_queries)
    sums_ref[1:2, :] = column_sum(d_keys)
    sums_ref[2:3, :] = column_sum(d_values)
    dq_ref[...] = d_queries.astype(BF)
    dk_ref[...] = d_keys.astype(BF)
    dv_ref[...] = d_values.astype(BF)


def attend_weights_kernel(groups, me_ref, *refs):
    dq_refs, dk_refs, dv_refs, sum_refs = (refs[at * groups:(at + 1) * groups] for at in range(4))
    *row_refs, mine_ref, send_ref, g_scr, stage_ref, flip_scr = refs[4 * groups:]
    own = dq_refs[0].shape[0]
    width = row_refs[0].shape[1]
    pad = groups * LANES
    piece = row_refs[0].shape[0]
    for at, row_ref in enumerate(row_refs):
        flip_scr[:, at * piece:(at + 1) * piece] = row_ref[...].T
    g_scr[width:, :] = jnp.zeros((g_scr.shape[0] - width, g_scr.shape[1]), F32)
    for group in range(groups):
        for which, ref in enumerate((dq_refs[group], dk_refs[group], dv_refs[group])):
            there = slice(which * pad + group * LANES, which * pad + (group + 1) * LANES)
            g_scr[:width, there] = mm(flip_scr[:, :ref.shape[0]], ref[...])
            g_scr[width:width + 1, there] = sum_refs[group][which:which + 1, :]
    valid = width // groups
    parts = [g_scr[:, at * LANES:at * LANES + valid] for at in range(3 * groups)]
    stage_ref[...] = jnp.zeros_like(stage_ref)
    stage_ref[:, :3 * width] = jnp.concatenate(parts, axis=1)
    scatter_blocks(stage_ref, place(me_ref), mine_ref, send_ref)


def attend_rows_kernel(groups, wqkv_ref, dres_ref, *refs):
    dq_refs, dk_refs, dv_refs = (refs[at * groups:(at + 1) * groups] for at in range(3))
    far_ref, near_ref, own_ref = refs[3 * groups:]
    width = dres_ref.shape[1]
    pad = groups * LANES
    half = far_ref.shape[0]
    total = dres_ref[...]
    for group in range(groups):
        total = total + mm_nt(dq_refs[group][...], wqkv_ref[:, group * LANES:(group + 1) * LANES])
    own_ref[...] = total
    step = min(half, 512)
    for at in range(0, 2 * half, step):
        there = slice(at, at + step)
        back = jnp.zeros((step, width), F32)
        for group in range(groups):
            k_cols = slice(pad + group * LANES, pad + (group + 1) * LANES)
            v_cols = slice(2 * pad + group * LANES, 2 * pad + (group + 1) * LANES)
            back += mm_nt(dk_refs[group][there, :], wqkv_ref[:, k_cols])
            back += mm_nt(dv_refs[group][there, :], wqkv_ref[:, v_cols])
        out_ref, start = (near_ref, at) if at < half else (far_ref, at - half)
        out_ref[start:start + step, :] = back.astype(BF)


def stack_kernel(many, *refs):
    ins, (out,) = refs[:many], refs[many:]
    at = 0
    for turn, ref in enumerate(ins):
        if out.ndim > ref.ndim:
            out[turn] = ref[...]
        else:
            out[at:at + ref.shape[0]] = ref[...]
            at += ref.shape[0]


def copy_kernel(*refs):
    half = len(refs) // 2
    for source, target in zip(refs[:half], refs[half:]):
        target[...] = source[...]


def add_kernel(many, *refs):
    ins, outs = refs[:many], refs[many:]
    for at, out in enumerate(outs):
        if out.ndim == ins[0].ndim:
            size = out.shape[0]
            parts = [ref[at * size:(at + 1) * size] for ref in ins]
        else:
            parts = [ref[at] for ref in ins]
        out[...] = functools.reduce(jnp.add, [part.astype(F32) for part in parts]).astype(out.dtype)


def side_kernel(many, *refs):
    thin, rest = refs[:many], refs[many:]
    places = len(rest) // 2
    value = functools.reduce(jnp.add, [part[...].astype(F32) for part in thin]).astype(BF)
    planes, rows, lanes = value.shape
    for ref, out in zip(rest[:places], rest[places:]):
        for plane in range(planes):
            out[plane * rows:(plane + 1) * rows, :] = value[plane]
        height, width = ref.shape
        for turn, lane in enumerate(range(0, width, lanes)):
            at = slice(planes * rows + turn * height, planes * rows + (turn + 1) * height)
            part = ref[:, lane:lane + lanes]
            if part.shape[1] < lanes:
                out[at, :] = jnp.zeros((height, lanes), BF)
            out[at, :part.shape[1]] = part


def tail_kernel(planes, *refs):
    ins, (sum_ref,) = refs[:planes], refs[planes:]
    _, rows, lanes = sum_ref.shape
    for place in range(planes):
        parts = [ref[(place ^ key) * rows:((place ^ key) + 1) * rows, :].astype(F32) for key, ref in enumerate(ins)]
        sum_ref[place] = functools.reduce(jnp.add, parts).astype(BF)


def settle_kernel(planes, rows, me_ref, *refs):
    *ins, place_ref = refs
    lanes = ins[0].shape[1]
    height, width = place_ref.shape[1:]
    for key, ref in enumerate(ins):
        for turn, lane in enumerate(range(0, width, lanes)):
            at = planes * rows + turn * height
            many = min(lanes, width - lane)
            place_ref[jnp.bitwise_xor(me_ref[0], key), :, lane:lane + many] = ref[at:at + height, :many].astype(F32)


def collect(stage_ref, planes, me_ref, blocks):
    xy_at, z_at, c_at = place(me_ref)
    rows = stage_ref.shape[0] // 4
    each = stage_ref.shape[1] // (2 * planes)
    for core, ref in enumerate(blocks):
        for xy in range(4):
            for plane in range(planes):
                at = pl.ds(pl.multiple_of(jnp.bitwise_xor(xy, xy_at) * rows, 16), rows)
                lanes = jnp.bitwise_xor(core, c_at) * planes + jnp.bitwise_xor(plane, z_at)
                stage_ref[at, pl.ds(pl.multiple_of(lanes * each, LANES), each)] = ref[xy, plane]


def unpack_wide_kernel(layout, ff, width, t_width, planes, me_ref, *refs):
    blocks, (gout, gup, gdown, gproj, *vec_refs, mark_ref, wide_ref) = refs[:2], refs[2:]
    mark_ref[...] = jnp.zeros_like(mark_ref)
    at_up, at_down, at_proj, at_out = layout
    collect(wide_ref, planes, me_ref, blocks)
    gup[...] = wide_ref[:width, at_up:at_up + ff].astype(F32)
    gdown[...] = wide_ref[:width, at_down:at_down + ff].astype(F32)
    gproj[...] = wide_ref[:width, at_proj:at_proj + t_width].astype(F32)
    gout[...] = wide_ref[:width, at_out:at_out + width].astype(F32)
    rest = wide_ref[width:, :].astype(F32)
    for at in range(6):
        vec_refs[at][...] = rest[at:at + 1, at_out:at_out + width].reshape(width)
    vec_refs[6][...] = rest[:1, at_up:at_up + ff].reshape(ff)
    vec_refs[7][...] = rest[:1, at_proj:at_proj + t_width].reshape(t_width)


def unpack_thin_kernel(planes, me_ref, *refs):
    blocks, outs, thin_ref = refs[:2], refs[2:8], refs[8]
    width = outs[0].shape[0]
    collect(thin_ref, planes, me_ref, blocks)
    values = thin_ref[...].astype(F32)
    for at in range(3):
        lanes = slice(at * width, (at + 1) * width)
        outs[at][...] = values[:width, lanes]
        outs[3 + at][...] = values[width:width + 1, lanes].reshape(width)


def swap(value, axis, key):
    if isinstance(axis, tuple):
        size = math.prod(lax.axis_size(name) for name in axis)
    else:
        size = lax.axis_size(axis)
    turn = turn_of("swap")
    RESULTS[turn] = lax.ppermute(value, axis, [(at, at ^ key) for at in range(size)])
    return RESULTS[turn]


def swap_xy(value, key):
    return swap(value, ("batch", "p"), (key // 2) * lax.axis_size("p") + (key % 2) * 2)


def bits_of(size):
    return [1 << at for at in range(size.bit_length() - 1)]


def passed(value):
    turn = turn_of("passed")
    return value if RESULTS["tuned"] and turn in DIRECT else swap(value, "p", 1)


def stacked(parts, wait=(), joined=True, cost=0.1):
    rows = sum(part.shape[0] for part in parts)
    shape = (rows,) + parts[0].shape[1:] if joined else (len(parts),) + parts[0].shape
    return call(
        functools.partial(stack_kernel, len(parts)), [sds(shape, parts[0].dtype)], name="stack", cost=cost, wait=wait
    )(*parts)[0]


def spread_over_z(parts):
    return [parts[0]] + [swap(parts[key], "z", key) for key in range(1, len(parts))]


def plane_pieces(value):
    bits = list(reversed(bits_of(lax.axis_size("p"))))
    for bit in bits[:-2]:
        value = jnp.concatenate([value, swap(value, "p", bit)], axis=0)
    pieces = [value]
    for bit in bits[-2:]:
        pieces = pieces + [swap(piece, "p", bit) for piece in pieces]
    return pieces


def plane_both(value, across):
    bits = list(reversed(bits_of(lax.axis_size("p"))))
    pieces = [value, across]
    for bit in bits[1:]:
        pieces = pieces + [swap(piece, "p", bit) for piece in pieces]
    many = len(pieces) // 4
    return [jnp.concatenate(pieces[at * many:(at + 1) * many], axis=0) if many > 1 else pieces[at] for at in range(4)]


def gather_z(value, *done):
    return stacked([value] + [swap(value, "z", key) for key in range(1, lax.axis_size("z"))], wait=done)


def gather_plane(value):
    for bit in reversed(bits_of(lax.axis_size("p"))):
        value = jnp.concatenate([value, swap(value, "p", bit)], axis=0)
    return value


def copied(values, wait):
    return call(copy_kernel, [sds(value.shape, value.dtype) for value in values], name="copy", cost=0.1, wait=wait)(*values)


def add_cut(values, parts, dtype=BF, wait=()):
    rows = values[0].shape[0] // parts
    shape = values[0].shape[1:] if rows == 1 else (rows,) + values[0].shape[1:]
    return call(functools.partial(add_kernel, len(values)), [sds(shape, dtype)] * parts, name="add", cost=0.1, wait=wait)(*values)


def add_low(*values, wait=()):
    return add_cut(values, 1, wait=wait)[0]


def body(
    tokens_in, teacher_in, out_grad, mask_pos, slot_ids, w_query, b_query, w_key, b_key, w_value,
    b_value, w_out, b_out, ln1_gain, ln1_bias, w_up, b_up, w_down, b_down, ln2_gain, ln2_bias,
    w_proj, b_proj, t_query, t_key, t_value, t_out, t_up, t_down, embedding,
):
    planes, peers = lax.axis_size("z"), lax.axis_size("p")
    begin(peers == 4)
    z_at, p_at = lax.axis_index("z"), lax.axis_index("p")
    me = jnp.stack([z_at, p_at, lax.axis_index("batch")]).astype(jnp.int32)
    groups = planes * peers
    seq_count, per_device, width = tokens_in.shape
    t_width = teacher_in.shape[2]
    ff = w_up.shape[1]
    own = seq_count * per_device
    length = per_device * groups
    cap = mask_pos.shape[1] // groups
    slots = planes * cap
    size = width // HEADS
    per_group = max(n for n in range(1, LANES // size + 1) if HEADS % n == 0)
    pad = HEADS // per_group * LANES
    roomy = 16 + length // 256

    vectors = (b_out, ln1_gain, ln1_bias, b_down, ln2_gain, ln2_bias, b_up, b_proj, b_query, b_key, b_value)
    at_vec = [0]
    for vector in vectors:
        at_vec.append(at_vec[-1] - (-vector.shape[0] // LANES))
    vec_lines = -(-at_vec[-1] // 8) * 8
    down = w_down.T

    raws = (mask_pos, slot_ids, w_query, w_key, w_value, w_out) + vectors
    vec, live, want, line, wqkv, bqkv, wo = call(
        functools.partial(
            prepare_kernel, list(reversed(bits_of(peers))), cap, per_device, peers, embedding.shape[0], at_vec
        ),
        [
            sds((vec_lines, LANES), F32), sds((groups, 1, LANES), F32), sds((groups, 1, LANES), jnp.int32),
            sds((1, LANES), jnp.int32), sds((width, 3 * pad), BF), sds((1, 3 * pad), F32), sds((pad, width), BF),
        ],
        [pltpu.VMEM(raw.shape, raw.dtype) for raw in raws] + [pltpu.SemaphoreType.DMA((len(raws),))],
        name="prepare",
        cost=3,
        far=range(1, 1 + len(raws)),
    )(me, *raws)
    flipped = call(flip_kernel, [sds(embedding.shape[::-1], BF)], name="flip", cost=2)(embedding)[0]

    def packed(parts, wait=()):
        shape = sds((per_device, sum(part.shape[2] for part in parts)), BF)
        return call(
            functools.partial(pack_kernel, len(parts)),
            [shape] * planes,
            name="pack",
            cost=0.5,
            wait=wait,
        )(me, *parts)

    def unpacked(blocks, widths, wait=()):
        shapes = [sds((own, each), BF) for each in widths]
        return call(
            functools.partial(split_kernel, len(widths)), shapes, name="split", cost=0.2, wait=wait
        )(*blocks)

    blocks = spread_over_z(packed([teacher_in, tokens_in, out_grad]))
    t_rows, s_rows, og_rows = unpacked(blocks, [t_width, width, width], wait=[passed(line)])
    wide = t_width if length <= 2048 else 2 * LANES
    t_across = swap(t_rows, "p", bits_of(peers)[-1])
    if peers == 4:
        t_pieces = [t_rows, t_across, swap(t_rows, "p", 1), swap(t_across, "p", 1)]
    else:
        t_pieces = plane_both(t_rows, t_across)
    s_across = swap(copied([s_rows], [t_across])[0], "p", bits_of(peers)[-1])
    t_att, t_q, t_k, t_mark = call(
        teacher_attend_kernel,
        [sds((own, t_width), F32), sds((own, t_width), BF), sds((length, t_width), BF), sds((8, LANES), F32)],
        [pltpu.VMEM((length, wide), BF), pltpu.VMEM((length if wide == t_width else 16, t_width), BF)],
        limit=roomy,
        name="teacher_attend",
        cost=9,
    )(t_query, t_key, t_value, *t_pieces)
    t_output, t_pick = call(
        teacher_feed_kernel,
        [sds((own, t_width), F32), sds((slots, t_width), BF)],
        name="teacher_feed",
        cost=6,
    )(line, t_pieces[0], t_att, t_out, t_up, t_down)

    if peers == 4:
        near, far = copied([s_rows, s_across], [passed(t_mark)])
        s_pieces = [s_rows, s_across, swap(near, "p", 1), swap(far, "p", 1)]
    else:
        s_pieces = plane_both(s_rows, s_across)
    q, kv, keep, output, s_mark, *s_blocks = call(
        functools.partial(student_kernel, at_vec, planes),
        [
            sds((own, pad), BF), sds((length, 2 * pad), BF), sds((own, 3 * pad + LANES), F32),
            sds((own, width), BF), sds((8, LANES), F32),
        ] + [sds((slots + per_device, width), BF)] * planes,
        limit=roomy,
        name="student",
        cost=8,
        wait=[t_pick],
    )(line, vec, wqkv, bqkv, wo, w_up, down, *s_pieces)

    def placed(parts, dtype, wait=()):
        shape = sds((planes, per_device, width), dtype)
        return call(place_kernel, [shape], name="place", cost=0.1, wait=wait)(me, *parts)[0]

    t_parts = spread_over_z([t_pick] * planes)
    t_across = [swap(t_pick, "p", bits_of(peers)[-1])]
    t_parts = copied(t_parts, [passed(s_mark)])
    t_across += [swap(part, "p", bits_of(peers)[-1]) for part in t_parts[1:]]
    here = peers // 4 * planes * slots
    blocks = here // slots
    stat_shape = sds((blocks, 1, LANES), F32)
    logit_shapes = [sds((here, embedding.shape[0]), BF), stat_shape, stat_shape]
    def logits(at_bias, pieces, name, cost, wait=()):
        got = call(
            functools.partial(logits_kernel, at_bias, slots, 2), logit_shapes * 2, limit=20, name=name, cost=cost, wait=wait
        )(*pieces, flipped, *(() if at_bias is None else (w_proj, vec)))
        return [got[:3], got[3:]]

    def in_order(first, second):
        return zip(first[0], second[0], first[1], second[1])

    t_all = [stacked(t_parts)]
    if peers == 4:
        t_all += [None, swap(t_all[0], "p", 1), None]
    else:
        t_all = plane_both(t_all[0], stacked(t_across))
    s_parts = spread_over_z(s_blocks)
    t_first = logits(None, [t_all[0], t_all[2]], "t_logits", 4)
    s_all = [call(
        functools.partial(top_kernel, planes), [sds((planes * slots, width), BF)], name="top", cost=0.1,
        wait=[passed(t_first[0][1])],
    )(*s_parts)[0]]
    if peers == 4:
        s_across = swap(s_all[0], "p", 2)
        t_all[1] = stacked(t_across, wait=[s_all[0]])
        t_all[3] = swap(t_all[1], "p", 1)
        s_first = logits(at_vec[7], [s_all[0], swap(s_all[0], "p", 1)], "s_logits", 4)
        t_second = logits(None, [t_all[1], t_all[3]], "t_logits", 4, wait=[s_first[0][1]])
        far = copied([s_across], [passed(t_second[0][1])])[0]
        s_second = logits(at_vec[7], [s_across, swap(far, "p", 1)], "s_logits", 4)
        s_all = [s_all[0], s_across, swap(s_all[0], "p", 1), swap(far, "p", 1)]
    else:
        t_second = logits(None, [t_all[1], t_all[3]], "t_logits", 4)
        s_all = plane_pieces(s_all[0])
        s_first = logits(at_vec[7], [s_all[0], s_all[2]], "s_logits", 4)
        s_second = logits(at_vec[7], [s_all[1], s_all[3]], "s_logits", 4)
    s_raised, s_top, s_lse = in_order(s_first, s_second)
    t_raised, t_top, t_lse = in_order(t_first, t_second)
    stat = jnp.concatenate([jnp.concatenate(s_lse, axis=0), jnp.concatenate(t_lse, axis=0)], axis=1)
    stats = gather_plane(gather_z(stat[None]))
    sums = []
    crossing = []
    ready = []

    def make_ready(group, wait):
        if length <= 2048:
            shape = sds((per_group, length, own), BF)
            ready.append(call(
                functools.partial(attend_ready_kernel, 2.0 / (HEADS * length), size, group),
                [shape, shape],
                limit=20,
                name="attend_ready",
                cost=2,
                wait=wait,
            )(keep, q, kv, t_q, t_k))
        return [part[0] for part in ready]


    def combined(turn, wait):
        outs = [sds((here, width), BF), sds((width, t_width), F32), sds((1, t_width), F32)]
        back, *sums[:] = call(
            functools.partial(combine_kernel, turn * blocks, slots, bool(sums)),
            outs,
            [pltpu.VMEM((here, embedding.shape[0]), BF)],
            name="combine", cost=3, wait=wait,
        )(
            *sums, live, want, s_top[turn], t_top[turn], stats, s_raised[turn], t_raised[turn], s_all[turn], embedding, w_proj,
        )
        return back

    def reduced(turn, bits, wait=()):
        if not bits:
            return combined(turn, wait)
        bit = bits[-1]
        far = reduced(turn + len(s_all) // (2 * bit), bits[:-1], wait)
        near = reduced(turn, bits[:-1], [far])
        if len(bits) == 2:
            crossing.append(far)
            if peers == 4:
                return add_cut([near, swap(far, "p", bit)], planes)
        return add_low(near, swap(far, "p", bit))

    make_ready(0, [stat])
    wait = make_ready(1, [stat])
    back = reduced(0, bits_of(len(s_all)), wait)
    for group in range(2, pad // LANES):
        make_ready(group, [crossing[-1]])
    for bit in bits_of(peers)[2:]:
        half = back.shape[0] // 2
        back = add_low(back[:half], swap(back[half:], "p", bit))
    if peers > 4:
        back = add_cut([back], planes)
    again = call(
        functools.partial(feed_again_kernel, at_vec),
        [
            sds((own, width), BF), sds((own, ff), BF), sds((own, ff), F32), sds((own, width), F32),
            sds((width, t_width), F32), sds((1, t_width), F32),
        ],
        name="feed_again",
        cost=2,
        wait=[back[0]],
    )(vec, w_proj, w_up, og_rows, t_output, output, keep)
    ce = spread_over_z(back)

    lanes_of = lambda many: -(-many // LANES) * LANES
    at_up, at_down = 0, lanes_of(ff)
    at_proj = at_down + lanes_of(ff)
    at_out = at_proj + lanes_of(t_width)
    layout = (at_up, at_down, at_proj, at_out)
    unit = 2 * planes * LANES
    wide_lanes = -(-(at_out + lanes_of(width)) // unit) * unit
    thin_lanes = -(-3 * width // unit) * unit
    tall = -(-(width + 8) // 64) * 64
    wide_block = sds((4, planes, tall // 4, wide_lanes // (2 * planes)), BF)
    thin_block = sds((4, planes, tall // 4, thin_lanes // (2 * planes)), BF)
    d_att, d_res, wide_mine, wide_send = call(
        functools.partial(feed_back_kernel, layout, at_vec),
        [sds((own, pad), BF), sds((own, width), F32), wide_block, wide_block],
        [pltpu.VMEM((tall, wide_lanes), F32)],
        name="feed_back", cost=4,
    )(me, line, vec, *sums, *again, down, w_up, wo, keep, *ce)

    def attend_back(group, cost, *done):
        outs = [sds((own, LANES), BF), sds((length, LANES), BF), sds((length, LANES), BF), sds((8, LANES), F32)]
        if ready:
            return call(
                functools.partial(attend_rest_kernel, size, group), outs, limit=20, name="attend_back", cost=cost, wait=done
            )(d_att, keep, q, kv, *ready[group])
        return call(
            functools.partial(attend_back_kernel, 2.0 / (HEADS * length), size, group),
            outs,
            [pltpu.VMEM((own, LANES), F32)],
            limit=20,
            name="attend_back",
            cost=cost,
            wait=done,
        )(d_att, keep, q, kv, t_q, t_k)

    head_groups = pad // LANES
    wide_other = swap(wide_send, "p", 1)
    wide_parts = add_cut([wide_mine, wide_other], 4)
    wide_near = [swap_xy(wide_parts[key], key) for key in range(1, 4)]
    grads = [attend_back(0, 4)]
    for group in range(1, head_groups):
        grads.append(attend_back(group, 0.1, wide_parts[0], *grads[-1]))
    layer_out = call(
        functools.partial(bottom_kernel, slots), [sds((planes, per_device, width), BF)], name="bottom", cost=0.1
    )(me, *s_parts)[0]
    wide_line = add_cut([wide_parts[0]] + wide_near, planes, wait=[grads[-1][3]])
    kinds = [list(kind) for kind in zip(*grads)]
    thin_mine, thin_send = call(
        functools.partial(attend_weights_kernel, head_groups),
        [thin_block, thin_block],
        [
            pltpu.VMEM((tall, 3 * pad), F32), pltpu.VMEM((tall, thin_lanes), F32), pltpu.VMEM((width, length), BF),
        ],
        name="attend_weights",
        cost=0.1,
    )(me, *[part for kind in kinds for part in kind], *s_pieces)
    g_far, g_near, g_own = call(
        functools.partial(attend_rows_kernel, head_groups),
        [sds((length // 2, width), BF), sds((length // 2, width), BF), sds((own, width), F32)],
        name="attend_rows",
        cost=0.1,
        wait=[layer_out, wide_line[0], thin_mine],
    )(wqkv, d_res, *[part for kind in kinds[:3] for part in kind])

    thin_other, g_other = swap(thin_send, "p", 1), swap(g_far, "p", 1)
    wide_moved = spread_over_z(wide_line)
    thin_parts = add_cut([thin_mine, thin_other], 4, wait=[wide_moved[1]])
    thin_near = [swap_xy(thin_parts[key], key) for key in range(1, 4)]
    g_parts = add_cut([g_near, g_other], peers // 2)
    for bit in bits_of(peers)[1:-1]:
        half = len(g_parts) // 2
        moved = swap(jnp.concatenate(g_parts[half:], axis=0), "p", bit)
        g_parts = add_cut([jnp.concatenate(g_parts[:half], axis=0), moved], half)
    total = add_cut([g_own, g_parts[0], swap(g_parts[1], "p", bits_of(peers)[-1])], planes)

    def finished(value):
        for bit in bits_of(peers)[2:]:
            value = add_low(value, swap(value, "p", bit))
        return value

    wide_sum = finished(add_low(*wide_moved))
    thin_shape = (planes, tall // 4, thin_lanes // (2 * planes))
    side_rows = planes * tall // 4 + per_device * (lanes_of(width) // LANES)
    tails = call(
        functools.partial(side_kernel, 4), [sds((side_rows, LANES), BF)] * planes, name="side", cost=0.1, wait=[wide_sum]
    )(thin_parts[0], *thin_near, *total)
    wide_all = stacked(spread_over_z([wide_sum] * planes), joined=False)
    tails = spread_over_z(tails)
    thin_all = call(
        functools.partial(tail_kernel, planes), [sds(thin_shape, BF)], name="tail", cost=0.1, wait=[wide_all]
    )(*tails)[0]
    input_grad = call(
        functools.partial(settle_kernel, planes, tall // 4),
        [sds((planes, per_device, width), F32)],
        name="settle",
        cost=0.1,
    )(me, *tails)[0]
    thin_all = finished(thin_all)
    wide_far = [swap_xy(wide_all, key) for key in range(1, 4)]
    thin_far = [swap_xy(thin_all, key) for key in range(1, 4)]
    wide_all = stacked([wide_all] + wide_far, joined=False, wait=[thin_all])
    wide_all = [wide_all, swap(wide_all, "p", 1)]
    square = sds((width, width), F32)
    gout, gup, gdown, gproj, *vecs = call(
        functools.partial(unpack_wide_kernel, layout, ff, width, t_width, planes),
        [square, sds((width, ff), F32), sds((width, ff), F32), sds((width, t_width), F32)]
        + [sds(vector.shape, F32) for vector in vectors[:8]] + [sds((8, LANES), F32)],
        [pltpu.VMEM((tall, wide_lanes), BF)],
        limit=24,
        name="unpack_wide",
        cost=3,
    )(me, *wide_all)
    gbo, gg1, gc1, gbd, gg2, gc2, gbup, gbproj, wide_mark = vecs
    thin_all = stacked([thin_all] + thin_far, joined=False, wait=[passed(wide_mark)])
    thin_all = [thin_all, swap(thin_all, "p", 1)]
    gq, gk, gv, gbq, gbk, gbv = call(
        functools.partial(unpack_thin_kernel, planes),
        [square] * 3 + [sds((width,), F32)] * 3,
        [pltpu.VMEM((tall, thin_lanes), BF)],
        name="unpack_thin",
        cost=1,
    )(me, *thin_all)
    return (
        layer_out, input_grad, gq, gbq, gk, gbk, gv, gbv, gout, gbo, gg1, gc1, gup, gbup, gdown.T, gbd, gg2, gc2,
        gproj, gbproj,
    )


def solution(mesh):
    batch, seq = mesh.shape["batch"], mesh.shape["seq"]
    split = P("batch", ("z", "p"), None)
    in_specs = (split,) * 3 + (P("batch", None),) * 2 + (P(),) * 24 + (P(("z", "p"), None),)
    out_specs = (split,) * 2 + (P(),) * 18

    def run(*args):
        planes = args[0].shape[0] // batch
        fine = Mesh(mesh.devices.reshape(batch, planes, seq // planes), ("batch", "z", "p"))
        return jax.shard_map(body, mesh=fine, in_specs=in_specs, out_specs=out_specs, check_vma=False)(*args)

    return run
```

```python
import functools
import math

import jax
import jax.numpy as jnp
from jax import lax
from jax.experimental import pallas as pl
from jax.experimental.pallas import tpu as pltpu
from jax.sharding import Mesh
from jax.sharding import PartitionSpec as P

HEADS = 12
EPSILON = 1e-06
HID_WEIGHT = 0.05
CE_WEIGHT = 4.0
MIXING = 0.5
ROOT_HALF = 0.7071067811865476
ROOT_TWO_PI = 2.5066282746310002
LANES = 128
BF = jnp.bfloat16
F32 = jnp.float32
MIB = 1 << 20


def mm(left, right):
    return lax.dot_general(left, right, (((1,), (0,)), ((), ())), preferred_element_type=F32)


def mm_nt(left, right):
    return lax.dot_general(left, right, (((1,), (1,)), ((), ())), preferred_element_type=F32)


def mm_tn(left, right):
    return lax.dot_general(left, right, (((0,), (0,)), ((), ())), preferred_element_type=F32)


def normalize(values):
    centered = values - jnp.mean(values, axis=-1, keepdims=True)
    inverse = lax.rsqrt(jnp.mean(centered * centered, axis=-1, keepdims=True) + EPSILON)
    return centered * inverse, inverse


def norm_back(grads, scaled, inverse):
    return inverse * (
        grads
        - jnp.mean(grads, axis=-1, keepdims=True)
        - scaled * jnp.mean(grads * scaled, axis=-1, keepdims=True)
    )


def gelu(inputs):
    return inputs * (0.5 * (1.0 + lax.erf(inputs * ROOT_HALF)))


def column_sum(values):
    return jnp.sum(values.astype(F32), axis=0, keepdims=True)


def attend(at, q_ref, k_ref, v_ref, per_group, size, emit):
    rows = at.size if isinstance(at, pl.Slice) else at.stop - at.start
    heads = q_ref.shape[1] // LANES * per_group
    lane = lax.broadcasted_iota(jnp.int32, (rows, LANES), 1)
    scaling = math.log2(math.e) / math.sqrt(size)

    def scores_of(head):
        cols = slice(head // per_group * LANES, (head // per_group + 1) * LANES)
        low = head % per_group * size
        mask = (lane >= low) & (lane < low + size)
        query = jnp.where(mask, q_ref[at, cols].astype(F32), 0.0).astype(BF)
        return cols, mask, mm_nt(query, k_ref[:, cols])

    later = scores_of(0)
    for head in range(heads):
        cols, mask, scores = later
        later = scores_of(head + 1) if head + 1 < heads else None
        top = jnp.max(scores, axis=-1, keepdims=True) * scaling
        weights = jnp.exp2(scores * scaling - top)
        total = jnp.sum(weights, axis=-1, keepdims=True)
        mixed = mm(weights.astype(BF), v_ref[:, cols])
        emit(head, cols, mask, mixed * (1.0 / total), top + jnp.log2(total))


def over_rows(own, length, one):
    if length <= 2048:
        one(slice(0, own))
    else:
        step = 64

        def inside(turn, carry):
            one(pl.ds(pl.multiple_of(turn * step, step), step))
            return carry

        lax.fori_loop(0, own // step, inside, 0)


COSTS = {
    1: 0.05, 8: 4, 12: 7, 14: 2, 15: 12, 17: 0.5, 20: 4, 27: 1, 31: 12, 41: 7, 44: 7, 45: 0.1, 47: 12, 49: 7, 55: 1,
    58: 20, 60: 20, 63: 20, 65: 4, 67: 7, 69: 0.5, 71: 12, 75: 7, 77: 20, 81: 20, 83: 2, 84: 12, 85: 0.1, 86: 1,
    87: 12, 97: 2, 99: 12, 100: 1, 101: 12, 105: 4, 109: 1, 117: 20, 119: 1, 121: 20, 123: 20,
}
FREE = frozenset((
    8, 20, 41, 44, 61, 63, 64, 65, 69, 70, 75, 85, 87, 93, 97, 100, 101, 109,
))
DIRECT = frozenset((16, 46, 120))
AFTER = {
    12: (9,), 15: (5, 8, 11), 17: (8,), 27: (9, 22), 31: (13,), 36: (29,), 39: (33,), 44: (43,), 45: (26, 36),
    47: (33,), 49: (39,), 60: (51, 59), 63: (38, 45), 64: (48, 63), 69: (51,), 75: (69, 71), 77: (69,), 82: (71,),
    85: (79,), 93: (84, 85), 97: (93, 95), 99: (92,), 100: (93, 95), 101: (95,), 105: (82,), 109: (107,), 117: (99,),
    121: (99, 111),
}
RESULTS = []
TUNED = []


def begin(tuned):
    RESULTS.clear()
    TUNED.clear()
    TUNED.append(tuned)


def call(kernel, outs, scratch=(), limit=16, name=None, cost=1, far=(), wait=()):
    spaces = {"vmem": pltpu.VMEM, "smem": pltpu.SMEM, "far": pl.ANY}

    def space(at, arg):
        small = arg.ndim == 1 and arg.dtype == jnp.int32
        return pl.BlockSpec(memory_space=spaces["far" if at in far else "smem" if small else "vmem"])

    def run(*args):
        turn, price, later = len(RESULTS), cost, list(wait)
        if TUNED[0]:
            price = COSTS.get(turn, cost)
            later = [] if turn in FREE else later
            later += [RESULTS[at] for at in AFTER.get(turn, ())]
        count = len(args)

        def body_of(*refs):
            kernel(*refs[:count], *refs[count + len(later):])

        results = pl.pallas_call(
            body_of,
            out_shape=outs,
            in_specs=[space(at, arg) for at, arg in enumerate(args)] + [pl.BlockSpec(memory_space=pl.ANY)] * len(later),
            out_specs=[pl.BlockSpec(memory_space=pltpu.VMEM)] * len(outs),
            scratch_shapes=list(scratch),
            compiler_params=pltpu.CompilerParams(vmem_limit_bytes=limit * MIB),
            cost_estimate=pl.CostEstimate(
                flops=int(price * 1e9), bytes_accessed=int(price * 3e6), transcendentals=0
            ),
            name=name,
        )(*args, *later)
        RESULTS.append(results[0])
        return results

    return run


def sds(shape, dtype):
    return jax.ShapeDtypeStruct(shape, dtype)


def lines_of(ref, first, width):
    count = -(-width // LANES)
    return jnp.concatenate([ref[at:at + 1, :] for at in range(first, first + count)], axis=1)[:, :width]


def pack_kernel(many, me_ref, *refs):
    held, outs = refs[:many], refs[many:]
    for key, out in enumerate(outs):
        at = 0
        for ref in held:
            width = ref.shape[2]
            out[:, at:at + width] = ref[jnp.bitwise_xor(me_ref[0], key)]
            at += width


def split_kernel(many, *refs):
    ins, outs = refs[:-many], refs[-many:]
    rows = ins[0].shape[0]
    for turn, ref in enumerate(ins):
        at = 0
        for out in outs:
            width = out.shape[1]
            out[turn * rows:(turn + 1) * rows, :] = ref[:, at:at + width]
            at += width


def flip_kernel(table_ref, flip_ref):
    flip_ref[...] = table_ref[...].T


def prepare_kernel(order, cap, per_device, peers, vocab_rows, at_vec, me_ref, *refs):
    many_in = 6 + len(at_vec) - 1
    sources, outs, copied = refs[:many_in], refs[many_in:many_in + 7], refs[many_in + 7:-1]
    vec_ref, live_ref, want_ref, line_ref, wqkv_ref, bqkv_ref, wo_ref = outs
    copies = [pltpu.make_async_copy(*pair, refs[-1].at[at]) for at, pair in enumerate(zip(sources, copied))]
    for copy in copies:
        copy.start()
    for copy in copies:
        copy.wait()
    pos_ref, ids_ref, wq_ref, wk_ref, wv_ref, wout_ref, *vec_refs = copied
    vec_ref[...] = jnp.zeros_like(vec_ref)
    rows_of = [ref[...].astype(F32).reshape(1, ref.shape[0]) for ref in vec_refs]
    for first, value in zip(at_vec, rows_of):
        for at in range(0, value.shape[1], LANES):
            part = value[:, at:at + LANES]
            vec_ref[first + at // LANES:first + at // LANES + 1, :part.shape[1]] = part
    width = wq_ref.shape[0]
    pad = wo_ref.shape[0]
    valid = width * LANES // pad
    row = lax.broadcasted_iota(jnp.int32, (width, pad), 0)
    col = lax.broadcasted_iota(jnp.int32, (width, pad), 1)
    inside = lax.rem(col, LANES)
    select = jnp.where((inside < valid) & (row == lax.div(col, LANES) * valid + inside), 1.0, 0.0).astype(BF)
    for at, ref in enumerate((wq_ref, wk_ref, wv_ref)):
        wqkv_ref[:, at * pad:(at + 1) * pad] = mm(ref[...], select).astype(BF)
        bias = jnp.broadcast_to(rows_of[8 + at], (8, width)).astype(BF)
        bqkv_ref[:, at * pad:(at + 1) * pad] = mm(bias, select)[:1]
    wo_ref[...] = mm_tn(select, wout_ref[...]).astype(BF)

    planes, many = pos_ref.shape
    z_at, p_at = me_ref[0], me_ref[1]
    first = (z_at * peers + p_at) * vocab_rows
    lane = lax.broadcasted_iota(jnp.int32, (8, LANES), 1)

    def lines(ref, seq, peer):
        whole = jnp.broadcast_to(ref[pl.ds(seq, 1), :], (8, many))
        out = jnp.full((8, LANES), -1, jnp.int32)
        for plane in range(planes):
            shift = lax.rem(plane * cap - (plane * peers + peer) * cap + 2 * many, many)
            moved = pltpu.roll(whole, shift, 1)[:, :LANES]
            out = jnp.where((lane >= plane * cap) & (lane < (plane + 1) * cap), moved, out)
        return out

    own = lines(pos_ref, z_at, p_at)
    local = own
    for plane in range(planes):
        move = jnp.bitwise_xor(z_at, plane) * per_device - (plane * peers + p_at) * per_device
        local = jnp.where((lane >= plane * cap) & (lane < (plane + 1) * cap), own + move, local)
    line_ref[...] = jnp.where(own >= 0, local, -1)[:1]

    def one(turn, carry):
        key = jnp.int32(0)
        for bit, value in enumerate(order):
            key = jnp.where(lax.rem(lax.div(turn, 1 << bit), 2) == 1, jnp.bitwise_xor(key, value), key)
        for plane in range(planes):
            seq, peer = jnp.bitwise_xor(z_at, plane), jnp.bitwise_xor(p_at, key)
            live_ref[turn * planes + plane] = jnp.where(lines(pos_ref, seq, peer) >= 0, 1.0, 0.0)[:1]
            want_ref[turn * planes + plane] = (lines(ids_ref, seq, peer) - first)[:1]
        return carry

    lax.fori_loop(0, peers, one, 0)


def top_kernel(many, *refs):
    ins, (out,) = refs[:many], refs[many:]
    rows = out.shape[0] // many
    for turn, ref in enumerate(ins):
        out[turn * rows:(turn + 1) * rows, :] = ref[:rows, :]


def bottom_kernel(first, me_ref, *refs):
    *ins, out_ref = refs
    for key, ref in enumerate(ins):
        out_ref[jnp.bitwise_xor(me_ref[0], key)] = ref[first:, :]


def place_kernel(me_ref, *refs):
    *ins, out_ref = refs
    for key, ref in enumerate(ins):
        out_ref[jnp.bitwise_xor(me_ref[0], key)] = ref[...].astype(out_ref.dtype)


def pick(line_ref, slots, values):
    own = values.shape[0]
    at = lax.broadcasted_iota(jnp.int32, (own, LANES), 0)
    chosen = jnp.where(at == line_ref[...], 1.0, 0.0).astype(BF)
    return mm_tn(chosen, values)[:slots]


def teacher_attend_kernel(tq_ref, tk_ref, tv_ref, *refs):
    *row_refs, att_ref, q_ref, k_ref, mark_ref, v_scr, x_scr = refs
    mark_ref[...] = jnp.zeros_like(mark_ref)
    own = q_ref.shape[0]
    width = tq_ref.shape[1]
    size = width // HEADS
    per_group = LANES // size
    wide = v_scr.shape[1]
    q_ref[...] = mm(row_refs[0][:own], tq_ref[...]).astype(BF)
    for part in range(width // wide):
        cols = slice(part * wide, (part + 1) * wide)
        at = 0
        for row_ref in row_refs:
            there = slice(at, at + row_ref.shape[0])
            if x_scr.shape[0] == v_scr.shape[0]:
                x_scr[there, :] = row_ref[...]
            else:
                k_ref[there, cols] = mm(row_ref[...], tk_ref[:, cols]).astype(BF)
                v_scr[there, :] = mm(row_ref[...], tv_ref[:, cols]).astype(BF)
            at += row_ref.shape[0]
        if x_scr.shape[0] == v_scr.shape[0]:
            k_ref[:, cols] = mm(x_scr[...], tk_ref[:, cols]).astype(BF)
            v_scr[...] = mm(x_scr[...], tv_ref[:, cols]).astype(BF)
        out_ref = att_ref.at[:, cols]

        def one(at):
            def emit(head, there, mask, mixed, lse):
                out_ref[at, there] = mixed if head % per_group == 0 else jnp.where(mask, mixed, out_ref[at, there])

            attend(at, q_ref.at[:, cols], k_ref.at[:, cols], v_scr, per_group, size, emit)

        over_rows(own, v_scr.shape[0], one)


def teacher_feed_kernel(line_ref, rows_ref, att_ref, to_ref, up_ref, down_ref, out_ref, pick_ref):
    own, width = att_ref.shape
    branch = mm(att_ref[...].astype(BF), to_ref[...])
    hidden, _ = normalize(rows_ref[:own].astype(F32) + branch)
    low = hidden.astype(BF)
    step = width
    outer = jnp.zeros((own, width), F32)
    for at in range(0, up_ref.shape[1], step):
        inner = gelu(mm(low, up_ref[:, at:at + step])).astype(BF)
        outer = outer + mm(inner, down_ref[at:at + step])
    output, _ = normalize(hidden + outer)
    out_ref[...] = output
    pick_ref[...] = pick(line_ref, pick_ref.shape[0], output.astype(BF)).astype(BF)


def student_kernel(
    at_vec, planes, line_ref, vec_ref, wqkv_ref, bqkv_ref, wo_ref, up_ref, down_ref, *refs,
):
    *row_refs, q_ref, kv_ref, keep_ref, out_ref, mark_ref = refs[:-planes]
    block_refs = refs[-planes:]
    mark_ref[...] = jnp.zeros_like(mark_ref)
    own, pad = q_ref.shape
    length = kv_ref.shape[0]
    width = wo_ref.shape[1]
    ff = up_ref.shape[1]
    size = width // HEADS
    per_group = HEADS * LANES // pad
    rows = row_refs[0][:own]
    q_ref[...] = (mm(rows, wqkv_ref[:, :pad]) + bqkv_ref[:, :pad]).astype(BF)
    at = 0
    for row_ref in row_refs:
        there = slice(at, at + row_ref.shape[0])
        kv_ref[there, :] = (mm(row_ref[...], wqkv_ref[:, pad:]) + bqkv_ref[:, pad:]).astype(BF)
        at += row_ref.shape[0]
    k_ref, v_ref = kv_ref.at[:, :pad], kv_ref.at[:, pad:]
    keep_ref[:, pad:] = jnp.zeros((own, keep_ref.shape[1] - pad), F32)
    stat = slice(3 * pad, 3 * pad + LANES)

    def one(at):
        def emit(head, there, mask, mixed, lse):
            old = 0.0 if head % per_group == 0 else keep_ref[at, there]
            keep_ref[at, there] = jnp.where(mask, mixed, old)
            lane = lax.broadcasted_iota(jnp.int32, (lse.shape[0], LANES), 1)
            keep_ref[at, stat] = jnp.where(lane == head, lse, keep_ref[at, stat])

        attend(at, q_ref, k_ref, v_ref, per_group, size, emit)

    over_rows(own, length, one)
    bo, g1, c1, bdown, g2, c2 = (lines_of(vec_ref, at, width) for at in at_vec[:6])
    branch = mm(keep_ref[:, :pad].astype(BF), wo_ref[...]) + bo
    n1, i1 = normalize(rows.astype(F32) + branch)
    hidden = n1 * g1 + c1
    inner = mm(hidden.astype(BF), up_ref[...]) + lines_of(vec_ref, at_vec[6], ff)
    outer = mm_nt(gelu(inner).astype(BF), down_ref[...]) + bdown
    n2, i2 = normalize(hidden + outer)
    output = (n2 * g2 + c2).astype(BF)
    keep_ref[:, pad:pad + width] = n1
    keep_ref[:, 2 * pad:2 * pad + width] = n2
    at = lax.broadcasted_iota(jnp.int32, (own, LANES), 1)
    keep_ref[:, stat] = jnp.where(at == HEADS, i1, jnp.where(at == HEADS + 1, i2, keep_ref[:, stat]))
    out_ref[...] = output
    each = own // planes
    slots = block_refs[0].shape[0] - each
    picked = pick(line_ref, slots, output).astype(BF)
    for at, ref in enumerate(block_refs):
        ref[:slots] = picked
        ref[slots:] = output[at * each:(at + 1) * each]


def logits_kernel(at_bias, slots, many, *refs):
    pieces, flip_ref, refs = refs[:many], refs[many], refs[many + 1:]
    if at_bias is not None:
        (proj_ref, vec_ref), refs = refs[:2], refs[2:]
        bias = lines_of(vec_ref, at_bias, proj_ref.shape[1])
    rows = pieces[0].shape[0]
    block = 2 * slots
    lane = lax.broadcasted_iota(jnp.int32, (block, LANES), 1)

    def logits_of(piece, at):
        picked = pieces[piece][at, :]
        if at_bias is not None:
            picked = (mm(picked, proj_ref[...]) + bias).astype(BF)
        return mm(picked, flip_ref[...])

    def finish(logits, piece, at, first):
        raised_ref, top_ref, lse_ref = refs[3 * piece:3 * piece + 3]
        top = jnp.max(logits, axis=-1, keepdims=True)
        weights = jnp.exp(logits - top)
        total = top + jnp.log(jnp.sum(weights, axis=-1, keepdims=True))
        raised_ref[at, :] = weights.astype(BF)
        both = jnp.where(lane == 0, top, jnp.where(lane == 1, total, 0.0))
        for part in range(2):
            value = both[part * slots:(part + 1) * slots]
            if slots < LANES:
                value = jnp.concatenate([value, jnp.zeros((LANES - slots, LANES), F32)], axis=0)
            value = value.T
            top_ref[first + part] = value[0:1]
            lse_ref[first + part] = value[1:2]

    if rows // block <= 2:
        work = [(piece, at) for piece in range(many) for at in range(0, rows, block)]
        later = logits_of(work[0][0], slice(work[0][1], work[0][1] + block))
        for turn, (piece, at) in enumerate(work):
            logits = later
            if turn + 1 < len(work):
                after_piece, after_at = work[turn + 1]
                later = logits_of(after_piece, slice(after_at, after_at + block))
            finish(logits, piece, slice(at, at + block), at // slots)
    else:
        for piece in range(many):

            def one(turn, carry, piece=piece):
                at = pl.ds(pl.multiple_of(turn * block, block), block)
                finish(logits_of(piece, at), piece, at, 2 * turn)
                return carry

            lax.fori_loop(0, rows // block, one, 0)


def combine_kernel(first, slots, chained, *refs):
    if chained:
        gproj_in, gbproj_in, *refs = refs
    (
        live_ref, want_ref, s_top_ref, t_top_ref, all_ref, s_ref, t_ref, rows_ref, table_ref, proj_ref,
        back_ref, gproj_ref, gbproj_ref, low_scr,
    ) = refs
    blocks = s_top_ref.shape[0]
    sources = all_ref.shape[0]
    line = lax.broadcasted_iota(jnp.int32, (LANES, LANES), 0)
    column = lax.broadcasted_iota(jnp.int32, (slots, table_ref.shape[0]), 1)
    gbproj_ref[...] = gbproj_in[...] if chained else jnp.zeros_like(gbproj_ref)

    def share(block, which, top):
        known = [all_ref[key, jnp.bitwise_xor(block, key), which:which + 1, :] for key in range(sources)]
        peak = functools.reduce(jnp.maximum, known)
        total = functools.reduce(jnp.add, [jnp.exp(value - peak) for value in known])
        return jnp.exp(top - peak) / total

    def logit_grads(step):
        block = step + first
        at = pl.ds(pl.multiple_of(step * slots, slots), slots)
        live = CE_WEIGHT * live_ref[block]
        s_part = live * share(block, 0, s_top_ref[step])
        t_part = live * (MIXING * share(block, 1, t_top_ref[step]))
        lines = jnp.where(line == 0, s_part, jnp.where(line == 1, t_part, live * (1.0 - MIXING)))
        lines = jnp.where(line == 3, want_ref[block].astype(F32), lines)
        cols = lines.T[:slots]
        hot = jnp.where(column == cols[:, 3:4].astype(jnp.int32), cols[:, 2:3], 0.0)
        grads = cols[:, 0:1] * s_ref[at, :].astype(F32) - cols[:, 1:2] * t_ref[at, :].astype(F32) - hot
        return grads.astype(BF)

    def fill(turn):
        for step in (2 * turn, 2 * turn + 1):
            low_scr[pl.ds(pl.multiple_of(step * slots, slots), slots), :] = logit_grads(step)

    def use(turn):
        at = pl.ds(pl.multiple_of(2 * turn * slots, 2 * slots), 2 * slots)
        picked = mm(low_scr[at, :], table_ref[...])
        gbproj_ref[...] += column_sum(picked)
        picked = picked.astype(BF)
        back_ref[at, :] = mm_nt(picked, proj_ref[...]).astype(BF)
        gproj_ref[...] += mm_tn(rows_ref[at, :], picked)

    def one(turn, carry):
        fill(turn)
        use(turn)
        return carry

    gproj_ref[...] = gproj_in[...] if chained else jnp.zeros_like(gproj_ref)
    if blocks == 4:
        fill(0)
        fill(1)
        use(0)
        use(1)
    else:
        lax.fori_loop(0, blocks // 2, one, 0)


def place(me_ref):
    peer = me_ref[1]
    return me_ref[2] * 2 + lax.rem(lax.div(peer, 2), 2), me_ref[0], lax.rem(peer, 2)


def scatter_blocks(stage_ref, me, keep_ref, send_ref):
    xy_at, z_at, c_at = me
    planes = keep_ref.shape[1]
    rows, wide = keep_ref.shape[2:]
    half = planes * wide
    for xy in range(4):
        for plane in range(planes):
            at, lanes = xy * rows, plane * wide
            key = (jnp.bitwise_xor(xy, xy_at), jnp.bitwise_xor(plane, z_at))
            low = stage_ref[at:at + rows, lanes:lanes + wide]
            high = stage_ref[at:at + rows, half + lanes:half + lanes + wide]
            keep_ref[key] = jnp.where(c_at == 0, low, high).astype(BF)
            send_ref[key] = jnp.where(c_at == 0, high, low).astype(BF)


def feed_again_kernel(at_vec, vec_ref, proj_ref, up_ref, og_ref, tout_ref, out_ref, keep_ref, *refs):
    hid_ref, act_ref, slope_ref, dout_ref, gproj_ref, gbproj_ref = refs
    own, width = og_ref.shape
    pad = (keep_ref.shape[1] - LANES) // 3
    g1, c1 = (lines_of(vec_ref, at_vec[at], width) for at in (1, 2))
    hidden = (keep_ref[:, pad:pad + width] * g1 + c1).astype(BF)
    inner = mm(hidden, up_ref[...]) + lines_of(vec_ref, at_vec[6], up_ref.shape[1])
    cumulative = 0.5 * (1.0 + lax.erf(inner * ROOT_HALF))
    hid_ref[...] = hidden
    act_ref[...] = (inner * cumulative).astype(BF)
    slope_ref[...] = cumulative + inner * (jnp.exp(-0.5 * inner * inner) * (1.0 / ROOT_TWO_PI))
    output = out_ref[...]
    mapped = mm(output, proj_ref[...]) + lines_of(vec_ref, at_vec[7], proj_ref.shape[1])
    d_map = (2.0 * HID_WEIGHT * (mapped - tout_ref[...])).astype(BF)
    gproj_ref[...] = mm_tn(output, d_map)
    gbproj_ref[...] = column_sum(d_map)
    dout_ref[...] = og_ref[...].astype(F32) + mm_nt(d_map, proj_ref[...])


def feed_back_kernel(
    layout, at_vec, me_ref, line_ref, vec_ref, gproj_ref, gbproj_ref, hid_ref, act_ref, slope_ref, dout_ref,
    gproj_add, gbproj_add, down_ref, up_ref, wo_ref, keep_ref, *refs,
):
    *ce_refs, datt_ref, dres_ref, mine_ref, send_ref, stage_ref = refs
    own, width = dout_ref.shape
    pad = wo_ref.shape[0]
    at_up, at_down, at_proj, at_out = layout
    t_width = gproj_ref.shape[1]
    ff = up_ref.shape[1]
    at = lax.broadcasted_iota(jnp.int32, (own, LANES), 0)
    slots = ce_refs[0].shape[0]
    chosen = jnp.where(at == line_ref[...], 1.0, 0.0).astype(BF)[:, :slots]
    ce = functools.reduce(jnp.add, [ref[...].astype(F32) for ref in ce_refs])
    high = ce.astype(BF)
    rest = (ce - high.astype(F32)).astype(BF)
    d_out = dout_ref[...] + mm(chosen, high) + mm(chosen, rest)
    g1, g2 = (lines_of(vec_ref, at_vec[at], width) for at in (1, 4))
    n1, n2 = keep_ref[:, pad:pad + width], keep_ref[:, 2 * pad:2 * pad + width]
    stat = 3 * pad + HEADS
    i1, i2 = keep_ref[:, stat:stat + 1], keep_ref[:, stat + 1:stat + 2]
    stage_ref[width:, :] = jnp.zeros((stage_ref.shape[0] - width, stage_ref.shape[1]), F32)
    stage_ref[:width, at_proj:at_proj + t_width] = gproj_ref[...] + gproj_add[...]
    stage_ref[width:width + 1, at_proj:at_proj + t_width] = gbproj_ref[...] + gbproj_add[...]
    d_res2 = norm_back(d_out * g2, n2, i2)
    d_outer = d_res2.astype(BF)
    stage_ref[:width, at_down:at_down + ff] = mm_tn(d_outer, act_ref[...])
    d_inner = (mm(d_outer, down_ref[...]) * slope_ref[...]).astype(BF)
    stage_ref[:width, at_up:at_up + ff] = mm_tn(hid_ref[...], d_inner)
    stage_ref[width:width + 1, at_up:at_up + ff] = column_sum(d_inner)
    d_hid = d_res2 + mm_nt(d_inner, up_ref[...])
    d_res1 = norm_back(d_hid * g1, n1, i1)
    d_branch = d_res1.astype(BF)
    datt_ref[...] = mm_nt(d_branch, wo_ref[...]).astype(BF)
    dres_ref[...] = d_res1
    gout = mm_tn(keep_ref[:, :pad].astype(BF), d_branch)
    head_groups = pad // LANES
    valid = width // head_groups
    for group in range(head_groups):
        stage_ref[group * valid:(group + 1) * valid, at_out:at_out + width] = gout[group * LANES:group * LANES + valid]
    lines = [
        column_sum(d_branch),
        column_sum(d_hid * n1),
        column_sum(d_hid),
        column_sum(d_outer),
        column_sum(d_out * n2),
        column_sum(d_out),
    ]
    for at, value in enumerate(lines):
        stage_ref[width + at:width + at + 1, at_out:at_out + width] = value
    scatter_blocks(stage_ref, place(me_ref), mine_ref, send_ref)


def attend_back_kernel(
    weight_mse, size, group, datt_ref, keep_ref, q_ref, kv_ref, tq_ref, tk_ref,
    dq_ref, dk_ref, dv_ref, sums_ref, dq_scr,
):
    own, pad = q_ref.shape
    per_group = HEADS * LANES // pad
    t_size = tq_ref.shape[1] // HEADS
    t_group = LANES // t_size
    length = kv_ref.shape[0]
    chunk = length if length <= 2048 else 256
    cols = slice(group * LANES, (group + 1) * LANES)
    v_cols = slice(pad + group * LANES, pad + (group + 1) * LANES)
    s_scaling = 1.0 / math.sqrt(size)
    t_scaling = 1.0 / math.sqrt(t_size)
    lane = lax.broadcasted_iota(jnp.int32, (own, LANES), 1)
    query_all = q_ref[:, cols].astype(F32)
    grad_all = datt_ref[:, cols].astype(F32)
    product = grad_all * keep_ref[:, cols]
    lses = keep_ref[:, 3 * pad:].T
    dots = jnp.zeros((own, LANES), F32)
    heads = []
    for turn in range(per_group):
        head = group * per_group + turn
        mask = (lane >= turn * size) & (lane < (turn + 1) * size)
        dots = jnp.where(lane == turn, jnp.sum(jnp.where(mask, product, 0.0), axis=-1, keepdims=True), dots)
        t_cols = slice(head // t_group * LANES, (head // t_group + 1) * LANES)
        t_low = head % t_group * t_size
        t_mask = (lane >= t_low) & (lane < t_low + t_size)
        heads.append((
            mask,
            jnp.where(mask, query_all, 0.0).astype(BF),
            jnp.where(mask, grad_all, 0.0).astype(BF),
            t_cols,
            jnp.where(t_mask, tq_ref[:, t_cols].astype(F32), 0.0).astype(BF),
            lses[head:head + 1],
        ))
    dots = dots.T
    dq_scr[...] = jnp.zeros_like(dq_scr)
    sums_ref[...] = jnp.zeros_like(sums_ref)

    def one_chunk(at):
        keys, values = kv_ref[at, cols], kv_ref[at, v_cols]
        d_keys, d_values = jnp.zeros(keys.shape, F32), jnp.zeros(keys.shape, F32)

        def products(turn):
            _, query, grad, t_cols, t_query, _ = heads[turn]
            return mm_nt(keys, query), mm_nt(tk_ref[at, t_cols], t_query), mm_nt(values, grad)

        later = products(0)
        for turn, (mask, query, grad, _, _, lse) in enumerate(heads):
            scores, teacher, d_probs = later
            later = products(turn + 1) if turn + 1 < per_group else None
            probs = jnp.exp2(scores * (s_scaling * math.log2(math.e)) - lse)
            d_scores = (
                probs * (d_probs - dots[turn:turn + 1])
                + (scores * (weight_mse * s_scaling) - teacher * (weight_mse * t_scaling))
            ).astype(BF)
            d_keys += mm(d_scores, query)
            d_values += mm(probs.astype(BF), grad)
            dq_scr[...] += jnp.where(mask, mm_tn(d_scores, keys), 0.0)
        d_keys = d_keys * s_scaling
        sums_ref[1:2, :] += column_sum(d_keys)
        sums_ref[2:3, :] += column_sum(d_values)
        dk_ref[at, :] = d_keys.astype(BF)
        dv_ref[at, :] = d_values.astype(BF)

    if chunk == length:
        one_chunk(slice(0, length))
    else:

        def inside(turn, carry):
            one_chunk(pl.ds(pl.multiple_of(turn * chunk, chunk), chunk))
            return carry

        lax.fori_loop(0, length // chunk, inside, 0)
    d_queries = dq_scr[...] * s_scaling
    sums_ref[0:1, :] = column_sum(d_queries)
    dq_ref[...] = d_queries.astype(BF)


def attend_ready_kernel(weight_mse, size, group, keep_ref, q_ref, kv_ref, tq_ref, tk_ref, probs_ref, gap_ref):
    own, pad = q_ref.shape
    per_group = probs_ref.shape[0]
    t_size = tq_ref.shape[1] // HEADS
    t_group = LANES // t_size
    cols = slice(group * LANES, (group + 1) * LANES)
    s_scaling = 1.0 / math.sqrt(size)
    t_scaling = 1.0 / math.sqrt(t_size)
    lane = lax.broadcasted_iota(jnp.int32, (own, LANES), 1)
    lses = keep_ref[:, 3 * pad:].T

    def products(turn):
        head = group * per_group + turn
        mask = (lane >= turn * size) & (lane < (turn + 1) * size)
        query = jnp.where(mask, q_ref[:, cols].astype(F32), 0.0).astype(BF)
        t_cols = slice(head // t_group * LANES, (head // t_group + 1) * LANES)
        t_low = head % t_group * t_size
        t_mask = (lane >= t_low) & (lane < t_low + t_size)
        t_query = jnp.where(t_mask, tq_ref[:, t_cols].astype(F32), 0.0).astype(BF)
        return mm_nt(kv_ref[:, cols], query), mm_nt(tk_ref[:, t_cols], t_query)

    later = products(0)
    for turn in range(per_group):
        scores, teacher = later
        later = products(turn + 1) if turn + 1 < per_group else None
        lse = lses[group * per_group + turn:group * per_group + turn + 1]
        probs_ref[turn] = jnp.exp2(scores * (s_scaling * math.log2(math.e)) - lse).astype(BF)
        gap_ref[turn] = (scores * (weight_mse * s_scaling) - teacher * (weight_mse * t_scaling)).astype(BF)


def attend_rest_kernel(
    size, group, datt_ref, keep_ref, q_ref, kv_ref, probs_ref, gap_ref, dq_ref, dk_ref, dv_ref, sums_ref,
):
    own, pad = q_ref.shape
    per_group = probs_ref.shape[0]
    cols = slice(group * LANES, (group + 1) * LANES)
    v_cols = slice(pad + group * LANES, pad + (group + 1) * LANES)
    s_scaling = 1.0 / math.sqrt(size)
    lane = lax.broadcasted_iota(jnp.int32, (own, LANES), 1)
    query_all, grad_all = q_ref[:, cols].astype(F32), datt_ref[:, cols].astype(F32)
    product = grad_all * keep_ref[:, cols]
    masks = [(lane >= turn * size) & (lane < (turn + 1) * size) for turn in range(per_group)]
    dots = jnp.zeros((own, LANES), F32)
    for turn, mask in enumerate(masks):
        dots = jnp.where(lane == turn, jnp.sum(jnp.where(mask, product, 0.0), axis=-1, keepdims=True), dots)
    dots = dots.T
    keys, values = kv_ref[:, cols], kv_ref[:, v_cols]
    grads = [jnp.where(mask, grad_all, 0.0).astype(BF) for mask in masks]
    d_queries = jnp.zeros((own, LANES), F32)
    d_keys, d_values = jnp.zeros(keys.shape, F32), jnp.zeros(keys.shape, F32)
    later = mm_nt(values, grads[0])
    for turn, mask in enumerate(masks):
        d_probs = later
        later = mm_nt(values, grads[turn + 1]) if turn + 1 < per_group else None
        probs = probs_ref[turn]
        d_scores = (
            probs.astype(F32) * (d_probs - dots[turn:turn + 1]) + gap_ref[turn].astype(F32)
        ).astype(BF)
        d_keys += mm(d_scores, jnp.where(mask, query_all, 0.0).astype(BF))
        d_values += mm(probs, grads[turn])
        d_queries += jnp.where(mask, mm_tn(d_scores, keys), 0.0)
    d_keys, d_queries = d_keys * s_scaling, d_queries * s_scaling
    sums_ref[...] = jnp.zeros_like(sums_ref)
    sums_ref[0:1, :] = column_sum(d_queries)
    sums_ref[1:2, :] = column_sum(d_keys)
    sums_ref[2:3, :] = column_sum(d_values)
    dq_ref[...] = d_queries.astype(BF)
    dk_ref[...] = d_keys.astype(BF)
    dv_ref[...] = d_values.astype(BF)


def attend_weights_kernel(groups, me_ref, *refs):
    dq_refs, dk_refs, dv_refs, sum_refs = (refs[at * groups:(at + 1) * groups] for at in range(4))
    *row_refs, mine_ref, send_ref, g_scr, stage_ref, flip_scr = refs[4 * groups:]
    own = dq_refs[0].shape[0]
    width = row_refs[0].shape[1]
    pad = groups * LANES
    piece = row_refs[0].shape[0]
    for at, row_ref in enumerate(row_refs):
        flip_scr[:, at * piece:(at + 1) * piece] = row_ref[...].T
    g_scr[width:, :] = jnp.zeros((g_scr.shape[0] - width, g_scr.shape[1]), F32)
    for group in range(groups):
        for which, ref in enumerate((dq_refs[group], dk_refs[group], dv_refs[group])):
            there = slice(which * pad + group * LANES, which * pad + (group + 1) * LANES)
            g_scr[:width, there] = mm(flip_scr[:, :ref.shape[0]], ref[...])
            g_scr[width:width + 1, there] = sum_refs[group][which:which + 1, :]
    valid = width // groups
    parts = [g_scr[:, at * LANES:at * LANES + valid] for at in range(3 * groups)]
    stage_ref[...] = jnp.zeros_like(stage_ref)
    stage_ref[:, :3 * width] = jnp.concatenate(parts, axis=1)
    scatter_blocks(stage_ref, place(me_ref), mine_ref, send_ref)


def attend_rows_kernel(groups, wqkv_ref, dres_ref, *refs):
    dq_refs, dk_refs, dv_refs = (refs[at * groups:(at + 1) * groups] for at in range(3))
    far_ref, near_ref, own_ref = refs[3 * groups:]
    width = dres_ref.shape[1]
    pad = groups * LANES
    half = far_ref.shape[0]
    total = dres_ref[...]
    for group in range(groups):
        total = total + mm_nt(dq_refs[group][...], wqkv_ref[:, group * LANES:(group + 1) * LANES])
    own_ref[...] = total
    step = min(half, 512)
    for at in range(0, 2 * half, step):
        there = slice(at, at + step)
        back = jnp.zeros((step, width), F32)
        for group in range(groups):
            k_cols = slice(pad + group * LANES, pad + (group + 1) * LANES)
            v_cols = slice(2 * pad + group * LANES, 2 * pad + (group + 1) * LANES)
            back += mm_nt(dk_refs[group][there, :], wqkv_ref[:, k_cols])
            back += mm_nt(dv_refs[group][there, :], wqkv_ref[:, v_cols])
        out_ref, start = (near_ref, at) if at < half else (far_ref, at - half)
        out_ref[start:start + step, :] = back.astype(BF)


def stack_kernel(many, *refs):
    ins, (out,) = refs[:many], refs[many:]
    at = 0
    for turn, ref in enumerate(ins):
        if out.ndim > ref.ndim:
            out[turn] = ref[...]
        else:
            out[at:at + ref.shape[0]] = ref[...]
            at += ref.shape[0]


def copy_kernel(*refs):
    half = len(refs) // 2
    for source, target in zip(refs[:half], refs[half:]):
        target[...] = source[...]


def add_kernel(many, *refs):
    ins, outs = refs[:many], refs[many:]
    for at, out in enumerate(outs):
        if out.ndim == ins[0].ndim:
            size = out.shape[0]
            parts = [ref[at * size:(at + 1) * size] for ref in ins]
        else:
            parts = [ref[at] for ref in ins]
        out[...] = functools.reduce(jnp.add, [part.astype(F32) for part in parts]).astype(out.dtype)


def side_kernel(many, *refs):
    thin, rest = refs[:many], refs[many:]
    places = len(rest) // 2
    value = functools.reduce(jnp.add, [part[...].astype(F32) for part in thin]).astype(BF)
    planes, rows, lanes = value.shape
    for ref, out in zip(rest[:places], rest[places:]):
        for plane in range(planes):
            out[plane * rows:(plane + 1) * rows, :] = value[plane]
        height, width = ref.shape
        for turn, lane in enumerate(range(0, width, lanes)):
            at = slice(planes * rows + turn * height, planes * rows + (turn + 1) * height)
            part = ref[:, lane:lane + lanes]
            if part.shape[1] < lanes:
                out[at, :] = jnp.zeros((height, lanes), BF)
            out[at, :part.shape[1]] = part


def tail_kernel(planes, *refs):
    ins, (sum_ref,) = refs[:planes], refs[planes:]
    _, rows, lanes = sum_ref.shape
    for place in range(planes):
        parts = [ref[(place ^ key) * rows:((place ^ key) + 1) * rows, :].astype(F32) for key, ref in enumerate(ins)]
        sum_ref[place] = functools.reduce(jnp.add, parts).astype(BF)


def settle_kernel(planes, rows, me_ref, *refs):
    *ins, place_ref = refs
    lanes = ins[0].shape[1]
    height, width = place_ref.shape[1:]
    for key, ref in enumerate(ins):
        for turn, lane in enumerate(range(0, width, lanes)):
            at = planes * rows + turn * height
            many = min(lanes, width - lane)
            place_ref[jnp.bitwise_xor(me_ref[0], key), :, lane:lane + many] = ref[at:at + height, :many].astype(F32)


def collect(stage_ref, planes, me_ref, blocks):
    xy_at, z_at, c_at = place(me_ref)
    rows = stage_ref.shape[0] // 4
    each = stage_ref.shape[1] // (2 * planes)
    for core, ref in enumerate(blocks):
        for xy in range(4):
            for plane in range(planes):
                at = pl.ds(pl.multiple_of(jnp.bitwise_xor(xy, xy_at) * rows, 16), rows)
                lanes = jnp.bitwise_xor(core, c_at) * planes + jnp.bitwise_xor(plane, z_at)
                stage_ref[at, pl.ds(pl.multiple_of(lanes * each, LANES), each)] = ref[xy, plane]


def unpack_wide_kernel(layout, ff, width, t_width, planes, me_ref, *refs):
    blocks, (gout, gup, gdown, gproj, *vec_refs, mark_ref, wide_ref) = refs[:2], refs[2:]
    mark_ref[...] = jnp.zeros_like(mark_ref)
    at_up, at_down, at_proj, at_out = layout
    collect(wide_ref, planes, me_ref, blocks)
    gup[...] = wide_ref[:width, at_up:at_up + ff].astype(F32)
    gdown[...] = wide_ref[:width, at_down:at_down + ff].astype(F32)
    gproj[...] = wide_ref[:width, at_proj:at_proj + t_width].astype(F32)
    gout[...] = wide_ref[:width, at_out:at_out + width].astype(F32)
    rest = wide_ref[width:, :].astype(F32)
    for at in range(6):
        vec_refs[at][...] = rest[at:at + 1, at_out:at_out + width].reshape(width)
    vec_refs[6][...] = rest[:1, at_up:at_up + ff].reshape(ff)
    vec_refs[7][...] = rest[:1, at_proj:at_proj + t_width].reshape(t_width)


def unpack_thin_kernel(planes, me_ref, *refs):
    blocks, outs, thin_ref = refs[:2], refs[2:8], refs[8]
    width = outs[0].shape[0]
    collect(thin_ref, planes, me_ref, blocks)
    values = thin_ref[...].astype(F32)
    for at in range(3):
        lanes = slice(at * width, (at + 1) * width)
        outs[at][...] = values[:width, lanes]
        outs[3 + at][...] = values[width:width + 1, lanes].reshape(width)


def swap(value, axis, key):
    if isinstance(axis, tuple):
        size = math.prod(lax.axis_size(name) for name in axis)
    else:
        size = lax.axis_size(axis)
    RESULTS.append(lax.ppermute(value, axis, [(at, at ^ key) for at in range(size)]))
    return RESULTS[-1]


def swap_xy(value, key):
    return swap(value, ("batch", "p"), (key // 2) * lax.axis_size("p") + (key % 2) * 2)


def bits_of(size):
    return [1 << at for at in range(size.bit_length() - 1)]


def passed(value):
    turn = len(RESULTS)
    RESULTS.append(value)
    return value if TUNED[0] and turn in DIRECT else swap(value, "p", 1)


def stacked(parts, wait=(), joined=True, cost=0.1):
    rows = sum(part.shape[0] for part in parts)
    shape = (rows,) + parts[0].shape[1:] if joined else (len(parts),) + parts[0].shape
    return call(
        functools.partial(stack_kernel, len(parts)), [sds(shape, parts[0].dtype)], name="stack", cost=cost, wait=wait
    )(*parts)[0]


def spread_over_z(parts):
    return [parts[0]] + [swap(parts[key], "z", key) for key in range(1, len(parts))]


def plane_pieces(value):
    bits = list(reversed(bits_of(lax.axis_size("p"))))
    for bit in bits[:-2]:
        value = jnp.concatenate([value, swap(value, "p", bit)], axis=0)
    pieces = [value]
    for bit in bits[-2:]:
        pieces = pieces + [swap(piece, "p", bit) for piece in pieces]
    return pieces


def plane_both(value, across):
    bits = list(reversed(bits_of(lax.axis_size("p"))))
    pieces = [value, across]
    for bit in bits[1:]:
        pieces = pieces + [swap(piece, "p", bit) for piece in pieces]
    many = len(pieces) // 4
    return [jnp.concatenate(pieces[at * many:(at + 1) * many], axis=0) if many > 1 else pieces[at] for at in range(4)]


def gather_z(value, *done):
    return stacked([value] + [swap(value, "z", key) for key in range(1, lax.axis_size("z"))], wait=done)


def gather_plane(value):
    for bit in reversed(bits_of(lax.axis_size("p"))):
        value = jnp.concatenate([value, swap(value, "p", bit)], axis=0)
    return value


def copied(values, wait):
    return call(copy_kernel, [sds(value.shape, value.dtype) for value in values], name="copy", cost=0.1, wait=wait)(*values)


def add_cut(values, parts, dtype=BF, wait=()):
    rows = values[0].shape[0] // parts
    shape = values[0].shape[1:] if rows == 1 else (rows,) + values[0].shape[1:]
    return call(functools.partial(add_kernel, len(values)), [sds(shape, dtype)] * parts, name="add", cost=0.1, wait=wait)(*values)


def add_low(*values, wait=()):
    return add_cut(values, 1, wait=wait)[0]


def body(
    tokens_in, teacher_in, out_grad, mask_pos, slot_ids, w_query, b_query, w_key, b_key, w_value,
    b_value, w_out, b_out, ln1_gain, ln1_bias, w_up, b_up, w_down, b_down, ln2_gain, ln2_bias,
    w_proj, b_proj, t_query, t_key, t_value, t_out, t_up, t_down, embedding,
):
    planes, peers = lax.axis_size("z"), lax.axis_size("p")
    begin(peers == 4)
    z_at, p_at = lax.axis_index("z"), lax.axis_index("p")
    me = jnp.stack([z_at, p_at, lax.axis_index("batch")]).astype(jnp.int32)
    groups = planes * peers
    seq_count, per_device, width = tokens_in.shape
    t_width = teacher_in.shape[2]
    ff = w_up.shape[1]
    own = seq_count * per_device
    length = per_device * groups
    cap = mask_pos.shape[1] // groups
    slots = planes * cap
    size = width // HEADS
    per_group = max(n for n in range(1, LANES // size + 1) if HEADS % n == 0)
    pad = HEADS // per_group * LANES
    roomy = 16 + length // 256

    vectors = (b_out, ln1_gain, ln1_bias, b_down, ln2_gain, ln2_bias, b_up, b_proj, b_query, b_key, b_value)
    at_vec = [0]
    for vector in vectors:
        at_vec.append(at_vec[-1] - (-vector.shape[0] // LANES))
    vec_lines = -(-at_vec[-1] // 8) * 8
    down = w_down.T

    raws = (mask_pos, slot_ids, w_query, w_key, w_value, w_out) + vectors
    vec, live, want, line, wqkv, bqkv, wo = call(
        functools.partial(
            prepare_kernel, list(reversed(bits_of(peers))), cap, per_device, peers, embedding.shape[0], at_vec
        ),
        [
            sds((vec_lines, LANES), F32), sds((groups, 1, LANES), F32), sds((groups, 1, LANES), jnp.int32),
            sds((1, LANES), jnp.int32), sds((width, 3 * pad), BF), sds((1, 3 * pad), F32), sds((pad, width), BF),
        ],
        [pltpu.VMEM(raw.shape, raw.dtype) for raw in raws] + [pltpu.SemaphoreType.DMA((len(raws),))],
        name="prepare",
        cost=3,
        far=range(1, 1 + len(raws)),
    )(me, *raws)
    flipped = call(flip_kernel, [sds(embedding.shape[::-1], BF)], name="flip", cost=2)(embedding)[0]

    def packed(parts, wait=()):
        shape = sds((per_device, sum(part.shape[2] for part in parts)), BF)
        return call(
            functools.partial(pack_kernel, len(parts)),
            [shape] * planes,
            name="pack",
            cost=0.5,
            wait=wait,
        )(me, *parts)

    def unpacked(blocks, widths, wait=()):
        shapes = [sds((own, each), BF) for each in widths]
        return call(
            functools.partial(split_kernel, len(widths)), shapes, name="split", cost=0.2, wait=wait
        )(*blocks)

    blocks = spread_over_z(packed([teacher_in, tokens_in, out_grad]))
    t_rows, s_rows, og_rows = unpacked(blocks, [t_width, width, width], wait=[passed(line)])
    wide = t_width if length <= 2048 else 2 * LANES
    t_across = swap(t_rows, "p", bits_of(peers)[-1])
    if peers == 4:
        t_pieces = [t_rows, t_across, swap(t_rows, "p", 1), swap(t_across, "p", 1)]
    else:
        t_pieces = plane_both(t_rows, t_across)
    s_across = swap(copied([s_rows], [t_across])[0], "p", bits_of(peers)[-1])
    t_att, t_q, t_k, t_mark = call(
        teacher_attend_kernel,
        [sds((own, t_width), F32), sds((own, t_width), BF), sds((length, t_width), BF), sds((8, LANES), F32)],
        [pltpu.VMEM((length, wide), BF), pltpu.VMEM((length if wide == t_width else 16, t_width), BF)],
        limit=roomy,
        name="teacher_attend",
        cost=9,
    )(t_query, t_key, t_value, *t_pieces)
    t_output, t_pick = call(
        teacher_feed_kernel,
        [sds((own, t_width), F32), sds((slots, t_width), BF)],
        name="teacher_feed",
        cost=6,
    )(line, t_pieces[0], t_att, t_out, t_up, t_down)

    if peers == 4:
        near, far = copied([s_rows, s_across], [passed(t_mark)])
        s_pieces = [s_rows, s_across, swap(near, "p", 1), swap(far, "p", 1)]
    else:
        s_pieces = plane_both(s_rows, s_across)
    q, kv, keep, output, s_mark, *s_blocks = call(
        functools.partial(student_kernel, at_vec, planes),
        [
            sds((own, pad), BF), sds((length, 2 * pad), BF), sds((own, 3 * pad + LANES), F32),
            sds((own, width), BF), sds((8, LANES), F32),
        ] + [sds((slots + per_device, width), BF)] * planes,
        limit=roomy,
        name="student",
        cost=8,
        wait=[t_pick],
    )(line, vec, wqkv, bqkv, wo, w_up, down, *s_pieces)

    def placed(parts, dtype, wait=()):
        shape = sds((planes, per_device, width), dtype)
        return call(place_kernel, [shape], name="place", cost=0.1, wait=wait)(me, *parts)[0]

    t_parts = spread_over_z([t_pick] * planes)
    t_across = [swap(t_pick, "p", bits_of(peers)[-1])]
    t_parts = copied(t_parts, [passed(s_mark)])
    t_across += [swap(part, "p", bits_of(peers)[-1]) for part in t_parts[1:]]
    here = peers // 4 * planes * slots
    blocks = here // slots
    stat_shape = sds((blocks, 1, LANES), F32)
    logit_shapes = [sds((here, embedding.shape[0]), BF), stat_shape, stat_shape]
    def logits(at_bias, pieces, name, cost, wait=()):
        got = call(
            functools.partial(logits_kernel, at_bias, slots, 2), logit_shapes * 2, limit=20, name=name, cost=cost, wait=wait
        )(*pieces, flipped, *(() if at_bias is None else (w_proj, vec)))
        return [got[:3], got[3:]]

    def in_order(first, second):
        return zip(first[0], second[0], first[1], second[1])

    t_all = [stacked(t_parts)]
    if peers == 4:
        t_all += [None, swap(t_all[0], "p", 1), None]
    else:
        t_all = plane_both(t_all[0], stacked(t_across))
    s_parts = spread_over_z(s_blocks)
    t_first = logits(None, [t_all[0], t_all[2]], "t_logits", 4)
    s_all = [call(
        functools.partial(top_kernel, planes), [sds((planes * slots, width), BF)], name="top", cost=0.1,
        wait=[passed(t_first[0][1])],
    )(*s_parts)[0]]
    if peers == 4:
        s_across = swap(s_all[0], "p", 2)
        t_all[1] = stacked(t_across, wait=[s_all[0]])
        t_all[3] = swap(t_all[1], "p", 1)
        s_first = logits(at_vec[7], [s_all[0], swap(s_all[0], "p", 1)], "s_logits", 4)
        t_second = logits(None, [t_all[1], t_all[3]], "t_logits", 4, wait=[s_first[0][1]])
        far = copied([s_across], [passed(t_second[0][1])])[0]
        s_second = logits(at_vec[7], [s_across, swap(far, "p", 1)], "s_logits", 4)
        s_all = [s_all[0], s_across, swap(s_all[0], "p", 1), swap(far, "p", 1)]
    else:
        t_second = logits(None, [t_all[1], t_all[3]], "t_logits", 4)
        s_all = plane_pieces(s_all[0])
        s_first = logits(at_vec[7], [s_all[0], s_all[2]], "s_logits", 4)
        s_second = logits(at_vec[7], [s_all[1], s_all[3]], "s_logits", 4)
    s_raised, s_top, s_lse = in_order(s_first, s_second)
    t_raised, t_top, t_lse = in_order(t_first, t_second)
    stat = jnp.concatenate([jnp.concatenate(s_lse, axis=0), jnp.concatenate(t_lse, axis=0)], axis=1)
    stats = gather_plane(gather_z(stat[None]))
    sums = []
    crossing = []
    ready = []

    def make_ready(group, wait):
        if length <= 2048:
            shape = sds((per_group, length, own), BF)
            ready.append(call(
                functools.partial(attend_ready_kernel, 2.0 / (HEADS * length), size, group),
                [shape, shape],
                limit=20,
                name="attend_ready",
                cost=2,
                wait=wait,
            )(keep, q, kv, t_q, t_k))
        return [part[0] for part in ready]


    def combined(turn, wait):
        outs = [sds((here, width), BF), sds((width, t_width), F32), sds((1, t_width), F32)]
        back, *sums[:] = call(
            functools.partial(combine_kernel, turn * blocks, slots, bool(sums)),
            outs,
            [pltpu.VMEM((here, embedding.shape[0]), BF)],
            name="combine", cost=3, wait=wait,
        )(
            *sums, live, want, s_top[turn], t_top[turn], stats, s_raised[turn], t_raised[turn], s_all[turn], embedding, w_proj,
        )
        return back

    def reduced(turn, bits, wait=()):
        if not bits:
            return combined(turn, wait)
        bit = bits[-1]
        far = reduced(turn + len(s_all) // (2 * bit), bits[:-1], wait)
        near = reduced(turn, bits[:-1], [far])
        if len(bits) == 2:
            crossing.append(far)
            if peers == 4:
                return add_cut([near, swap(far, "p", bit)], planes)
        return add_low(near, swap(far, "p", bit))

    make_ready(0, [stat])
    wait = make_ready(1, [stat])
    back = reduced(0, bits_of(len(s_all)), wait)
    for group in range(2, pad // LANES):
        make_ready(group, [crossing[-1]])
    for bit in bits_of(peers)[2:]:
        half = back.shape[0] // 2
        back = add_low(back[:half], swap(back[half:], "p", bit))
    if peers > 4:
        back = add_cut([back], planes)
    again = call(
        functools.partial(feed_again_kernel, at_vec),
        [
            sds((own, width), BF), sds((own, ff), BF), sds((own, ff), F32), sds((own, width), F32),
            sds((width, t_width), F32), sds((1, t_width), F32),
        ],
        name="feed_again",
        cost=2,
        wait=[back[0]],
    )(vec, w_proj, w_up, og_rows, t_output, output, keep)
    ce = spread_over_z(back)

    lanes_of = lambda many: -(-many // LANES) * LANES
    at_up, at_down = 0, lanes_of(ff)
    at_proj = at_down + lanes_of(ff)
    at_out = at_proj + lanes_of(t_width)
    layout = (at_up, at_down, at_proj, at_out)
    unit = 2 * planes * LANES
    wide_lanes = -(-(at_out + lanes_of(width)) // unit) * unit
    thin_lanes = -(-3 * width // unit) * unit
    tall = -(-(width + 8) // 64) * 64
    wide_block = sds((4, planes, tall // 4, wide_lanes // (2 * planes)), BF)
    thin_block = sds((4, planes, tall // 4, thin_lanes // (2 * planes)), BF)
    d_att, d_res, wide_mine, wide_send = call(
        functools.partial(feed_back_kernel, layout, at_vec),
        [sds((own, pad), BF), sds((own, width), F32), wide_block, wide_block],
        [pltpu.VMEM((tall, wide_lanes), F32)],
        name="feed_back", cost=4,
    )(me, line, vec, *sums, *again, down, w_up, wo, keep, *ce)

    def attend_back(group, cost, *done):
        outs = [sds((own, LANES), BF), sds((length, LANES), BF), sds((length, LANES), BF), sds((8, LANES), F32)]
        if ready:
            return call(
                functools.partial(attend_rest_kernel, size, group), outs, limit=20, name="attend_back", cost=cost, wait=done
            )(d_att, keep, q, kv, *ready[group])
        return call(
            functools.partial(attend_back_kernel, 2.0 / (HEADS * length), size, group),
            outs,
            [pltpu.VMEM((own, LANES), F32)],
            limit=20,
            name="attend_back",
            cost=cost,
            wait=done,
        )(d_att, keep, q, kv, t_q, t_k)

    head_groups = pad // LANES
    wide_other = swap(wide_send, "p", 1)
    wide_parts = add_cut([wide_mine, wide_other], 4)
    wide_near = [swap_xy(wide_parts[key], key) for key in range(1, 4)]
    grads = [attend_back(0, 4)]
    for group in range(1, head_groups):
        grads.append(attend_back(group, 0.1, wide_parts[0], *grads[-1]))
    layer_out = call(
        functools.partial(bottom_kernel, slots), [sds((planes, per_device, width), BF)], name="bottom", cost=0.1
    )(me, *s_parts)[0]
    wide_line = add_cut([wide_parts[0]] + wide_near, planes, wait=[grads[-1][3]])
    kinds = [list(kind) for kind in zip(*grads)]
    thin_mine, thin_send = call(
        functools.partial(attend_weights_kernel, head_groups),
        [thin_block, thin_block],
        [
            pltpu.VMEM((tall, 3 * pad), F32), pltpu.VMEM((tall, thin_lanes), F32), pltpu.VMEM((width, length), BF),
        ],
        name="attend_weights",
        cost=0.1,
    )(me, *[part for kind in kinds for part in kind], *s_pieces)
    g_far, g_near, g_own = call(
        functools.partial(attend_rows_kernel, head_groups),
        [sds((length // 2, width), BF), sds((length // 2, width), BF), sds((own, width), F32)],
        name="attend_rows",
        cost=0.1,
        wait=[layer_out, wide_line[0], thin_mine],
    )(wqkv, d_res, *[part for kind in kinds[:3] for part in kind])

    thin_other, g_other = swap(thin_send, "p", 1), swap(g_far, "p", 1)
    wide_moved = spread_over_z(wide_line)
    thin_parts = add_cut([thin_mine, thin_other], 4, wait=[wide_moved[1]])
    thin_near = [swap_xy(thin_parts[key], key) for key in range(1, 4)]
    g_parts = add_cut([g_near, g_other], peers // 2)
    for bit in bits_of(peers)[1:-1]:
        half = len(g_parts) // 2
        moved = swap(jnp.concatenate(g_parts[half:], axis=0), "p", bit)
        g_parts = add_cut([jnp.concatenate(g_parts[:half], axis=0), moved], half)
    total = add_cut([g_own, g_parts[0], swap(g_parts[1], "p", bits_of(peers)[-1])], planes)

    def finished(value):
        for bit in bits_of(peers)[2:]:
            value = add_low(value, swap(value, "p", bit))
        return value

    wide_sum = finished(add_low(*wide_moved))
    thin_shape = (planes, tall // 4, thin_lanes // (2 * planes))
    side_rows = planes * tall // 4 + per_device * (lanes_of(width) // LANES)
    tails = call(
        functools.partial(side_kernel, 4), [sds((side_rows, LANES), BF)] * planes, name="side", cost=0.1, wait=[wide_sum]
    )(thin_parts[0], *thin_near, *total)
    wide_all = stacked(spread_over_z([wide_sum] * planes), joined=False)
    tails = spread_over_z(tails)
    thin_all = call(
        functools.partial(tail_kernel, planes), [sds(thin_shape, BF)], name="tail", cost=0.1, wait=[wide_all]
    )(*tails)[0]
    input_grad = call(
        functools.partial(settle_kernel, planes, tall // 4),
        [sds((planes, per_device, width), F32)],
        name="settle",
        cost=0.1,
    )(me, *tails)[0]
    thin_all = finished(thin_all)
    wide_far = [swap_xy(wide_all, key) for key in range(1, 4)]
    thin_far = [swap_xy(thin_all, key) for key in range(1, 4)]
    wide_all = stacked([wide_all] + wide_far, joined=False, wait=[thin_all])
    wide_all = [wide_all, swap(wide_all, "p", 1)]
    square = sds((width, width), F32)
    gout, gup, gdown, gproj, *vecs = call(
        functools.partial(unpack_wide_kernel, layout, ff, width, t_width, planes),
        [square, sds((width, ff), F32), sds((width, ff), F32), sds((width, t_width), F32)]
        + [sds(vector.shape, F32) for vector in vectors[:8]] + [sds((8, LANES), F32)],
        [pltpu.VMEM((tall, wide_lanes), BF)],
        limit=24,
        name="unpack_wide",
        cost=3,
    )(me, *wide_all)
    gbo, gg1, gc1, gbd, gg2, gc2, gbup, gbproj, wide_mark = vecs
    thin_all = stacked([thin_all] + thin_far, joined=False, wait=[passed(wide_mark)])
    thin_all = [thin_all, swap(thin_all, "p", 1)]
    gq, gk, gv, gbq, gbk, gbv = call(
        functools.partial(unpack_thin_kernel, planes),
        [square] * 3 + [sds((width,), F32)] * 3,
        [pltpu.VMEM((tall, thin_lanes), BF)],
        name="unpack_thin",
        cost=1,
    )(me, *thin_all)
    return (
        layer_out, input_grad, gq, gbq, gk, gbk, gv, gbv, gout, gbo, gg1, gc1, gup, gbup, gdown.T, gbd, gg2, gc2,
        gproj, gbproj,
    )


def solution(mesh):
    batch, seq = mesh.shape["batch"], mesh.shape["seq"]
    split = P("batch", ("z", "p"), None)
    in_specs = (split,) * 3 + (P("batch", None),) * 2 + (P(),) * 24 + (P(("z", "p"), None),)
    out_specs = (split,) * 2 + (P(),) * 18

    def run(*args):
        planes = args[0].shape[0] // batch
        fine = Mesh(mesh.devices.reshape(batch, planes, seq // planes), ("batch", "z", "p"))
        return jax.shard_map(body, mesh=fine, in_specs=in_specs, out_specs=out_specs, check_vma=False)(*args)

    return run
```

```python
import functools
import math

import jax
import jax.numpy as jnp
from jax import lax
from jax.experimental import pallas as pl
from jax.experimental.pallas import tpu as pltpu
from jax.sharding import Mesh
from jax.sharding import PartitionSpec as P

HEADS = 12
EPSILON = 1e-06
HID_WEIGHT = 0.05
CE_WEIGHT = 4.0
MIXING = 0.5
ROOT_HALF = 0.7071067811865476
ROOT_TWO_PI = 2.5066282746310002
LANES = 128
BF = jnp.bfloat16
F32 = jnp.float32
MIB = 1 << 20


def mm(left, right):
    return lax.dot_general(left, right, (((1,), (0,)), ((), ())), preferred_element_type=F32)


def mm_nt(left, right):
    return lax.dot_general(left, right, (((1,), (1,)), ((), ())), preferred_element_type=F32)


def mm_tn(left, right):
    return lax.dot_general(left, right, (((0,), (0,)), ((), ())), preferred_element_type=F32)


def normalize(values):
    centered = values - jnp.mean(values, axis=-1, keepdims=True)
    inverse = lax.rsqrt(jnp.mean(centered * centered, axis=-1, keepdims=True) + EPSILON)
    return centered * inverse, inverse


def norm_back(grads, scaled, inverse):
    return inverse * (
        grads
        - jnp.mean(grads, axis=-1, keepdims=True)
        - scaled * jnp.mean(grads * scaled, axis=-1, keepdims=True)
    )


def gelu(inputs):
    return inputs * (0.5 * (1.0 + lax.erf(inputs * ROOT_HALF)))


def column_sum(values):
    return jnp.sum(values.astype(F32), axis=0, keepdims=True)


def attend(at, q_ref, k_ref, v_ref, per_group, size, emit):
    rows = at.size if isinstance(at, pl.Slice) else at.stop - at.start
    heads = q_ref.shape[1] // LANES * per_group
    lane = lax.broadcasted_iota(jnp.int32, (rows, LANES), 1)
    scaling = math.log2(math.e) / math.sqrt(size)

    def scores_of(head):
        cols = slice(head // per_group * LANES, (head // per_group + 1) * LANES)
        low = head % per_group * size
        mask = (lane >= low) & (lane < low + size)
        query = jnp.where(mask, q_ref[at, cols].astype(F32), 0.0).astype(BF)
        return cols, mask, mm_nt(query, k_ref[:, cols])

    later = scores_of(0)
    for head in range(heads):
        cols, mask, scores = later
        later = scores_of(head + 1) if head + 1 < heads else None
        top = jnp.max(scores, axis=-1, keepdims=True) * scaling
        weights = jnp.exp2(scores * scaling - top)
        total = jnp.sum(weights, axis=-1, keepdims=True)
        mixed = mm(weights.astype(BF), v_ref[:, cols])
        emit(head, cols, mask, mixed * (1.0 / total), top + jnp.log2(total))


def over_rows(own, length, one):
    if length <= 2048:
        one(slice(0, own))
    else:
        step = 64

        def inside(turn, carry):
            one(pl.ds(pl.multiple_of(turn * step, step), step))
            return carry

        lax.fori_loop(0, own // step, inside, 0)


COSTS = {
    1: 1, 6: 4, 10: 0.05, 16: 7, 18: 2, 19: 12, 21: 0.5, 24: 4, 31: 1, 35: 12, 40: 7, 44: 7, 47: 7, 48: 0.1, 50: 12,
    52: 7, 58: 1, 61: 20, 63: 20, 66: 20, 68: 4, 70: 7, 72: 0.5, 73: 12, 74: 12, 78: 20, 80: 20, 84: 20, 86: 2,
    87: 12, 88: 20, 89: 20, 90: 12, 96: 0.05, 100: 2, 102: 0.5, 103: 1, 104: 12, 108: 0.05, 112: 1, 113: 4, 120: 20,
    122: 1, 124: 20, 126: 20,
}
FREE = frozenset((
    6, 10, 24, 44, 47, 64, 66, 67, 68, 72, 78, 88, 90, 96, 100, 103, 104, 112,
))
DIRECT = frozenset((20, 41, 49, 123))
AFTER = {
    6: (5,), 13: (1,), 16: (11,), 19: (5, 10, 15), 21: (10,), 31: (14, 26), 35: (17,), 40: (33,), 42: (37, 39),
    48: (30, 34), 50: (37,), 52: (42,), 63: (55, 62), 66: (43, 48), 67: (53, 66), 72: (55,), 73: (71,), 78: (72, 74),
    80: (72,), 88: (83,), 96: (87, 88), 100: (87, 96, 99), 102: (97,), 103: (96, 98, 99), 104: (82, 94, 95, 99),
    108: (85, 100), 120: (102,), 122: (119,), 124: (102, 115),
}
RESULTS = []
TUNED = []


def begin(tuned):
    RESULTS.clear()
    TUNED.clear()
    TUNED.append(tuned)


def call(kernel, outs, scratch=(), limit=16, name=None, cost=1, far=(), wait=()):
    spaces = {"vmem": pltpu.VMEM, "smem": pltpu.SMEM, "far": pl.ANY}

    def space(at, arg):
        small = arg.ndim == 1 and arg.dtype == jnp.int32
        return pl.BlockSpec(memory_space=spaces["far" if at in far else "smem" if small else "vmem"])

    def run(*args):
        turn, price, later = len(RESULTS), cost, list(wait)
        if TUNED[0]:
            price = COSTS.get(turn, cost)
            later = [] if turn in FREE else later
            later += [RESULTS[at] for at in AFTER.get(turn, ())]
        count = len(args)

        def body_of(*refs):
            kernel(*refs[:count], *refs[count + len(later):])

        results = pl.pallas_call(
            body_of,
            out_shape=outs,
            in_specs=[space(at, arg) for at, arg in enumerate(args)] + [pl.BlockSpec(memory_space=pl.ANY)] * len(later),
            out_specs=[pl.BlockSpec(memory_space=pltpu.VMEM)] * len(outs),
            scratch_shapes=list(scratch),
            compiler_params=pltpu.CompilerParams(vmem_limit_bytes=limit * MIB),
            cost_estimate=pl.CostEstimate(
                flops=int(price * 1e9), bytes_accessed=int(price * 3e6), transcendentals=0
            ),
            name=name,
        )(*args, *later)
        RESULTS.append(results[0])
        return results

    return run


def sds(shape, dtype):
    return jax.ShapeDtypeStruct(shape, dtype)


def lines_of(ref, first, width):
    count = -(-width // LANES)
    return jnp.concatenate([ref[at:at + 1, :] for at in range(first, first + count)], axis=1)[:, :width]


def pack_kernel(many, me_ref, *refs):
    held, outs = refs[:many], refs[many:]
    for key, out in enumerate(outs):
        at = 0
        for ref in held:
            width = ref.shape[2]
            out[:, at:at + width] = ref[jnp.bitwise_xor(me_ref[0], key)]
            at += width


def split_kernel(many, *refs):
    ins, outs = refs[:-many], refs[-many:]
    rows = ins[0].shape[0]
    for turn, ref in enumerate(ins):
        at = 0
        for out in outs:
            width = out.shape[1]
            out[turn * rows:(turn + 1) * rows, :] = ref[:, at:at + width]
            at += width


def head_kernel(rows_ref, out_ref):
    out_ref[...] = rows_ref[:, :out_ref.shape[1]]


def bottom_rows_kernel(rows_ref, out_ref):
    out_ref[...] = rows_ref[rows_ref.shape[0] - out_ref.shape[0]:, :]


def flip_kernel(table_ref, flip_ref):
    flip_ref[...] = table_ref[...].T


def prepare_kernel(order, cap, per_device, peers, vocab_rows, at_vec, me_ref, *refs):
    many_in = 6 + len(at_vec) - 1
    sources, outs, copied = refs[:many_in], refs[many_in:many_in + 7], refs[many_in + 7:-1]
    vec_ref, live_ref, want_ref, line_ref, wqkv_ref, bqkv_ref, wo_ref = outs
    copies = [pltpu.make_async_copy(*pair, refs[-1].at[at]) for at, pair in enumerate(zip(sources, copied))]
    for copy in copies:
        copy.start()
    for copy in copies:
        copy.wait()
    pos_ref, ids_ref, wq_ref, wk_ref, wv_ref, wout_ref, *vec_refs = copied
    vec_ref[...] = jnp.zeros_like(vec_ref)
    rows_of = [ref[...].astype(F32).reshape(1, ref.shape[0]) for ref in vec_refs]
    for first, value in zip(at_vec, rows_of):
        for at in range(0, value.shape[1], LANES):
            part = value[:, at:at + LANES]
            vec_ref[first + at // LANES:first + at // LANES + 1, :part.shape[1]] = part
    width = wq_ref.shape[0]
    pad = wo_ref.shape[0]
    valid = width * LANES // pad
    row = lax.broadcasted_iota(jnp.int32, (width, pad), 0)
    col = lax.broadcasted_iota(jnp.int32, (width, pad), 1)
    inside = lax.rem(col, LANES)
    select = jnp.where((inside < valid) & (row == lax.div(col, LANES) * valid + inside), 1.0, 0.0).astype(BF)
    for at, ref in enumerate((wq_ref, wk_ref, wv_ref)):
        wqkv_ref[:, at * pad:(at + 1) * pad] = mm(ref[...], select).astype(BF)
        bias = jnp.broadcast_to(rows_of[8 + at], (8, width)).astype(BF)
        bqkv_ref[:, at * pad:(at + 1) * pad] = mm(bias, select)[:1]
    wo_ref[...] = mm_tn(select, wout_ref[...]).astype(BF)

    planes, many = pos_ref.shape
    z_at, p_at = me_ref[0], me_ref[1]
    first = (z_at * peers + p_at) * vocab_rows
    lane = lax.broadcasted_iota(jnp.int32, (8, LANES), 1)

    def lines(ref, seq, peer):
        whole = jnp.broadcast_to(ref[pl.ds(seq, 1), :], (8, many))
        out = jnp.full((8, LANES), -1, jnp.int32)
        for plane in range(planes):
            shift = lax.rem(plane * cap - (plane * peers + peer) * cap + 2 * many, many)
            moved = pltpu.roll(whole, shift, 1)[:, :LANES]
            out = jnp.where((lane >= plane * cap) & (lane < (plane + 1) * cap), moved, out)
        return out

    own = lines(pos_ref, z_at, p_at)
    local = own
    for plane in range(planes):
        move = jnp.bitwise_xor(z_at, plane) * per_device - (plane * peers + p_at) * per_device
        local = jnp.where((lane >= plane * cap) & (lane < (plane + 1) * cap), own + move, local)
    line_ref[...] = jnp.where(own >= 0, local, -1)[:1]

    def one(turn, carry):
        key = jnp.int32(0)
        for bit, value in enumerate(order):
            key = jnp.where(lax.rem(lax.div(turn, 1 << bit), 2) == 1, jnp.bitwise_xor(key, value), key)
        for plane in range(planes):
            seq, peer = jnp.bitwise_xor(z_at, plane), jnp.bitwise_xor(p_at, key)
            live_ref[turn * planes + plane] = jnp.where(lines(pos_ref, seq, peer) >= 0, 1.0, 0.0)[:1]
            want_ref[turn * planes + plane] = (lines(ids_ref, seq, peer) - first)[:1]
        return carry

    lax.fori_loop(0, peers, one, 0)


def top_kernel(many, *refs):
    ins, (out,) = refs[:many], refs[many:]
    rows = out.shape[0] // many
    for turn, ref in enumerate(ins):
        out[turn * rows:(turn + 1) * rows, :] = ref[:rows, :]


def bottom_kernel(first, me_ref, *refs):
    *ins, out_ref = refs
    for key, ref in enumerate(ins):
        out_ref[jnp.bitwise_xor(me_ref[0], key)] = ref[first:, :]


def place_kernel(me_ref, *refs):
    *ins, out_ref = refs
    for key, ref in enumerate(ins):
        out_ref[jnp.bitwise_xor(me_ref[0], key)] = ref[...].astype(out_ref.dtype)


def pick(line_ref, slots, values):
    own = values.shape[0]
    at = lax.broadcasted_iota(jnp.int32, (own, LANES), 0)
    chosen = jnp.where(at == line_ref[...], 1.0, 0.0).astype(BF)
    return mm_tn(chosen, values)[:slots]


def teacher_attend_kernel(tq_ref, tk_ref, tv_ref, *refs):
    *row_refs, att_ref, q_ref, k_ref, mark_ref, v_scr, x_scr = refs
    mark_ref[...] = jnp.zeros_like(mark_ref)
    own = q_ref.shape[0]
    width = tq_ref.shape[1]
    size = width // HEADS
    per_group = LANES // size
    wide = v_scr.shape[1]
    q_ref[...] = mm(row_refs[0][:own], tq_ref[...]).astype(BF)
    for part in range(width // wide):
        cols = slice(part * wide, (part + 1) * wide)
        at = 0
        for row_ref in row_refs:
            there = slice(at, at + row_ref.shape[0])
            if x_scr.shape[0] == v_scr.shape[0]:
                x_scr[there, :] = row_ref[...]
            else:
                k_ref[there, cols] = mm(row_ref[...], tk_ref[:, cols]).astype(BF)
                v_scr[there, :] = mm(row_ref[...], tv_ref[:, cols]).astype(BF)
            at += row_ref.shape[0]
        if x_scr.shape[0] == v_scr.shape[0]:
            k_ref[:, cols] = mm(x_scr[...], tk_ref[:, cols]).astype(BF)
            v_scr[...] = mm(x_scr[...], tv_ref[:, cols]).astype(BF)
        out_ref = att_ref.at[:, cols]

        def one(at):
            def emit(head, there, mask, mixed, lse):
                out_ref[at, there] = mixed if head % per_group == 0 else jnp.where(mask, mixed, out_ref[at, there])

            attend(at, q_ref.at[:, cols], k_ref.at[:, cols], v_scr, per_group, size, emit)

        over_rows(own, v_scr.shape[0], one)


def teacher_feed_kernel(line_ref, rows_ref, att_ref, to_ref, up_ref, down_ref, out_ref, pick_ref):
    own, width = att_ref.shape
    branch = mm(att_ref[...].astype(BF), to_ref[...])
    hidden, _ = normalize(rows_ref[:own].astype(F32) + branch)
    low = hidden.astype(BF)
    step = width
    outer = jnp.zeros((own, width), F32)
    for at in range(0, up_ref.shape[1], step):
        inner = gelu(mm(low, up_ref[:, at:at + step])).astype(BF)
        outer = outer + mm(inner, down_ref[at:at + step])
    output, _ = normalize(hidden + outer)
    out_ref[...] = output
    pick_ref[...] = pick(line_ref, pick_ref.shape[0], output.astype(BF)).astype(BF)


def student_kernel(
    at_vec, planes, line_ref, vec_ref, wqkv_ref, bqkv_ref, wo_ref, up_ref, down_ref, *refs,
):
    *row_refs, q_ref, kv_ref, keep_ref, out_ref, mark_ref = refs[:-planes]
    block_refs = refs[-planes:]
    mark_ref[...] = jnp.zeros_like(mark_ref)
    own, pad = q_ref.shape
    length = kv_ref.shape[0]
    width = wo_ref.shape[1]
    ff = up_ref.shape[1]
    size = width // HEADS
    per_group = HEADS * LANES // pad
    rows = row_refs[0][:own]
    q_ref[...] = (mm(rows, wqkv_ref[:, :pad]) + bqkv_ref[:, :pad]).astype(BF)
    at = 0
    for row_ref in row_refs:
        there = slice(at, at + row_ref.shape[0])
        kv_ref[there, :] = (mm(row_ref[...], wqkv_ref[:, pad:]) + bqkv_ref[:, pad:]).astype(BF)
        at += row_ref.shape[0]
    k_ref, v_ref = kv_ref.at[:, :pad], kv_ref.at[:, pad:]
    keep_ref[:, pad:] = jnp.zeros((own, keep_ref.shape[1] - pad), F32)
    stat = slice(3 * pad, 3 * pad + LANES)

    def one(at):
        def emit(head, there, mask, mixed, lse):
            old = 0.0 if head % per_group == 0 else keep_ref[at, there]
            keep_ref[at, there] = jnp.where(mask, mixed, old)
            lane = lax.broadcasted_iota(jnp.int32, (lse.shape[0], LANES), 1)
            keep_ref[at, stat] = jnp.where(lane == head, lse, keep_ref[at, stat])

        attend(at, q_ref, k_ref, v_ref, per_group, size, emit)

    over_rows(own, length, one)
    bo, g1, c1, bdown, g2, c2 = (lines_of(vec_ref, at, width) for at in at_vec[:6])
    branch = mm(keep_ref[:, :pad].astype(BF), wo_ref[...]) + bo
    n1, i1 = normalize(rows.astype(F32) + branch)
    hidden = n1 * g1 + c1
    inner = mm(hidden.astype(BF), up_ref[...]) + lines_of(vec_ref, at_vec[6], ff)
    outer = mm_nt(gelu(inner).astype(BF), down_ref[...]) + bdown
    n2, i2 = normalize(hidden + outer)
    output = (n2 * g2 + c2).astype(BF)
    keep_ref[:, pad:pad + width] = n1
    keep_ref[:, 2 * pad:2 * pad + width] = n2
    at = lax.broadcasted_iota(jnp.int32, (own, LANES), 1)
    keep_ref[:, stat] = jnp.where(at == HEADS, i1, jnp.where(at == HEADS + 1, i2, keep_ref[:, stat]))
    out_ref[...] = output
    each = own // planes
    slots = block_refs[0].shape[0] - each
    picked = pick(line_ref, slots, output).astype(BF)
    for at, ref in enumerate(block_refs):
        ref[:slots] = picked
        ref[slots:] = output[at * each:(at + 1) * each]


def logits_kernel(at_bias, slots, many, *refs):
    pieces, flip_ref, refs = refs[:many], refs[many], refs[many + 1:]
    if at_bias is not None:
        (proj_ref, vec_ref), refs = refs[:2], refs[2:]
        bias = lines_of(vec_ref, at_bias, proj_ref.shape[1])
    rows = pieces[0].shape[0]
    block = 2 * slots
    lane = lax.broadcasted_iota(jnp.int32, (block, LANES), 1)

    def logits_of(piece, at):
        picked = pieces[piece][at, :]
        if at_bias is not None:
            picked = (mm(picked, proj_ref[...]) + bias).astype(BF)
        return mm(picked, flip_ref[...])

    def finish(logits, piece, at, first):
        raised_ref, top_ref, lse_ref = refs[3 * piece:3 * piece + 3]
        top = jnp.max(logits, axis=-1, keepdims=True)
        weights = jnp.exp(logits - top)
        total = top + jnp.log(jnp.sum(weights, axis=-1, keepdims=True))
        raised_ref[at, :] = weights.astype(BF)
        both = jnp.where(lane == 0, top, jnp.where(lane == 1, total, 0.0))
        for part in range(2):
            value = both[part * slots:(part + 1) * slots]
            if slots < LANES:
                value = jnp.concatenate([value, jnp.zeros((LANES - slots, LANES), F32)], axis=0)
            value = value.T
            top_ref[first + part] = value[0:1]
            lse_ref[first + part] = value[1:2]

    if rows // block <= 2:
        work = [(piece, at) for piece in range(many) for at in range(0, rows, block)]
        later = logits_of(work[0][0], slice(work[0][1], work[0][1] + block))
        for turn, (piece, at) in enumerate(work):
            logits = later
            if turn + 1 < len(work):
                after_piece, after_at = work[turn + 1]
                later = logits_of(after_piece, slice(after_at, after_at + block))
            finish(logits, piece, slice(at, at + block), at // slots)
    else:
        for piece in range(many):

            def one(turn, carry, piece=piece):
                at = pl.ds(pl.multiple_of(turn * block, block), block)
                finish(logits_of(piece, at), piece, at, 2 * turn)
                return carry

            lax.fori_loop(0, rows // block, one, 0)


def combine_kernel(first, slots, chained, *refs):
    if chained:
        gproj_in, gbproj_in, *refs = refs
    (
        live_ref, want_ref, s_top_ref, t_top_ref, all_ref, s_ref, t_ref, rows_ref, table_ref, proj_ref,
        back_ref, gproj_ref, gbproj_ref, low_scr,
    ) = refs
    blocks = s_top_ref.shape[0]
    sources = all_ref.shape[0]
    line = lax.broadcasted_iota(jnp.int32, (LANES, LANES), 0)
    column = lax.broadcasted_iota(jnp.int32, (slots, table_ref.shape[0]), 1)
    gbproj_ref[...] = gbproj_in[...] if chained else jnp.zeros_like(gbproj_ref)

    def share(block, which, top):
        known = [all_ref[key, jnp.bitwise_xor(block, key), which:which + 1, :] for key in range(sources)]
        peak = functools.reduce(jnp.maximum, known)
        total = functools.reduce(jnp.add, [jnp.exp(value - peak) for value in known])
        return jnp.exp(top - peak) / total

    def logit_grads(step):
        block = step + first
        at = pl.ds(pl.multiple_of(step * slots, slots), slots)
        live = CE_WEIGHT * live_ref[block]
        s_part = live * share(block, 0, s_top_ref[step])
        t_part = live * (MIXING * share(block, 1, t_top_ref[step]))
        lines = jnp.where(line == 0, s_part, jnp.where(line == 1, t_part, live * (1.0 - MIXING)))
        lines = jnp.where(line == 3, want_ref[block].astype(F32), lines)
        cols = lines.T[:slots]
        hot = jnp.where(column == cols[:, 3:4].astype(jnp.int32), cols[:, 2:3], 0.0)
        grads = cols[:, 0:1] * s_ref[at, :].astype(F32) - cols[:, 1:2] * t_ref[at, :].astype(F32) - hot
        return grads.astype(BF)

    def fill(turn):
        for step in (2 * turn, 2 * turn + 1):
            low_scr[pl.ds(pl.multiple_of(step * slots, slots), slots), :] = logit_grads(step)

    def use(turn):
        at = pl.ds(pl.multiple_of(2 * turn * slots, 2 * slots), 2 * slots)
        picked = mm(low_scr[at, :], table_ref[...])
        gbproj_ref[...] += column_sum(picked)
        picked = picked.astype(BF)
        back_ref[at, :] = mm_nt(picked, proj_ref[...]).astype(BF)
        gproj_ref[...] += mm_tn(rows_ref[at, :], picked)

    def one(turn, carry):
        fill(turn)
        use(turn)
        return carry

    gproj_ref[...] = gproj_in[...] if chained else jnp.zeros_like(gproj_ref)
    if blocks == 4:
        fill(0)
        fill(1)
        use(0)
        use(1)
    else:
        lax.fori_loop(0, blocks // 2, one, 0)


def place(me_ref):
    peer = me_ref[1]
    return me_ref[2] * 2 + lax.rem(lax.div(peer, 2), 2), me_ref[0], lax.rem(peer, 2)


def scatter_blocks(stage_ref, me, keep_ref, send_ref):
    xy_at, z_at, c_at = me
    planes = keep_ref.shape[1]
    rows, wide = keep_ref.shape[2:]
    half = planes * wide
    for xy in range(4):
        for plane in range(planes):
            at, lanes = xy * rows, plane * wide
            key = (jnp.bitwise_xor(xy, xy_at), jnp.bitwise_xor(plane, z_at))
            low = stage_ref[at:at + rows, lanes:lanes + wide]
            high = stage_ref[at:at + rows, half + lanes:half + lanes + wide]
            keep_ref[key] = jnp.where(c_at == 0, low, high).astype(BF)
            send_ref[key] = jnp.where(c_at == 0, high, low).astype(BF)


def feed_again_kernel(at_vec, vec_ref, proj_ref, up_ref, og_ref, tout_ref, out_ref, keep_ref, *refs):
    hid_ref, act_ref, slope_ref, dout_ref, gproj_ref, gbproj_ref = refs
    own, width = og_ref.shape
    pad = (keep_ref.shape[1] - LANES) // 3
    g1, c1 = (lines_of(vec_ref, at_vec[at], width) for at in (1, 2))
    hidden = (keep_ref[:, pad:pad + width] * g1 + c1).astype(BF)
    inner = mm(hidden, up_ref[...]) + lines_of(vec_ref, at_vec[6], up_ref.shape[1])
    cumulative = 0.5 * (1.0 + lax.erf(inner * ROOT_HALF))
    hid_ref[...] = hidden
    act_ref[...] = (inner * cumulative).astype(BF)
    slope_ref[...] = cumulative + inner * (jnp.exp(-0.5 * inner * inner) * (1.0 / ROOT_TWO_PI))
    output = out_ref[...]
    mapped = mm(output, proj_ref[...]) + lines_of(vec_ref, at_vec[7], proj_ref.shape[1])
    d_map = (2.0 * HID_WEIGHT * (mapped - tout_ref[...])).astype(BF)
    gproj_ref[...] = mm_tn(output, d_map)
    gbproj_ref[...] = column_sum(d_map)
    dout_ref[...] = og_ref[...].astype(F32) + mm_nt(d_map, proj_ref[...])


def feed_back_kernel(
    layout, at_vec, me_ref, line_ref, vec_ref, gproj_ref, gbproj_ref, hid_ref, act_ref, slope_ref, dout_ref,
    gproj_add, gbproj_add, down_ref, up_ref, wo_ref, keep_ref, *refs,
):
    *ce_refs, datt_ref, dres_ref, mine_ref, send_ref, stage_ref = refs
    own, width = dout_ref.shape
    pad = wo_ref.shape[0]
    at_up, at_down, at_proj, at_out = layout
    t_width = gproj_ref.shape[1]
    ff = up_ref.shape[1]
    at = lax.broadcasted_iota(jnp.int32, (own, LANES), 0)
    slots = ce_refs[0].shape[0]
    chosen = jnp.where(at == line_ref[...], 1.0, 0.0).astype(BF)[:, :slots]
    ce = functools.reduce(jnp.add, [ref[...].astype(F32) for ref in ce_refs])
    high = ce.astype(BF)
    rest = (ce - high.astype(F32)).astype(BF)
    d_out = dout_ref[...] + mm(chosen, high) + mm(chosen, rest)
    g1, g2 = (lines_of(vec_ref, at_vec[at], width) for at in (1, 4))
    n1, n2 = keep_ref[:, pad:pad + width], keep_ref[:, 2 * pad:2 * pad + width]
    stat = 3 * pad + HEADS
    i1, i2 = keep_ref[:, stat:stat + 1], keep_ref[:, stat + 1:stat + 2]
    stage_ref[width:, :] = jnp.zeros((stage_ref.shape[0] - width, stage_ref.shape[1]), F32)
    stage_ref[:width, at_proj:at_proj + t_width] = gproj_ref[...] + gproj_add[...]
    stage_ref[width:width + 1, at_proj:at_proj + t_width] = gbproj_ref[...] + gbproj_add[...]
    d_res2 = norm_back(d_out * g2, n2, i2)
    d_outer = d_res2.astype(BF)
    stage_ref[:width, at_down:at_down + ff] = mm_tn(d_outer, act_ref[...])
    d_inner = (mm(d_outer, down_ref[...]) * slope_ref[...]).astype(BF)
    stage_ref[:width, at_up:at_up + ff] = mm_tn(hid_ref[...], d_inner)
    stage_ref[width:width + 1, at_up:at_up + ff] = column_sum(d_inner)
    d_hid = d_res2 + mm_nt(d_inner, up_ref[...])
    d_res1 = norm_back(d_hid * g1, n1, i1)
    d_branch = d_res1.astype(BF)
    datt_ref[...] = mm_nt(d_branch, wo_ref[...]).astype(BF)
    dres_ref[...] = d_res1
    gout = mm_tn(keep_ref[:, :pad].astype(BF), d_branch)
    head_groups = pad // LANES
    valid = width // head_groups
    for group in range(head_groups):
        stage_ref[group * valid:(group + 1) * valid, at_out:at_out + width] = gout[group * LANES:group * LANES + valid]
    lines = [
        column_sum(d_branch),
        column_sum(d_hid * n1),
        column_sum(d_hid),
        column_sum(d_outer),
        column_sum(d_out * n2),
        column_sum(d_out),
    ]
    for at, value in enumerate(lines):
        stage_ref[width + at:width + at + 1, at_out:at_out + width] = value
    scatter_blocks(stage_ref, place(me_ref), mine_ref, send_ref)


def attend_back_kernel(
    weight_mse, size, group, datt_ref, keep_ref, q_ref, kv_ref, tq_ref, tk_ref,
    dq_ref, dk_ref, dv_ref, sums_ref, dq_scr,
):
    own, pad = q_ref.shape
    per_group = HEADS * LANES // pad
    t_size = tq_ref.shape[1] // HEADS
    t_group = LANES // t_size
    length = kv_ref.shape[0]
    chunk = length if length <= 2048 else 256
    cols = slice(group * LANES, (group + 1) * LANES)
    v_cols = slice(pad + group * LANES, pad + (group + 1) * LANES)
    s_scaling = 1.0 / math.sqrt(size)
    t_scaling = 1.0 / math.sqrt(t_size)
    lane = lax.broadcasted_iota(jnp.int32, (own, LANES), 1)
    query_all = q_ref[:, cols].astype(F32)
    grad_all = datt_ref[:, cols].astype(F32)
    product = grad_all * keep_ref[:, cols]
    lses = keep_ref[:, 3 * pad:].T
    dots = jnp.zeros((own, LANES), F32)
    heads = []
    for turn in range(per_group):
        head = group * per_group + turn
        mask = (lane >= turn * size) & (lane < (turn + 1) * size)
        dots = jnp.where(lane == turn, jnp.sum(jnp.where(mask, product, 0.0), axis=-1, keepdims=True), dots)
        t_cols = slice(head // t_group * LANES, (head // t_group + 1) * LANES)
        t_low = head % t_group * t_size
        t_mask = (lane >= t_low) & (lane < t_low + t_size)
        heads.append((
            mask,
            jnp.where(mask, query_all, 0.0).astype(BF),
            jnp.where(mask, grad_all, 0.0).astype(BF),
            t_cols,
            jnp.where(t_mask, tq_ref[:, t_cols].astype(F32), 0.0).astype(BF),
            lses[head:head + 1],
        ))
    dots = dots.T
    dq_scr[...] = jnp.zeros_like(dq_scr)
    sums_ref[...] = jnp.zeros_like(sums_ref)

    def one_chunk(at):
        keys, values = kv_ref[at, cols], kv_ref[at, v_cols]
        d_keys, d_values = jnp.zeros(keys.shape, F32), jnp.zeros(keys.shape, F32)

        def products(turn):
            _, query, grad, t_cols, t_query, _ = heads[turn]
            return mm_nt(keys, query), mm_nt(tk_ref[at, t_cols], t_query), mm_nt(values, grad)

        later = products(0)
        for turn, (mask, query, grad, _, _, lse) in enumerate(heads):
            scores, teacher, d_probs = later
            later = products(turn + 1) if turn + 1 < per_group else None
            probs = jnp.exp2(scores * (s_scaling * math.log2(math.e)) - lse)
            d_scores = (
                probs * (d_probs - dots[turn:turn + 1])
                + (scores * (weight_mse * s_scaling) - teacher * (weight_mse * t_scaling))
            ).astype(BF)
            d_keys += mm(d_scores, query)
            d_values += mm(probs.astype(BF), grad)
            dq_scr[...] += jnp.where(mask, mm_tn(d_scores, keys), 0.0)
        d_keys = d_keys * s_scaling
        sums_ref[1:2, :] += column_sum(d_keys)
        sums_ref[2:3, :] += column_sum(d_values)
        dk_ref[at, :] = d_keys.astype(BF)
        dv_ref[at, :] = d_values.astype(BF)

    if chunk == length:
        one_chunk(slice(0, length))
    else:

        def inside(turn, carry):
            one_chunk(pl.ds(pl.multiple_of(turn * chunk, chunk), chunk))
            return carry

        lax.fori_loop(0, length // chunk, inside, 0)
    d_queries = dq_scr[...] * s_scaling
    sums_ref[0:1, :] = column_sum(d_queries)
    dq_ref[...] = d_queries.astype(BF)


def attend_ready_kernel(weight_mse, size, group, keep_ref, q_ref, kv_ref, tq_ref, tk_ref, probs_ref, gap_ref):
    own, pad = q_ref.shape
    per_group = probs_ref.shape[0]
    t_size = tq_ref.shape[1] // HEADS
    t_group = LANES // t_size
    cols = slice(group * LANES, (group + 1) * LANES)
    s_scaling = 1.0 / math.sqrt(size)
    t_scaling = 1.0 / math.sqrt(t_size)
    lane = lax.broadcasted_iota(jnp.int32, (own, LANES), 1)
    lses = keep_ref[:, 3 * pad:].T

    def products(turn):
        head = group * per_group + turn
        mask = (lane >= turn * size) & (lane < (turn + 1) * size)
        query = jnp.where(mask, q_ref[:, cols].astype(F32), 0.0).astype(BF)
        t_cols = slice(head // t_group * LANES, (head // t_group + 1) * LANES)
        t_low = head % t_group * t_size
        t_mask = (lane >= t_low) & (lane < t_low + t_size)
        t_query = jnp.where(t_mask, tq_ref[:, t_cols].astype(F32), 0.0).astype(BF)
        return mm_nt(kv_ref[:, cols], query), mm_nt(tk_ref[:, t_cols], t_query)

    later = products(0)
    for turn in range(per_group):
        scores, teacher = later
        later = products(turn + 1) if turn + 1 < per_group else None
        lse = lses[group * per_group + turn:group * per_group + turn + 1]
        probs_ref[turn] = jnp.exp2(scores * (s_scaling * math.log2(math.e)) - lse).astype(BF)
        gap_ref[turn] = (scores * (weight_mse * s_scaling) - teacher * (weight_mse * t_scaling)).astype(BF)


def attend_rest_kernel(
    size, group, datt_ref, keep_ref, q_ref, kv_ref, probs_ref, gap_ref, dq_ref, dk_ref, dv_ref, sums_ref,
):
    own, pad = q_ref.shape
    per_group = probs_ref.shape[0]
    cols = slice(group * LANES, (group + 1) * LANES)
    v_cols = slice(pad + group * LANES, pad + (group + 1) * LANES)
    s_scaling = 1.0 / math.sqrt(size)
    lane = lax.broadcasted_iota(jnp.int32, (own, LANES), 1)
    query_all, grad_all = q_ref[:, cols].astype(F32), datt_ref[:, cols].astype(F32)
    product = grad_all * keep_ref[:, cols]
    masks = [(lane >= turn * size) & (lane < (turn + 1) * size) for turn in range(per_group)]
    dots = jnp.zeros((own, LANES), F32)
    for turn, mask in enumerate(masks):
        dots = jnp.where(lane == turn, jnp.sum(jnp.where(mask, product, 0.0), axis=-1, keepdims=True), dots)
    dots = dots.T
    keys, values = kv_ref[:, cols], kv_ref[:, v_cols]
    grads = [jnp.where(mask, grad_all, 0.0).astype(BF) for mask in masks]
    d_queries = jnp.zeros((own, LANES), F32)
    d_keys, d_values = jnp.zeros(keys.shape, F32), jnp.zeros(keys.shape, F32)
    later = mm_nt(values, grads[0])
    for turn, mask in enumerate(masks):
        d_probs = later
        later = mm_nt(values, grads[turn + 1]) if turn + 1 < per_group else None
        probs = probs_ref[turn]
        d_scores = (
            probs.astype(F32) * (d_probs - dots[turn:turn + 1]) + gap_ref[turn].astype(F32)
        ).astype(BF)
        d_keys += mm(d_scores, jnp.where(mask, query_all, 0.0).astype(BF))
        d_values += mm(probs, grads[turn])
        d_queries += jnp.where(mask, mm_tn(d_scores, keys), 0.0)
    d_keys, d_queries = d_keys * s_scaling, d_queries * s_scaling
    sums_ref[...] = jnp.zeros_like(sums_ref)
    sums_ref[0:1, :] = column_sum(d_queries)
    sums_ref[1:2, :] = column_sum(d_keys)
    sums_ref[2:3, :] = column_sum(d_values)
    dq_ref[...] = d_queries.astype(BF)
    dk_ref[...] = d_keys.astype(BF)
    dv_ref[...] = d_values.astype(BF)


def attend_weights_kernel(groups, me_ref, *refs):
    dq_refs, dk_refs, dv_refs, sum_refs = (refs[at * groups:(at + 1) * groups] for at in range(4))
    *row_refs, mine_ref, send_ref, g_scr, stage_ref, flip_scr = refs[4 * groups:]
    own = dq_refs[0].shape[0]
    width = row_refs[0].shape[1]
    pad = groups * LANES
    piece = row_refs[0].shape[0]
    for at, row_ref in enumerate(row_refs):
        flip_scr[:, at * piece:(at + 1) * piece] = row_ref[...].T
    g_scr[width:, :] = jnp.zeros((g_scr.shape[0] - width, g_scr.shape[1]), F32)
    for group in range(groups):
        for which, ref in enumerate((dq_refs[group], dk_refs[group], dv_refs[group])):
            there = slice(which * pad + group * LANES, which * pad + (group + 1) * LANES)
            g_scr[:width, there] = mm(flip_scr[:, :ref.shape[0]], ref[...])
            g_scr[width:width + 1, there] = sum_refs[group][which:which + 1, :]
    valid = width // groups
    parts = [g_scr[:, at * LANES:at * LANES + valid] for at in range(3 * groups)]
    stage_ref[...] = jnp.zeros_like(stage_ref)
    stage_ref[:, :3 * width] = jnp.concatenate(parts, axis=1)
    scatter_blocks(stage_ref, place(me_ref), mine_ref, send_ref)


def attend_rows_kernel(groups, wqkv_ref, dres_ref, *refs):
    dq_refs, dk_refs, dv_refs = (refs[at * groups:(at + 1) * groups] for at in range(3))
    far_ref, near_ref, own_ref = refs[3 * groups:]
    width = dres_ref.shape[1]
    pad = groups * LANES
    half = far_ref.shape[0]
    total = dres_ref[...]
    for group in range(groups):
        total = total + mm_nt(dq_refs[group][...], wqkv_ref[:, group * LANES:(group + 1) * LANES])
    own_ref[...] = total
    step = min(half, 512)
    for at in range(0, 2 * half, step):
        there = slice(at, at + step)
        back = jnp.zeros((step, width), F32)
        for group in range(groups):
            k_cols = slice(pad + group * LANES, pad + (group + 1) * LANES)
            v_cols = slice(2 * pad + group * LANES, 2 * pad + (group + 1) * LANES)
            back += mm_nt(dk_refs[group][there, :], wqkv_ref[:, k_cols])
            back += mm_nt(dv_refs[group][there, :], wqkv_ref[:, v_cols])
        out_ref, start = (near_ref, at) if at < half else (far_ref, at - half)
        out_ref[start:start + step, :] = back.astype(BF)


def stack_kernel(many, *refs):
    ins, (out,) = refs[:many], refs[many:]
    at = 0
    for turn, ref in enumerate(ins):
        if out.ndim > ref.ndim:
            out[turn] = ref[...]
        else:
            out[at:at + ref.shape[0]] = ref[...]
            at += ref.shape[0]


def copy_kernel(*refs):
    half = len(refs) // 2
    for source, target in zip(refs[:half], refs[half:]):
        target[...] = source[...]


def add_kernel(many, *refs):
    ins, outs = refs[:many], refs[many:]
    for at, out in enumerate(outs):
        if out.ndim == ins[0].ndim:
            size = out.shape[0]
            parts = [ref[at * size:(at + 1) * size] for ref in ins]
        else:
            parts = [ref[at] for ref in ins]
        out[...] = functools.reduce(jnp.add, [part.astype(F32) for part in parts]).astype(out.dtype)


def side_kernel(many, *refs):
    thin, rest = refs[:many], refs[many:]
    places = len(rest) // 2
    value = functools.reduce(jnp.add, [part[...].astype(F32) for part in thin]).astype(BF)
    planes, rows, lanes = value.shape
    for ref, out in zip(rest[:places], rest[places:]):
        for plane in range(planes):
            out[plane * rows:(plane + 1) * rows, :] = value[plane]
        height, width = ref.shape
        for turn, lane in enumerate(range(0, width, lanes)):
            at = slice(planes * rows + turn * height, planes * rows + (turn + 1) * height)
            part = ref[:, lane:lane + lanes]
            if part.shape[1] < lanes:
                out[at, :] = jnp.zeros((height, lanes), BF)
            out[at, :part.shape[1]] = part


def tail_kernel(planes, *refs):
    ins, (sum_ref,) = refs[:planes], refs[planes:]
    _, rows, lanes = sum_ref.shape
    for place in range(planes):
        parts = [ref[(place ^ key) * rows:((place ^ key) + 1) * rows, :].astype(F32) for key, ref in enumerate(ins)]
        sum_ref[place] = functools.reduce(jnp.add, parts).astype(BF)


def settle_kernel(planes, rows, me_ref, *refs):
    *ins, place_ref = refs
    lanes = ins[0].shape[1]
    height, width = place_ref.shape[1:]
    for key, ref in enumerate(ins):
        for turn, lane in enumerate(range(0, width, lanes)):
            at = planes * rows + turn * height
            many = min(lanes, width - lane)
            place_ref[jnp.bitwise_xor(me_ref[0], key), :, lane:lane + many] = ref[at:at + height, :many].astype(F32)


def collect(stage_ref, planes, me_ref, blocks):
    xy_at, z_at, c_at = place(me_ref)
    rows = stage_ref.shape[0] // 4
    each = stage_ref.shape[1] // (2 * planes)
    for core, ref in enumerate(blocks):
        for xy in range(4):
            for plane in range(planes):
                at = pl.ds(pl.multiple_of(jnp.bitwise_xor(xy, xy_at) * rows, 16), rows)
                lanes = jnp.bitwise_xor(core, c_at) * planes + jnp.bitwise_xor(plane, z_at)
                stage_ref[at, pl.ds(pl.multiple_of(lanes * each, LANES), each)] = ref[xy, plane]


def unpack_wide_kernel(layout, ff, width, t_width, planes, me_ref, *refs):
    blocks, (gout, gup, gdown, gproj, *vec_refs, mark_ref, wide_ref) = refs[:2], refs[2:]
    mark_ref[...] = jnp.zeros_like(mark_ref)
    at_up, at_down, at_proj, at_out = layout
    collect(wide_ref, planes, me_ref, blocks)
    gup[...] = wide_ref[:width, at_up:at_up + ff].astype(F32)
    gdown[...] = wide_ref[:width, at_down:at_down + ff].astype(F32)
    gproj[...] = wide_ref[:width, at_proj:at_proj + t_width].astype(F32)
    gout[...] = wide_ref[:width, at_out:at_out + width].astype(F32)
    rest = wide_ref[width:, :].astype(F32)
    for at in range(6):
        vec_refs[at][...] = rest[at:at + 1, at_out:at_out + width].reshape(width)
    vec_refs[6][...] = rest[:1, at_up:at_up + ff].reshape(ff)
    vec_refs[7][...] = rest[:1, at_proj:at_proj + t_width].reshape(t_width)


def unpack_thin_kernel(planes, me_ref, *refs):
    blocks, outs, thin_ref = refs[:2], refs[2:8], refs[8]
    width = outs[0].shape[0]
    collect(thin_ref, planes, me_ref, blocks)
    values = thin_ref[...].astype(F32)
    for at in range(3):
        lanes = slice(at * width, (at + 1) * width)
        outs[at][...] = values[:width, lanes]
        outs[3 + at][...] = values[width:width + 1, lanes].reshape(width)


def swap(value, axis, key):
    if isinstance(axis, tuple):
        size = math.prod(lax.axis_size(name) for name in axis)
    else:
        size = lax.axis_size(axis)
    RESULTS.append(lax.ppermute(value, axis, [(at, at ^ key) for at in range(size)]))
    return RESULTS[-1]


def swap_xy(value, key):
    return swap(value, ("batch", "p"), (key // 2) * lax.axis_size("p") + (key % 2) * 2)


def bits_of(size):
    return [1 << at for at in range(size.bit_length() - 1)]


def passed(value):
    turn = len(RESULTS)
    RESULTS.append(value)
    return value if TUNED[0] and turn in DIRECT else swap(value, "p", 1)


def stacked(parts, wait=(), joined=True, cost=0.1):
    rows = sum(part.shape[0] for part in parts)
    shape = (rows,) + parts[0].shape[1:] if joined else (len(parts),) + parts[0].shape
    return call(
        functools.partial(stack_kernel, len(parts)), [sds(shape, parts[0].dtype)], name="stack", cost=cost, wait=wait
    )(*parts)[0]


def spread_over_z(parts):
    return [parts[0]] + [swap(parts[key], "z", key) for key in range(1, len(parts))]


def plane_pieces(value):
    bits = list(reversed(bits_of(lax.axis_size("p"))))
    for bit in bits[:-2]:
        value = jnp.concatenate([value, swap(value, "p", bit)], axis=0)
    pieces = [value]
    for bit in bits[-2:]:
        pieces = pieces + [swap(piece, "p", bit) for piece in pieces]
    return pieces


def plane_both(value, across):
    bits = list(reversed(bits_of(lax.axis_size("p"))))
    pieces = [value, across]
    for bit in bits[1:]:
        pieces = pieces + [swap(piece, "p", bit) for piece in pieces]
    many = len(pieces) // 4
    return [jnp.concatenate(pieces[at * many:(at + 1) * many], axis=0) if many > 1 else pieces[at] for at in range(4)]


def gather_z(value, *done):
    return stacked([value] + [swap(value, "z", key) for key in range(1, lax.axis_size("z"))], wait=done)


def gather_plane(value):
    for bit in reversed(bits_of(lax.axis_size("p"))):
        value = jnp.concatenate([value, swap(value, "p", bit)], axis=0)
    return value


def copied(values, wait):
    return call(copy_kernel, [sds(value.shape, value.dtype) for value in values], name="copy", cost=0.1, wait=wait)(*values)


def add_cut(values, parts, dtype=BF, wait=()):
    rows = values[0].shape[0] // parts
    shape = values[0].shape[1:] if rows == 1 else (rows,) + values[0].shape[1:]
    return call(functools.partial(add_kernel, len(values)), [sds(shape, dtype)] * parts, name="add", cost=0.1, wait=wait)(*values)


def add_low(*values, wait=()):
    return add_cut(values, 1, wait=wait)[0]


def body(
    tokens_in, teacher_in, out_grad, mask_pos, slot_ids, w_query, b_query, w_key, b_key, w_value,
    b_value, w_out, b_out, ln1_gain, ln1_bias, w_up, b_up, w_down, b_down, ln2_gain, ln2_bias,
    w_proj, b_proj, t_query, t_key, t_value, t_out, t_up, t_down, embedding,
):
    planes, peers = lax.axis_size("z"), lax.axis_size("p")
    begin(peers == 4)
    z_at, p_at = lax.axis_index("z"), lax.axis_index("p")
    me = jnp.stack([z_at, p_at, lax.axis_index("batch")]).astype(jnp.int32)
    groups = planes * peers
    seq_count, per_device, width = tokens_in.shape
    t_width = teacher_in.shape[2]
    ff = w_up.shape[1]
    own = seq_count * per_device
    length = per_device * groups
    cap = mask_pos.shape[1] // groups
    slots = planes * cap
    size = width // HEADS
    per_group = max(n for n in range(1, LANES // size + 1) if HEADS % n == 0)
    pad = HEADS // per_group * LANES
    roomy = 16 + length // 256

    vectors = (b_out, ln1_gain, ln1_bias, b_down, ln2_gain, ln2_bias, b_up, b_proj, b_query, b_key, b_value)
    at_vec = [0]
    for vector in vectors:
        at_vec.append(at_vec[-1] - (-vector.shape[0] // LANES))
    vec_lines = -(-at_vec[-1] // 8) * 8
    down = w_down.T

    raws = (mask_pos, slot_ids, w_query, w_key, w_value, w_out) + vectors
    vec, live, want, line, wqkv, bqkv, wo = call(
        functools.partial(
            prepare_kernel, list(reversed(bits_of(peers))), cap, per_device, peers, embedding.shape[0], at_vec
        ),
        [
            sds((vec_lines, LANES), F32), sds((groups, 1, LANES), F32), sds((groups, 1, LANES), jnp.int32),
            sds((1, LANES), jnp.int32), sds((width, 3 * pad), BF), sds((1, 3 * pad), F32), sds((pad, width), BF),
        ],
        [pltpu.VMEM(raw.shape, raw.dtype) for raw in raws] + [pltpu.SemaphoreType.DMA((len(raws),))],
        name="prepare",
        cost=3,
        far=range(1, 1 + len(raws)),
    )(me, *raws)
    flipped = call(flip_kernel, [sds(embedding.shape[::-1], BF)], name="flip", cost=2)(embedding)[0]

    def packed(parts, wait=()):
        shape = sds((per_device, sum(part.shape[2] for part in parts)), BF)
        return call(
            functools.partial(pack_kernel, len(parts)),
            [shape] * planes,
            name="pack",
            cost=0.5,
            wait=wait,
        )(me, *parts)

    def unpacked(blocks, widths, wait=()):
        shapes = [sds((own, each), BF) for each in widths]
        return call(
            functools.partial(split_kernel, len(widths)), shapes, name="split", cost=0.2, wait=wait
        )(*blocks)

    blocks = spread_over_z(packed([teacher_in, tokens_in, out_grad]))
    t_own = call(head_kernel, [sds((per_device, t_width), BF)], name="head", cost=0.1)(blocks[0])[0]
    t_near = swap(t_own, "p", bits_of(peers)[-1])
    t_rows, s_rows, og_rows = unpacked(blocks, [t_width, width, width], wait=[passed(line)])
    t_far = call(bottom_rows_kernel, [sds((own - per_device, t_width), BF)], name="rest", cost=0.1)(t_rows)[0]
    wide = t_width if length <= 2048 else 2 * LANES
    t_across = stacked([t_near, swap(t_far, "p", bits_of(peers)[-1])])
    if peers == 4:
        t_pieces = [t_rows, t_across, swap(t_rows, "p", 1), swap(t_across, "p", 1)]
    else:
        t_pieces = plane_both(t_rows, t_across)
    s_across = swap(copied([s_rows], [t_across])[0], "p", bits_of(peers)[-1])
    t_att, t_q, t_k, t_mark = call(
        teacher_attend_kernel,
        [sds((own, t_width), F32), sds((own, t_width), BF), sds((length, t_width), BF), sds((8, LANES), F32)],
        [pltpu.VMEM((length, wide), BF), pltpu.VMEM((length if wide == t_width else 16, t_width), BF)],
        limit=roomy,
        name="teacher_attend",
        cost=9,
    )(t_query, t_key, t_value, *t_pieces)
    t_output, t_pick = call(
        teacher_feed_kernel,
        [sds((own, t_width), F32), sds((slots, t_width), BF)],
        name="teacher_feed",
        cost=6,
    )(line, t_pieces[0], t_att, t_out, t_up, t_down)

    if peers == 4:
        near, far = copied([s_rows, s_across], [passed(t_mark)])
        s_pieces = [s_rows, s_across, swap(near, "p", 1), swap(far, "p", 1)]
    else:
        s_pieces = plane_both(s_rows, s_across)
    q, kv, keep, output, s_mark, *s_blocks = call(
        functools.partial(student_kernel, at_vec, planes),
        [
            sds((own, pad), BF), sds((length, 2 * pad), BF), sds((own, 3 * pad + LANES), F32),
            sds((own, width), BF), sds((8, LANES), F32),
        ] + [sds((slots + per_device, width), BF)] * planes,
        limit=roomy,
        name="student",
        cost=8,
        wait=[t_pick],
    )(line, vec, wqkv, bqkv, wo, w_up, down, *s_pieces)

    def placed(parts, dtype, wait=()):
        shape = sds((planes, per_device, width), dtype)
        return call(place_kernel, [shape], name="place", cost=0.1, wait=wait)(me, *parts)[0]

    t_parts = spread_over_z([t_pick] * planes)
    t_across = [swap(t_pick, "p", bits_of(peers)[-1])]
    t_parts = copied(t_parts, [passed(s_mark)])
    t_across += [swap(part, "p", bits_of(peers)[-1]) for part in t_parts[1:]]
    here = peers // 4 * planes * slots
    blocks = here // slots
    stat_shape = sds((blocks, 1, LANES), F32)
    logit_shapes = [sds((here, embedding.shape[0]), BF), stat_shape, stat_shape]
    def logits(at_bias, pieces, name, cost, wait=()):
        got = call(
            functools.partial(logits_kernel, at_bias, slots, 2), logit_shapes * 2, limit=20, name=name, cost=cost, wait=wait
        )(*pieces, flipped, *(() if at_bias is None else (w_proj, vec)))
        return [got[:3], got[3:]]

    def in_order(first, second):
        return zip(first[0], second[0], first[1], second[1])

    t_all = [stacked(t_parts)]
    if peers == 4:
        t_all += [None, swap(t_all[0], "p", 1), None]
    else:
        t_all = plane_both(t_all[0], stacked(t_across))
    s_parts = spread_over_z(s_blocks)
    t_first = logits(None, [t_all[0], t_all[2]], "t_logits", 4)
    s_all = [call(
        functools.partial(top_kernel, planes), [sds((planes * slots, width), BF)], name="top", cost=0.1,
        wait=[passed(t_first[0][1])],
    )(*s_parts)[0]]
    if peers == 4:
        s_across = swap(s_all[0], "p", 2)
        t_all[1] = stacked(t_across, wait=[s_all[0]])
        t_all[3] = swap(t_all[1], "p", 1)
        s_first = logits(at_vec[7], [s_all[0], swap(s_all[0], "p", 1)], "s_logits", 4)
        t_second = logits(None, [t_all[1], t_all[3]], "t_logits", 4, wait=[s_first[0][1]])
        far = copied([s_across], [passed(t_second[0][1])])[0]
        s_second = logits(at_vec[7], [s_across, swap(far, "p", 1)], "s_logits", 4)
        s_all = [s_all[0], s_across, swap(s_all[0], "p", 1), swap(far, "p", 1)]
    else:
        t_second = logits(None, [t_all[1], t_all[3]], "t_logits", 4)
        s_all = plane_pieces(s_all[0])
        s_first = logits(at_vec[7], [s_all[0], s_all[2]], "s_logits", 4)
        s_second = logits(at_vec[7], [s_all[1], s_all[3]], "s_logits", 4)
    s_raised, s_top, s_lse = in_order(s_first, s_second)
    t_raised, t_top, t_lse = in_order(t_first, t_second)
    stat = jnp.concatenate([jnp.concatenate(s_lse, axis=0), jnp.concatenate(t_lse, axis=0)], axis=1)
    stats = gather_plane(gather_z(stat[None]))
    sums = []
    crossing = []
    ready = []

    def make_ready(group, wait):
        if length <= 2048:
            shape = sds((per_group, length, own), BF)
            ready.append(call(
                functools.partial(attend_ready_kernel, 2.0 / (HEADS * length), size, group),
                [shape, shape],
                limit=20,
                name="attend_ready",
                cost=2,
                wait=wait,
            )(keep, q, kv, t_q, t_k))
        return [part[0] for part in ready]


    def combined(turn, wait):
        outs = [sds((here, width), BF), sds((width, t_width), F32), sds((1, t_width), F32)]
        back, *sums[:] = call(
            functools.partial(combine_kernel, turn * blocks, slots, bool(sums)),
            outs,
            [pltpu.VMEM((here, embedding.shape[0]), BF)],
            name="combine", cost=3, wait=wait,
        )(
            *sums, live, want, s_top[turn], t_top[turn], stats, s_raised[turn], t_raised[turn], s_all[turn], embedding, w_proj,
        )
        return back

    def reduced(turn, bits, wait=()):
        if not bits:
            return combined(turn, wait)
        bit = bits[-1]
        far = reduced(turn + len(s_all) // (2 * bit), bits[:-1], wait)
        near = reduced(turn, bits[:-1], [far])
        if len(bits) == 2:
            crossing.append(far)
            if peers == 4:
                return add_cut([near, swap(far, "p", bit)], planes)
        return add_low(near, swap(far, "p", bit))

    make_ready(0, [stat])
    wait = make_ready(1, [stat])
    back = reduced(0, bits_of(len(s_all)), wait)
    for group in range(2, pad // LANES):
        make_ready(group, [crossing[-1]])
    for bit in bits_of(peers)[2:]:
        half = back.shape[0] // 2
        back = add_low(back[:half], swap(back[half:], "p", bit))
    if peers > 4:
        back = add_cut([back], planes)
    again = call(
        functools.partial(feed_again_kernel, at_vec),
        [
            sds((own, width), BF), sds((own, ff), BF), sds((own, ff), F32), sds((own, width), F32),
            sds((width, t_width), F32), sds((1, t_width), F32),
        ],
        name="feed_again",
        cost=2,
        wait=[back[0]],
    )(vec, w_proj, w_up, og_rows, t_output, output, keep)
    ce = spread_over_z(back)

    lanes_of = lambda many: -(-many // LANES) * LANES
    at_up, at_down = 0, lanes_of(ff)
    at_proj = at_down + lanes_of(ff)
    at_out = at_proj + lanes_of(t_width)
    layout = (at_up, at_down, at_proj, at_out)
    unit = 2 * planes * LANES
    wide_lanes = -(-(at_out + lanes_of(width)) // unit) * unit
    thin_lanes = -(-3 * width // unit) * unit
    tall = -(-(width + 8) // 64) * 64
    wide_block = sds((4, planes, tall // 4, wide_lanes // (2 * planes)), BF)
    thin_block = sds((4, planes, tall // 4, thin_lanes // (2 * planes)), BF)
    d_att, d_res, wide_mine, wide_send = call(
        functools.partial(feed_back_kernel, layout, at_vec),
        [sds((own, pad), BF), sds((own, width), F32), wide_block, wide_block],
        [pltpu.VMEM((tall, wide_lanes), F32)],
        name="feed_back", cost=4,
    )(me, line, vec, *sums, *again, down, w_up, wo, keep, *ce)

    def attend_back(group, cost, *done):
        outs = [sds((own, LANES), BF), sds((length, LANES), BF), sds((length, LANES), BF), sds((8, LANES), F32)]
        if ready:
            return call(
                functools.partial(attend_rest_kernel, size, group), outs, limit=20, name="attend_back", cost=cost, wait=done
            )(d_att, keep, q, kv, *ready[group])
        return call(
            functools.partial(attend_back_kernel, 2.0 / (HEADS * length), size, group),
            outs,
            [pltpu.VMEM((own, LANES), F32)],
            limit=20,
            name="attend_back",
            cost=cost,
            wait=done,
        )(d_att, keep, q, kv, t_q, t_k)

    head_groups = pad // LANES
    wide_other = swap(wide_send, "p", 1)
    wide_parts = add_cut([wide_mine, wide_other], 4)
    wide_near = [swap_xy(wide_parts[key], key) for key in range(1, 4)]
    grads = [attend_back(0, 4)]
    for group in range(1, head_groups):
        grads.append(attend_back(group, 0.1, wide_parts[0], *grads[-1]))
    layer_out = call(
        functools.partial(bottom_kernel, slots), [sds((planes, per_device, width), BF)], name="bottom", cost=0.1
    )(me, *s_parts)[0]
    wide_line = add_cut([wide_parts[0]] + wide_near, planes, wait=[grads[-1][3]])
    kinds = [list(kind) for kind in zip(*grads)]
    thin_mine, thin_send = call(
        functools.partial(attend_weights_kernel, head_groups),
        [thin_block, thin_block],
        [
            pltpu.VMEM((tall, 3 * pad), F32), pltpu.VMEM((tall, thin_lanes), F32), pltpu.VMEM((width, length), BF),
        ],
        name="attend_weights",
        cost=0.1,
    )(me, *[part for kind in kinds for part in kind], *s_pieces)
    g_far, g_near, g_own = call(
        functools.partial(attend_rows_kernel, head_groups),
        [sds((length // 2, width), BF), sds((length // 2, width), BF), sds((own, width), F32)],
        name="attend_rows",
        cost=0.1,
        wait=[layer_out, wide_line[0], thin_mine],
    )(wqkv, d_res, *[part for kind in kinds[:3] for part in kind])

    thin_other, g_other = swap(thin_send, "p", 1), swap(g_far, "p", 1)
    wide_moved = spread_over_z(wide_line)
    thin_parts = add_cut([thin_mine, thin_other], 4, wait=[wide_moved[1]])
    thin_near = [swap_xy(thin_parts[key], key) for key in range(1, 4)]
    g_parts = add_cut([g_near, g_other], peers // 2)
    for bit in bits_of(peers)[1:-1]:
        half = len(g_parts) // 2
        moved = swap(jnp.concatenate(g_parts[half:], axis=0), "p", bit)
        g_parts = add_cut([jnp.concatenate(g_parts[:half], axis=0), moved], half)
    total = add_cut([g_own, g_parts[0], swap(g_parts[1], "p", bits_of(peers)[-1])], planes)

    def finished(value):
        for bit in bits_of(peers)[2:]:
            value = add_low(value, swap(value, "p", bit))
        return value

    wide_sum = finished(add_low(*wide_moved))
    thin_shape = (planes, tall // 4, thin_lanes // (2 * planes))
    side_rows = planes * tall // 4 + per_device * (lanes_of(width) // LANES)
    tails = call(
        functools.partial(side_kernel, 4), [sds((side_rows, LANES), BF)] * planes, name="side", cost=0.1, wait=[wide_sum]
    )(thin_parts[0], *thin_near, *total)
    wide_all = stacked(spread_over_z([wide_sum] * planes), joined=False)
    tails = spread_over_z(tails)
    thin_all = call(
        functools.partial(tail_kernel, planes), [sds(thin_shape, BF)], name="tail", cost=0.1, wait=[wide_all]
    )(*tails)[0]
    input_grad = call(
        functools.partial(settle_kernel, planes, tall // 4),
        [sds((planes, per_device, width), F32)],
        name="settle",
        cost=0.1,
    )(me, *tails)[0]
    thin_all = finished(thin_all)
    wide_far = [swap_xy(wide_all, key) for key in range(1, 4)]
    thin_far = [swap_xy(thin_all, key) for key in range(1, 4)]
    wide_all = stacked([wide_all] + wide_far, joined=False, wait=[thin_all])
    wide_all = [wide_all, swap(wide_all, "p", 1)]
    square = sds((width, width), F32)
    gout, gup, gdown, gproj, *vecs = call(
        functools.partial(unpack_wide_kernel, layout, ff, width, t_width, planes),
        [square, sds((width, ff), F32), sds((width, ff), F32), sds((width, t_width), F32)]
        + [sds(vector.shape, F32) for vector in vectors[:8]] + [sds((8, LANES), F32)],
        [pltpu.VMEM((tall, wide_lanes), BF)],
        limit=24,
        name="unpack_wide",
        cost=3,
    )(me, *wide_all)
    gbo, gg1, gc1, gbd, gg2, gc2, gbup, gbproj, wide_mark = vecs
    thin_all = stacked([thin_all] + thin_far, joined=False, wait=[passed(wide_mark)])
    thin_all = [thin_all, swap(thin_all, "p", 1)]
    gq, gk, gv, gbq, gbk, gbv = call(
        functools.partial(unpack_thin_kernel, planes),
        [square] * 3 + [sds((width,), F32)] * 3,
        [pltpu.VMEM((tall, thin_lanes), BF)],
        name="unpack_thin",
        cost=1,
    )(me, *thin_all)
    return (
        layer_out, input_grad, gq, gbq, gk, gbk, gv, gbv, gout, gbo, gg1, gc1, gup, gbup, gdown.T, gbd, gg2, gc2,
        gproj, gbproj,
    )


def solution(mesh):
    batch, seq = mesh.shape["batch"], mesh.shape["seq"]
    split = P("batch", ("z", "p"), None)
    in_specs = (split,) * 3 + (P("batch", None),) * 2 + (P(),) * 24 + (P(("z", "p"), None),)
    out_specs = (split,) * 2 + (P(),) * 18

    def run(*args):
        planes = args[0].shape[0] // batch
        fine = Mesh(mesh.devices.reshape(batch, planes, seq // planes), ("batch", "z", "p"))
        return jax.shard_map(body, mesh=fine, in_specs=in_specs, out_specs=out_specs, check_vma=False)(*args)

    return run
```
